32 devices in a mesh: grp: 2 (over y), qp: 4 (over z), mode: 2 (over x), fc: 2 (over core).
Axes of the slice: x: 2, y: 2, z: 4, core: 2. Of those that a mesh axis runs over, the one named last changes fastest.
Arguments:
- home_vectors: bfloat16 [576, 288], P('grp'), parts along dimension 0, may hold values from -0.375 to 0.375
- home_freqs: bfloat16 [576], P('grp'), parts along dimension 0, may hold values from 0.5 to 4
- grid_vectors: bfloat16 [12, 288, 288], P('qp'), may hold values from -0.375 to 0.375
- partner_frequencies: bfloat16 [12, 288], P('qp'), may hold values from 0.5 to 4
- force_table: bfloat16 [288, 82944], P(None, ('mode', 'fc')), may hold values from -6 to 6
- partner: int32 [24], P(('grp', 'qp')), parts along dimension 0, may hold values from 0 to 11, as said below
- weights: int32 [24], P(('grp', 'qp')), parts along dimension 0, may hold values from 1 to 6
Outputs:
- widths: float32 [576], P(('grp', 'mode', 'fc')), parts along dimension 0
- collision: float32 [288, 24, 288], P(('mode', 'fc'), ('grp', 'qp')), parts along dimension 1
The draws below stay inside these ranges and needn't reach their ends.
There are 2 independent parts, one for each index of `grp`. The reference program is written for one: setup_inputs(seed, part) draws one part's arguments, and reference() takes and returns one part's arrays. A program takes and returns all parts, laid end to end along the dimension named above; an argument that names none is the same for every part. Nothing has to cross between parts.
Inputs may be any that keep to these rules, and one draw needn't show every extreme that they name: partner is a permutation of 0 to 11; the owner of point y is y // 3. The 3 entries on one device of qp have 3 different owners; for one position on the device, the owners over all devices of qp are all different.
All inputs are finite; a program needn't handle non-finite values.
Results may differ from the reference program's by a relative error of at most 0.0012.
Values may be sent and summed in bfloat16 or wider, within the bound.
No kernel may reach another device: no remote copies, remote signals or barrier semaphores. Data moves between devices by JAX's collectives and lax.ppermute only.
A program may use at most 128 MiB of HBM per device.

```python
import math
import jax
import jax.numpy as jnp
from jax import lax

M = 288
Q_DEV = 3
NQ = 12


def draw_partner(key, part):
    key = jax.random.fold_in(key, 7)
    count = NQ // Q_DEV
    sub_keys = jax.random.split(key, 3)
    order = jax.random.permutation(sub_keys[0], count)
    offset = jax.random.permutation(sub_keys[1], count)
    row_perm = jax.vmap(lambda sub_key: jax.random.permutation(sub_key, Q_DEV))(jax.random.split(sub_keys[2], count))
    accelerator_unit = jnp.arange(count, dtype=jnp.int32)[:, None]
    slot_ids = jnp.arange(Q_DEV, dtype=jnp.int32)[None, :]
    owner = order[(offset[accelerator_unit] + slot_ids) % count]
    chosen = row_perm[owner, jnp.broadcast_to(slot_ids, owner.shape)]
    return (owner * Q_DEV + chosen).reshape(-1).astype(jnp.int32)


def with_ends(drawn, key, smallest, high):
    longest = drawn.shape.index(max(drawn.shape))
    spots = []
    for shift in (0, 1):
        where = [jax.random.randint(jax.random.fold_in(key, axis), (), 0, length) for axis, length in enumerate(drawn.shape)]
        where[longest] = (where[longest] + shift) % drawn.shape[longest]
        spots.append(tuple(where))
    return drawn.at[spots[0]].set(smallest).at[spots[1]].set(high)


def block_levels(stream_key, dims, cuts, smallest, high):
    loudness, own = 1.0, jax.random.fold_in(stream_key, 6)
    for position, blocks in cuts:
        heights = jnp.exp(jax.random.uniform(jax.random.fold_in(own, position), (blocks,), jnp.float32, smallest / len(cuts), high / len(cuts)))
        loudness = loudness * jnp.repeat(heights, dims[position] // blocks).reshape([-1 if axis == position else 1 for axis in range(len(dims))])
    return loudness


def scatter_about(stream_key, dims, deviation, most, cuts=(), kind=jnp.bfloat16):
    result = jax.random.normal(stream_key, dims, jnp.float32) * deviation
    if len(cuts) > 0:
        result = block_levels(stream_key, dims, cuts, -0.22, 0.18) * result
    return jnp.clip(result, min=-most, max=most).astype(kind)


def setup_inputs(seed: int = 0, part: int = 0) -> dict:
    splits = jax.random.split(jax.random.key(seed), 8)
    part_splits = jax.random.split(jax.random.fold_in(splits[7], part), 8)
    return {
        "home_vectors": scatter_about(part_splits[0], (M, M), M ** -0.5, 0.375),
        "home_freqs": jnp.clip(jnp.exp(jax.random.uniform(part_splits[1], (M,), jnp.float32, math.log(0.5), math.log(4.0))), 0.5, 4.0).astype(jnp.bfloat16),
        "grid_vectors": scatter_about(splits[2], (NQ, M, M), M ** -0.5, 0.375, ((0, 4),)),
        "partner_frequencies": jnp.clip(jnp.exp(math.log(4.0) - 2.0794415 * jax.random.uniform(splits[3], (NQ, M), jnp.float32) ** block_levels(splits[3], (NQ, M), ((0, 4),), -0.2, 0.2)), 0.5, 4.0).astype(jnp.bfloat16),
        "force_table": scatter_about(splits[4], (M, M * M), 1.0, 6.0, ((1, 4),)),
        "partner": draw_partner(jax.random.fold_in(jax.random.fold_in(splits[7], part), 71), part),
        "weights": with_ends(jax.random.randint(part_splits[6], (NQ,), 1, 7), jax.random.fold_in(part_splits[6], 1), 1, 6).astype(jnp.int32),
    }


thermal_reservoir_kelvin = 1.0
smearing = 0.25


def lorentz(delta):
    return smearing / math.pi / (delta * delta + smearing * smearing)


def occupy(phonon_branch_energy):
    return 1.0 / (jnp.exp(phonon_branch_energy / thermal_reservoir_kelvin) - 1.0)


def coupled_contributions(collision_kernel_entries, home, first, second, weight, modes):
    home_b = home[:, None, None]
    first_b = first[None, :, None]
    second_b = second[None, None, :]
    power = collision_kernel_entries * collision_kernel_entries / (home_b * first_b * second_b)
    occ_one = occupy(first_b)
    occ_two = occupy(second_b)
    decay = (1.0 + occ_one + occ_two) * lorentz(home_b - first_b - second_b)
    merge_term = (occ_one - occ_two) * (lorentz(home_b + first_b - second_b) - lorentz(home_b - first_b + second_b))
    scale = weight.astype(jnp.float32) / modes
    return scale * jnp.sum(power * decay, axis=2), scale * jnp.sum(power * merge_term, axis=1)


def reference(home_vectors, home_freqs, grid_vectors, partner_frequencies, force_table, partner, weights):
    projected = jnp.dot(home_vectors.T, force_table.reshape(M, M * M), preferred_element_type=jnp.float32)
    projected = projected.reshape(M, M, M).astype(jnp.bfloat16).astype(jnp.float32)
    home = home_freqs.astype(jnp.float32)

    def one_pair(carry, index):
        first_vec = lax.dynamic_index_in_dim(grid_vectors, index, 0, False).astype(jnp.float32)
        first_freq = lax.dynamic_index_in_dim(partner_frequencies, index, 0, False).astype(jnp.float32)
        other = lax.dynamic_index_in_dim(partner, index, 0, False).astype(jnp.int32)
        second_vec = lax.dynamic_index_in_dim(grid_vectors, other, 0, False).astype(jnp.float32)
        second_freq = lax.dynamic_index_in_dim(partner_frequencies, other, 0, False).astype(jnp.float32)
        weight = lax.dynamic_index_in_dim(weights, index, 0, False)
        inner = jnp.einsum('ljk,jm->lkm', projected, first_vec, precision=lax.Precision.HIGHEST)
        inner = lax.optimization_barrier(inner.astype(jnp.bfloat16)).astype(jnp.float32)
        collision_kernel_entries = jnp.einsum('lkm,kn->lmn', inner, second_vec, precision=lax.Precision.HIGHEST)
        first_column, col_two = coupled_contributions(collision_kernel_entries, home, first_freq, second_freq, weight, M)
        return carry, (first_column, col_two)

    unused, outputs = lax.scan(one_pair, jnp.float32(0.0), jnp.arange(NQ, dtype=jnp.int32))
    col_ones, col_twos = outputs
    placed = jnp.zeros((NQ, M, M), jnp.float32).at[partner].add(col_twos)
    collision = jnp.transpose(col_ones + placed, (1, 0, 2))
    widths = jnp.mean(collision, axis=(1, 2))
    return widths, collision
```

```python
import functools
import math

import jax
import jax.numpy as jnp
from jax import lax
from jax.experimental import pallas as pl
from jax.experimental.pallas import tpu as pltpu
from jax.sharding import PartitionSpec as P

thermal_reservoir_kelvin = 1.0
smearing = 0.25

MAIN = 256
TILE = 128
F32 = jnp.float32
BF16 = jnp.bfloat16


def ceil_div(a, b):
    return -(-a // b)


def occupy(energy):
    return 1.0 / (jnp.exp(energy / thermal_reservoir_kelvin) - 1.0)


def dot_nn(a, b):
    return lax.dot_general(a, b, (((1,), (0,)), ((), ())), preferred_element_type=F32)


def dot_nt(a, b):
    return lax.dot_general(a, b, (((1,), (1,)), ((), ())), preferred_element_type=F32)


def project_kernel(groups, share, home_ref, force_ref, out_ref, main_ref, rest_ref):
    modes = home_ref.shape[1]
    lines = home_ref.shape[0]
    rest = modes - MAIN
    per_slot = MAIN // rest
    depth = out_ref.shape[2]
    step = pl.program_id(0)
    here = force_ref.shape[1] // modes
    result = dot_nn(home_ref[...], force_ref[...])
    for c in range(here):
        row = pl.multiple_of((step * here + c) * lines, 8)
        piece = result[:, c * modes : (c + 1) * modes]
        main_ref[0, pl.ds(row, lines), :] = piece[:, :TILE]
        main_ref[1, pl.ds(row, lines), :] = piece[:, TILE:MAIN]
        rest_ref[pl.ds(row, lines), :] = jnp.concatenate(
            [piece[:, MAIN:], jnp.zeros((lines, TILE - rest), F32)], axis=1
        )

    @pl.when(step == pl.num_programs(0) - 1)
    def _():
        lane = lax.broadcasted_iota(jnp.int32, (depth, TILE), 1)
        for t in range(groups):
            for r in range(share):
                line = t * share + r
                for h in range(2):
                    out_ref[t, r, :, h * TILE : (h + 1) * TILE] = main_ref[
                        h, pl.ds(line, depth, stride=lines), :
                    ].astype(BF16)
            for g in range(ceil_div(share, per_slot)):
                for h in range(2):
                    packed = jnp.zeros((depth, TILE), F32)
                    for b in range(per_slot // 2):
                        r = g * per_slot + h * (per_slot // 2) + b
                        if r < share:
                            piece = rest_ref[pl.ds(t * share + r, depth, stride=lines), :]
                            if b > 0:
                                piece = pltpu.roll(piece, b * rest, 1)
                            packed = jnp.where(lane // rest == b, piece, packed)
                    out_ref[t, share + g, :, h * TILE : (h + 1) * TILE] = packed.astype(BF16)


def project(home_rows, force_table, groups, share, modes):
    lines = home_rows.shape[0]
    depth = force_table.shape[1] // modes
    rest = modes - MAIN
    slots = share + ceil_div(share, MAIN // rest)
    here = 8 if depth % 8 == 0 else 4
    steps = depth // here
    return pl.pallas_call(
        functools.partial(project_kernel, groups, share),
        grid=(steps,),
        in_specs=[
            pl.BlockSpec((lines, modes), lambda i: (0, 0)),
            pl.BlockSpec((modes, here * modes), lambda i: (0, i)),
        ],
        out_specs=pl.BlockSpec((groups, slots, depth, MAIN), lambda i: (0, 0, 0, 0)),
        out_shape=jax.ShapeDtypeStruct((groups, slots, depth, MAIN), BF16),
        scratch_shapes=[
            pltpu.VMEM((2, depth * lines, TILE), F32),
            pltpu.VMEM((depth * lines, TILE), F32),
        ],
        compiler_params=pltpu.CompilerParams(vmem_limit_bytes=56 << 20),
        name="project",
    )(home_rows, force_table)


def coupling_kernel(
    share,
    partner_ref,
    weight_ref,
    home_ref,
    grid_ref,
    freq_row_ref,
    freq_col_ref,
    home_row_ref,
    moved_ref,
    out_ref,
    turned_ref,
    grid_t_ref,
    grid_rest_ref,
    inner_rest_ref,
    gather_ref,
    table_ref,
    sums_ref,
    pick_ref,
    inner0,
    inner1,
    inner2,
    value0,
    value1,
    value2,
):
    pairs = grid_ref.shape[0]
    modes = grid_ref.shape[2]
    rest = modes - MAIN
    sources, depth = moved_ref.shape[0], moved_ref.shape[2]
    per_slot = MAIN // rest
    rest_lanes = home_row_ref.shape[1]
    inners = (inner0, inner1, inner2)
    values = (value0, value1, value2)
    s2 = smearing * smearing

    eye = (
        lax.broadcasted_iota(jnp.int32, (modes, modes), 0)
        == lax.broadcasted_iota(jnp.int32, (modes, modes), 1)
    ).astype(BF16)

    def turn_grid(x, carry):
        turned = dot_nt(eye, grid_ref[x, :modes, :]).astype(BF16)
        grid_t_ref[x] = turned
        grid_rest_ref[pl.ds(pl.multiple_of(x * rest, rest), rest), :] = turned[MAIN:, :]
        return carry

    lax.fori_loop(0, pairs, turn_grid, 0)
    lane = lax.broadcasted_iota(jnp.int32, (depth, TILE), 1)
    inner_rest_ref[...] = jnp.zeros_like(inner_rest_ref)
    for r in range(share):
        slot, spot = share + r // per_slot, r % per_slot
        half, spot = spot // (per_slot // 2), spot % (per_slot // 2)
        for s in range(sources):
            gather_ref[s * depth : (s + 1) * depth, :MAIN] = moved_ref[s, r].astype(F32)
            tail = moved_ref[s, slot, :, half * TILE : (half + 1) * TILE].astype(F32)
            if spot > 0:
                tail = pltpu.roll(tail, TILE - spot * rest, 1)
            gather_ref[s * depth : (s + 1) * depth, MAIN:] = tail[:, :rest]
        block = gather_ref[...].astype(BF16)
        turned_ref[r] = dot_nt(eye, block).astype(BF16)
        found = dot_nn(grid_rest_ref[...], block).astype(BF16)
        for x in range(pairs):
            inner_rest_ref[x, r * rest : (r + 1) * rest, :] = found[x * rest : (x + 1) * rest, :]

    row_id = lax.broadcasted_iota(jnp.int32, pick_ref.shape, 0)
    col_id = lax.broadcasted_iota(jnp.int32, pick_ref.shape, 1)
    branch = jnp.where(
        row_id < share * TILE, row_id // TILE, (row_id - share * TILE) // rest
    )
    pick_ref[...] = (branch == col_id).astype(BF16)
    out_ref[...] = jnp.zeros_like(out_ref)

    def contract_first(x, r, into):
        into[...] = dot_nn(turned_ref[r], grid_ref[x, :modes, :MAIN]).astype(BF16)

    def contract_second(x, source, into):
        into[...] = dot_nn(grid_t_ref[partner_ref[x]], source[...])

    def weigh(x, r, source):
        w = home_ref[r]
        c1 = w * w - s2
        c2 = (4.0 * s2) * (w * w)
        total = jnp.zeros((8, MAIN), F32)
        rows = 16
        for n in range(0, modes, rows):
            v = source[n : n + rows, :]
            p = v * v
            d = table_ref[0, n : n + rows, :MAIN] - w
            t = (p * table_ref[2, n : n + rows, :MAIN]) * pl.reciprocal(d * d + s2, approx=True)
            total = total + t[:8] + t[8:]
            e = table_ref[1, n : n + rows, :MAIN] - c1
            u = (p * table_ref[3, n : n + rows, :MAIN]) * pl.reciprocal(e * e + c2, approx=True)
            sums_ref[r, n : n + rows, :] = (u[:, :TILE] + u[:, TILE:]).astype(BF16)
        line = jnp.sum(total, axis=0, keepdims=True) * (1.0 / w)
        out_ref[x, pl.ds(r, 1), :MAIN] += line

    def tables(x):
        w1 = freq_row_ref[x]
        spots = lax.broadcasted_iota(jnp.int32, freq_col_ref.shape, 1)
        w2 = jnp.sum(
            jnp.where(spots == partner_ref[x], freq_col_ref[...], 0.0), axis=1, keepdims=True
        )
        o1, o2 = occupy(w1), occupy(w2)
        scale = weight_ref[x] * (smearing / math.pi / modes)
        i1, i2 = scale / w1, 1.0 / w2
        for n in range(0, modes, 48):
            w2n, o2n, i2n = w2[n : n + 48], o2[n : n + 48], i2[n : n + 48]
            a = w1 - w2n
            both = i1 * i2n
            table_ref[0, n : n + 48, :] = w1 + w2n
            table_ref[1, n : n + 48, :] = a * a
            table_ref[2, n : n + 48, :] = (1.0 + o1 + o2n) * both
            table_ref[3, n : n + 48, :] = (4.0 * a) * (o2n - o1) * both

    def finish(x):
        target = partner_ref[x]
        left = grid_t_ref[target]
        for start in range(0, rest_lanes, TILE):
            found = dot_nt(left, inner_rest_ref[x, start : start + TILE, :])
            w = home_row_ref[:, start : start + TILE]
            c1 = w * w - s2
            c2 = (4.0 * s2) * (w * w)
            total = jnp.zeros((8, TILE), F32)
            for n in range(0, modes, 16):
                v = found[n : n + 16]
                p = v * v
                d = table_ref[0, n : n + 16, MAIN:] - w
                t = (p * table_ref[2, n : n + 16, MAIN:]) * pl.reciprocal(
                    d * d + s2, approx=True
                )
                total = total + t[:8] + t[8:]
                e = table_ref[1, n : n + 16, MAIN:] - c1
                u = (p * table_ref[3, n : n + 16, MAIN:]) * pl.reciprocal(
                    e * e + c2, approx=True
                )
                sums_ref[share + start // TILE, n : n + 16, :] = u.astype(BF16)
            line = jnp.sum(total, axis=0, keepdims=True) / w
            for b in range(TILE // rest):
                r = start // rest + b
                if r < share:
                    out_ref[x, r : r + 1, MAIN:] += line[:, b * rest : (b + 1) * rest]
        second = jnp.zeros((modes, TILE), F32)
        for c in range(share + rest_lanes // TILE):
            second += dot_nn(sums_ref[c], pick_ref[c * TILE : (c + 1) * TILE, :])
        out_ref[target, :share, :] += second.T[:share, :]

    unroll = 3
    assert share % unroll == 0
    contract_first(0, 0, inners[0])
    contract_first(0, 1, inners[1])
    contract_second(0, inners[0], values[0])

    def one_pair(x, carry):
        tables(x)

        def some(i, inner_carry):
            for u in range(unroll):
                r = i * unroll + u

                def ahead(by):
                    wraps = (r + by >= share).astype(jnp.int32)
                    return jnp.minimum(x + wraps, pairs - 1), r + by - wraps * share

                x2, r2 = ahead(2)
                contract_first(x2, r2, inners[(u + 2) % 3])
                x1, _ = ahead(1)
                contract_second(x1, inners[(u + 1) % 3], values[(u + 1) % 3])
                weigh(x, r, values[u])
            return inner_carry

        lax.fori_loop(0, share // unroll, some, 0)
        finish(x)
        return carry

    lax.fori_loop(0, pairs, one_pair, 0)

    totals = jnp.zeros(out_ref.shape[1:], F32)
    for y in range(pairs):
        totals = totals + out_ref[y]
    widths = jnp.sum(totals, axis=1, keepdims=True) * (1.0 / (pairs * modes))
    spread = jnp.where(
        lax.broadcasted_iota(jnp.int32, totals.shape, 0)
        == lax.broadcasted_iota(jnp.int32, totals.shape, 1),
        widths,
        0.0,
    )
    out_ref[:, share, :] = jnp.broadcast_to(
        jnp.sum(spread, axis=0, keepdims=True), (pairs, modes)
    )


def coupling(partner, weights, home, grid, freq_rows, freq_cols, home_row, moved, share, modes):
    pairs = grid.shape[0]
    rest = modes - MAIN
    rest_lanes = home_row.shape[1]
    padded = (share // 8 + 1) * 8
    smem = pl.BlockSpec(memory_space=pltpu.SMEM)
    vmem = pl.BlockSpec(memory_space=pltpu.VMEM)
    chunks = share + rest_lanes // TILE
    return pl.pallas_call(
        functools.partial(coupling_kernel, share),
        in_specs=[smem, smem, smem, vmem, vmem, vmem, vmem, vmem],
        out_specs=vmem,
        out_shape=jax.ShapeDtypeStruct((pairs, padded, modes), F32),
        scratch_shapes=[
            pltpu.VMEM((share, modes, modes), BF16),
            pltpu.VMEM((pairs, modes, modes), BF16),
            pltpu.VMEM((pairs * rest, modes), BF16),
            pltpu.VMEM((pairs, rest_lanes, modes), BF16),
            pltpu.VMEM((modes, modes), F32),
            pltpu.VMEM((4, modes, MAIN + TILE), F32),
            pltpu.VMEM((chunks, modes, TILE), BF16),
            pltpu.VMEM((chunks * TILE, TILE), BF16),
            pltpu.VMEM((modes, MAIN), BF16),
            pltpu.VMEM((modes, MAIN), BF16),
            pltpu.VMEM((modes, MAIN), BF16),
            pltpu.VMEM((modes, MAIN), F32),
            pltpu.VMEM((modes, MAIN), F32),
            pltpu.VMEM((modes, MAIN), F32),
        ],
        compiler_params=pltpu.CompilerParams(vmem_limit_bytes=56 << 20),
        name="coupling",
    )(partner, weights, home, grid, freq_rows, freq_cols, home_row, moved)


def local(
    home_vectors, home_freqs, grid_vectors, partner_frequencies, force_table, partner, weights
):
    own_pairs = partner.shape[0]
    modes = home_vectors.shape[0]
    n_mode = lax.axis_size("mode")
    n_fc = lax.axis_size("fc")
    n_qp = lax.axis_size("qp")
    groups = n_mode * n_fc
    group = modes // groups
    pairs = own_pairs * n_qp
    share = ceil_div(group, n_qp)
    rest = modes - MAIN
    here = lax.axis_index("qp")

    extra = jnp.zeros((own_pairs, 16, modes), BF16)
    extra = extra.at[:, 0, :].set(partner_frequencies)
    extra = extra.at[:, 1, 0].set(partner.astype(BF16))
    extra = extra.at[:, 1, 1].set(weights.astype(BF16))
    gathered = lax.all_gather(
        jnp.concatenate([grid_vectors, extra], axis=1), "qp", axis=0, tiled=True
    )

    rows = home_vectors.T.reshape(groups, group, modes)
    rows = jnp.pad(rows, ((0, 0), (0, share * n_qp - group), (0, 0)))
    rows = lax.dynamic_slice_in_dim(rows, here * share, share, axis=1)
    rows = rows.reshape(groups * share, modes)
    sent = project(rows, force_table, groups, share, modes)
    moved = lax.all_to_all(sent, ("mode", "fc"), split_axis=0, concat_axis=0, tiled=True)

    own = lax.axis_index(("mode", "fc"))
    home = home_freqs.astype(F32).reshape(groups, group)
    home = jnp.pad(home, ((0, 0), (0, share * n_qp - group)), constant_values=1.0)
    home = lax.dynamic_slice(home, (own, here * share), (1, share)).reshape(share)
    rest_lanes = ceil_div(share * rest, TILE) * TILE
    home_row = jnp.repeat(home, rest)
    home_row = jnp.pad(home_row, (0, rest_lanes - share * rest), constant_values=1.0)[None]

    freqs = gathered[:, modes, :].astype(F32)
    freq_rows = jnp.concatenate(
        [freqs[:, :MAIN]] + [freqs[:, MAIN:]] * (TILE // rest), axis=1
    )[:, None, :]
    all_partner = gathered[:, modes + 1, 0].astype(jnp.int32)
    all_weights = gathered[:, modes + 1, 1].astype(F32)
    found = coupling(
        all_partner, all_weights, home, gathered, freq_rows, freqs.T, home_row, moved, share, modes
    )

    padded = found.shape[1]
    back = lax.all_to_all(
        found.reshape(n_qp, own_pairs, padded, modes), "qp", split_axis=0, concat_axis=0, tiled=True
    )
    widths = back[:, 0, share, :share].reshape(n_qp * share)[:group]
    collision = jnp.transpose(back[:, :, :share, :], (0, 2, 1, 3))
    collision = collision.reshape(n_qp * share, own_pairs, modes)[:group]
    return (widths, collision)


def solution(mesh):
    placed = (
        P("grp", None),
        P("grp"),
        P("qp", None, None),
        P("qp", None),
        P(None, ("mode", "fc")),
        P(("grp", "qp")),
        P(("grp", "qp")),
    )
    return jax.shard_map(
        local,
        mesh=mesh,
        in_specs=placed,
        out_specs=(P(("grp", "mode", "fc")), P(("mode", "fc"), ("grp", "qp"), None)),
        check_vma=False,
    )
```

```python
import functools
import math

import jax
import jax.numpy as jnp
from jax import lax
from jax.experimental import pallas as pl
from jax.experimental.pallas import tpu as pltpu
from jax.sharding import PartitionSpec as P

thermal_reservoir_kelvin = 1.0
smearing = 0.25

MAIN = 256
TILE = 128
F32 = jnp.float32
BF16 = jnp.bfloat16


def ceil_div(a, b):
    return -(-a // b)


def occupy(energy):
    return 1.0 / (jnp.exp(energy / thermal_reservoir_kelvin) - 1.0)


def dot_nn(a, b):
    return lax.dot_general(a, b, (((1,), (0,)), ((), ())), preferred_element_type=F32)


def dot_nt(a, b):
    return lax.dot_general(a, b, (((1,), (1,)), ((), ())), preferred_element_type=F32)


def slots_of(count, modes):
    return count + ceil_div(count, MAIN // (modes - MAIN))


def project_kernel(groups, n_qp, group, chunks, here_ref, home_ref, force_ref, *refs):
    outs = refs[: len(chunks)]
    rows_ref, main_ref, rest_ref = refs[len(chunks) :]
    modes = home_ref.shape[0]
    lines = rows_ref.shape[0]
    share = lines // groups
    rest = modes - MAIN
    per_slot = MAIN // rest
    depth = outs[0].shape[2]
    step = pl.program_id(0)
    here = force_ref.shape[1] // modes

    @pl.when(step == 0)
    def _():
        line = lax.broadcasted_iota(jnp.int32, (lines, modes), 0)
        column = lax.broadcasted_iota(jnp.int32, (lines, modes), 1)
        own = here_ref[0] * share + line % share
        wanted = (line // share) * group + own
        select = jnp.logical_and(column == wanted, own < group).astype(BF16)
        rows_ref[...] = dot_nt(select, home_ref[...]).astype(BF16)

    result = dot_nn(rows_ref[...], force_ref[...])
    for c in range(here):
        row = pl.multiple_of((step * here + c) * lines, 8)
        piece = result[:, c * modes : (c + 1) * modes]
        main_ref[0, pl.ds(row, lines), :] = piece[:, :TILE]
        main_ref[1, pl.ds(row, lines), :] = piece[:, TILE:MAIN]
        rest_ref[pl.ds(row, lines), :] = jnp.concatenate(
            [piece[:, MAIN:], jnp.zeros((lines, TILE - rest), F32)], axis=1
        )

    @pl.when(step == pl.num_programs(0) - 1)
    def _():
        lane = lax.broadcasted_iota(jnp.int32, (depth, TILE), 1)
        for (first, count), out_ref in zip(chunks, outs):
            for t in range(groups):
                base = t * share + first
                for r in range(count):
                    for h in range(2):
                        out_ref[t, r, :, h * TILE : (h + 1) * TILE] = main_ref[
                            h, pl.ds(base + r, depth, stride=lines), :
                        ].astype(BF16)
                for g in range(ceil_div(count, per_slot)):
                    for h in range(2):
                        packed = jnp.zeros((depth, TILE), F32)
                        for b in range(per_slot // 2):
                            r = g * per_slot + h * (per_slot // 2) + b
                            if r < count:
                                piece = rest_ref[pl.ds(base + r, depth, stride=lines), :]
                                if b > 0:
                                    piece = pltpu.roll(piece, b * rest, 1)
                                packed = jnp.where(lane // rest == b, piece, packed)
                        out_ref[t, count + g, :, h * TILE : (h + 1) * TILE] = packed.astype(BF16)


def project(here, home_vectors, force_table, groups, n_qp, group, share, chunks):
    modes = home_vectors.shape[0]
    lines = groups * share
    depth = force_table.shape[1] // modes
    per_step = 8 if depth % 8 == 0 else 4
    steps = depth // per_step
    shapes = [(groups, slots_of(count, modes), depth, MAIN) for _, count in chunks]
    return pl.pallas_call(
        functools.partial(project_kernel, groups, n_qp, group, chunks),
        grid=(steps,),
        in_specs=[
            pl.BlockSpec(memory_space=pltpu.SMEM),
            pl.BlockSpec((modes, modes), lambda i: (0, 0)),
            pl.BlockSpec((modes, per_step * modes), lambda i: (0, i)),
        ],
        out_specs=[pl.BlockSpec(shape, lambda i: (0, 0, 0, 0)) for shape in shapes],
        out_shape=[jax.ShapeDtypeStruct(shape, BF16) for shape in shapes],
        scratch_shapes=[
            pltpu.VMEM((lines, modes), BF16),
            pltpu.VMEM((2, depth * lines, TILE), F32),
            pltpu.VMEM((depth * lines, TILE), F32),
        ],
        compiler_params=pltpu.CompilerParams(vmem_limit_bytes=56 << 20),
        name="project",
    )(here, home_vectors, force_table)


def identity(size):
    return (
        lax.broadcasted_iota(jnp.int32, (size, size), 0)
        == lax.broadcasted_iota(jnp.int32, (size, size), 1)
    ).astype(BF16)


def arrange_kernel(
    pack_ref, partner_ref, weight_ref, grid_ref, grid_t_ref, freq_row_ref, freq_col_ref
):
    owners, parts, each, rows, modes = pack_ref.shape
    half = modes // parts
    rest = modes - MAIN
    eye = identity(modes)
    source = lax.broadcasted_iota(jnp.int32, (modes, MAIN + TILE), 0)
    place = lax.broadcasted_iota(jnp.int32, (modes, MAIN + TILE), 1)
    wanted = jnp.where(place < MAIN, place, MAIN + (place - MAIN) % rest)
    spread = (source == wanted).astype(BF16)
    lane = lax.broadcasted_iota(jnp.int32, freq_col_ref.shape, 1)
    lane16 = lax.broadcasted_iota(jnp.int32, (16, modes), 1)
    line16 = lax.broadcasted_iota(jnp.int32, (16, modes), 0)
    freq_col_ref[...] = jnp.zeros_like(freq_col_ref)

    def one(q, carry):
        for s in range(each):
            x = q * each + s
            for part in range(parts):
                grid_ref[x, part * half : (part + 1) * half, :] = pack_ref[q, part, s, :half, :]
            grid_t_ref[x] = dot_nt(eye, grid_ref[x]).astype(BF16)
            side = pack_ref[q, 0, s, half : half + 16, :]
            freq_row_ref[x] = dot_nn(side, spread)[0:1, :]
            column = dot_nt(eye, side)[:, 0:1]
            freq_col_ref[...] = jnp.where(lane == x, column, freq_col_ref[...])
            wide = side.astype(F32)
            for spot, ref in ((0, partner_ref), (1, weight_ref)):
                found = jnp.sum(
                    jnp.where(jnp.logical_and(line16 == 1, lane16 == spot), wide, 0.0)
                )
                ref[x] = found.astype(ref.dtype)
        return carry

    lax.fori_loop(0, owners, one, 0)


def arrange(pack):
    owners, parts, each, _, modes = pack.shape
    pairs = owners * each
    smem = pl.BlockSpec(memory_space=pltpu.SMEM)
    vmem = pl.BlockSpec(memory_space=pltpu.VMEM)
    return pl.pallas_call(
        arrange_kernel,
        in_specs=[vmem],
        out_specs=[smem, smem, vmem, vmem, vmem, vmem],
        out_shape=[
            jax.ShapeDtypeStruct((pairs,), jnp.int32),
            jax.ShapeDtypeStruct((pairs,), F32),
            jax.ShapeDtypeStruct((pairs, modes, modes), BF16),
            jax.ShapeDtypeStruct((pairs, modes, modes), BF16),
            jax.ShapeDtypeStruct((pairs, 1, MAIN + TILE), F32),
            jax.ShapeDtypeStruct((modes, TILE), F32),
        ],
        compiler_params=pltpu.CompilerParams(vmem_limit_bytes=56 << 20),
        name="arrange",
    )(pack)


def coupling_kernel(
    share,
    block,
    buffers,
    partner_ref,
    weight_ref,
    home_ref,
    grid_ref,
    grid_t_ref,
    freq_row_ref,
    freq_col_ref,
    home_row_ref,
    moved_ref,
    out_ref,
    turned_ref,
    grid_rest_ref,
    inner_rest_ref,
    gather_ref,
    table_ref,
    sums_ref,
    pick_ref,
    *work,
):
    inners, values = work[:buffers], work[buffers:]
    pairs = grid_ref.shape[0]
    modes = grid_ref.shape[2]
    rest = modes - MAIN
    sources, depth = moved_ref.shape[0], moved_ref.shape[2]
    per_slot = MAIN // rest
    rest_lanes = home_row_ref.shape[1]
    s2 = smearing * smearing
    steps = share // block

    for x in range(pairs):
        grid_rest_ref[x * rest : (x + 1) * rest, :] = grid_t_ref[x, MAIN:, :]
    eye = identity(modes)
    inner_rest_ref[...] = jnp.zeros_like(inner_rest_ref)
    for r in range(share):
        slot, spot = share + r // per_slot, r % per_slot
        half, spot = spot // (per_slot // 2), spot % (per_slot // 2)
        for s in range(sources):
            gather_ref[s * depth : (s + 1) * depth, :MAIN] = moved_ref[s, r].astype(F32)
            tail = moved_ref[s, slot, :, half * TILE : (half + 1) * TILE].astype(F32)
            if spot > 0:
                tail = pltpu.roll(tail, TILE - spot * rest, 1)
            gather_ref[s * depth : (s + 1) * depth, MAIN:] = tail[:, :rest]
        whole = gather_ref[...].astype(BF16)
        turned_ref[r * modes : (r + 1) * modes, :] = dot_nt(eye, whole).astype(BF16)
        found = dot_nn(grid_rest_ref[...], whole).astype(BF16)
        for x in range(pairs):
            inner_rest_ref[x, r * rest : (r + 1) * rest, :] = found[x * rest : (x + 1) * rest, :]

    row_id = lax.broadcasted_iota(jnp.int32, pick_ref.shape, 0)
    col_id = lax.broadcasted_iota(jnp.int32, pick_ref.shape, 1)
    branch = jnp.where(
        row_id < share * TILE, row_id // TILE, (row_id - share * TILE) // rest
    )
    pick_ref[...] = (branch == col_id).astype(BF16)
    out_ref[...] = jnp.zeros_like(out_ref)

    def contract_first(x, step, into):
        start = pl.multiple_of(step * (block * modes), 16)
        found = dot_nn(turned_ref[pl.ds(start, block * modes), :], grid_ref[x, :, :MAIN])
        for b in range(block):
            into[:, b * MAIN : (b + 1) * MAIN] = found[b * modes : (b + 1) * modes].astype(BF16)

    def contract_second(x, source, into):
        into[...] = dot_nn(grid_t_ref[partner_ref[x]], source[...])

    def weigh(x, step, source):
        ws = [home_ref[step * block + b] for b in range(block)]
        c1s = [w * w - s2 for w in ws]
        c2s = [(4.0 * s2) * (w * w) for w in ws]
        totals = [jnp.zeros((8, MAIN), F32) for _ in ws]
        for n in range(0, modes, 16):
            t0 = table_ref[0, n : n + 16, :MAIN]
            t1 = table_ref[1, n : n + 16, :MAIN]
            t2 = table_ref[2, n : n + 16, :MAIN]
            t3 = table_ref[3, n : n + 16, :MAIN]
            for b in range(block):
                v = source[n : n + 16, b * MAIN : (b + 1) * MAIN]
                p = v * v
                d = t0 - ws[b]
                t = (p * t2) * pl.reciprocal(d * d + s2, approx=True)
                totals[b] = totals[b] + (t[:8] + t[8:])
                e = t1 - c1s[b]
                u = (p * t3) * pl.reciprocal(e * e + c2s[b], approx=True)
                sums_ref[step * block + b, n : n + 16, :] = (u[:, :TILE] + u[:, TILE:]).astype(BF16)
        for b in range(block):
            line = jnp.sum(totals[b], axis=0, keepdims=True) * (1.0 / ws[b])
            out_ref[x, pl.ds(step * block + b, 1), :MAIN] += line

    def tables(x):
        w1 = freq_row_ref[x]
        spots = lax.broadcasted_iota(jnp.int32, freq_col_ref.shape, 1)
        w2 = jnp.sum(
            jnp.where(spots == partner_ref[x], freq_col_ref[...], 0.0), axis=1, keepdims=True
        )
        o1, o2 = occupy(w1), occupy(w2)
        scale = weight_ref[x] * (smearing / math.pi / modes)
        i1, i2 = scale / w1, 1.0 / w2
        for n in range(0, modes, 48):
            w2n, o2n, i2n = w2[n : n + 48], o2[n : n + 48], i2[n : n + 48]
            a = w1 - w2n
            both = i1 * i2n
            table_ref[0, n : n + 48, :] = w1 + w2n
            table_ref[1, n : n + 48, :] = a * a
            table_ref[2, n : n + 48, :] = (1.0 + o1 + o2n) * both
            table_ref[3, n : n + 48, :] = (4.0 * a) * (o2n - o1) * both

    def finish(x):
        target = partner_ref[x]
        left = grid_t_ref[target]
        for start in range(0, rest_lanes, TILE):
            found = dot_nt(left, inner_rest_ref[x, start : start + TILE, :])
            w = home_row_ref[:, start : start + TILE]
            c1 = w * w - s2
            c2 = (4.0 * s2) * (w * w)
            total = jnp.zeros((8, TILE), F32)
            for n in range(0, modes, 16):
                v = found[n : n + 16]
                p = v * v
                d = table_ref[0, n : n + 16, MAIN:] - w
                t = (p * table_ref[2, n : n + 16, MAIN:]) * pl.reciprocal(
                    d * d + s2, approx=True
                )
                total = total + (t[:8] + t[8:])
                e = table_ref[1, n : n + 16, MAIN:] - c1
                u = (p * table_ref[3, n : n + 16, MAIN:]) * pl.reciprocal(
                    e * e + c2, approx=True
                )
                sums_ref[share + start // TILE, n : n + 16, :] = u.astype(BF16)
            line = jnp.sum(total, axis=0, keepdims=True) / w
            for b in range(TILE // rest):
                r = start // rest + b
                if r < share:
                    out_ref[x, r : r + 1, MAIN:] += line[:, b * rest : (b + 1) * rest]
        second = jnp.zeros((modes, TILE), F32)
        for c in range(share + rest_lanes // TILE):
            second += dot_nn(sums_ref[c], pick_ref[c * TILE : (c + 1) * TILE, :])
        out_ref[target, :share, :] += second.T[:share, :]

    if buffers > 1:
        contract_first(0, 0, inners[0])
        contract_first(0, 1, inners[1])
        contract_second(0, inners[0], values[0])

    def one_pair(x, carry):
        tables(x)

        def some(i, inner_carry):
            for u in range(buffers):
                step = i * buffers + u

                def ahead(by):
                    wraps = (step + by >= steps).astype(jnp.int32)
                    return jnp.minimum(x + wraps, pairs - 1), step + by - wraps * steps

                if buffers > 1:
                    x1, _ = ahead(1)
                    contract_second(x1, inners[(u + 1) % buffers], values[(u + 1) % buffers])
                    x2, step2 = ahead(2)
                    contract_first(x2, step2, inners[(u + 2) % buffers])
                else:
                    contract_first(x, step, inners[0])
                    contract_second(x, inners[0], values[0])
                weigh(x, step, values[u])
            return inner_carry

        lax.fori_loop(0, steps // buffers, some, 0)
        finish(x)
        return carry

    lax.fori_loop(0, pairs, one_pair, 0)

    totals = jnp.zeros(out_ref.shape[1:], F32)
    for y in range(pairs):
        totals = totals + out_ref[y]
    widths = jnp.sum(totals, axis=1, keepdims=True) * (1.0 / (pairs * modes))
    spread = jnp.where(
        lax.broadcasted_iota(jnp.int32, totals.shape, 0)
        == lax.broadcasted_iota(jnp.int32, totals.shape, 1),
        widths,
        0.0,
    )
    out_ref[:, share, :] = jnp.broadcast_to(
        jnp.sum(spread, axis=0, keepdims=True), (pairs, modes)
    )


def coupling(partner, weights, home, grid, grid_t, freq_rows, freq_cols, moved):
    pairs, modes = grid.shape[0], grid.shape[2]
    share = home.shape[0]
    rest = modes - MAIN
    rest_lanes = ceil_div(share * rest, TILE) * TILE
    home_row = jnp.repeat(home, rest)
    home_row = jnp.pad(home_row, (0, rest_lanes - share * rest), constant_values=1.0)[None]
    padded = (share // 8 + 1) * 8
    smem = pl.BlockSpec(memory_space=pltpu.SMEM)
    vmem = pl.BlockSpec(memory_space=pltpu.VMEM)
    tiles = share + rest_lanes // TILE
    block = 3 if share % 3 == 0 else 1
    steps = share // block
    buffers = 2 if steps % 2 == 0 else 3 if steps % 3 == 0 else 1
    return pl.pallas_call(
        functools.partial(coupling_kernel, share, block, buffers),
        in_specs=[smem, smem, smem, vmem, vmem, vmem, vmem, vmem, vmem],
        out_specs=vmem,
        out_shape=jax.ShapeDtypeStruct((pairs, padded, modes), F32),
        scratch_shapes=[
            pltpu.VMEM((share * modes, modes), BF16),
            pltpu.VMEM((pairs * rest, modes), BF16),
            pltpu.VMEM((pairs, rest_lanes, modes), BF16),
            pltpu.VMEM((modes, modes), F32),
            pltpu.VMEM((4, modes, MAIN + TILE), F32),
            pltpu.VMEM((tiles, modes, TILE), BF16),
            pltpu.VMEM((tiles * TILE, TILE), BF16),
        ]
        + [pltpu.VMEM((modes, block * MAIN), BF16)] * buffers
        + [pltpu.VMEM((modes, block * MAIN), F32)] * buffers,
        compiler_params=pltpu.CompilerParams(vmem_limit_bytes=56 << 20),
        cost_estimate=pl.CostEstimate(
            flops=4 * share * pairs * modes**3,
            bytes_accessed=8 * share * modes * modes,
            transcendentals=2 * share * pairs * modes**2,
        ),
        name="coupling",
    )(partner, weights, home, grid, grid_t, freq_rows, freq_cols, home_row, moved)


def local(
    home_vectors, home_freqs, grid_vectors, partner_frequencies, force_table, partner, weights
):
    own_pairs = partner.shape[0]
    modes = home_vectors.shape[0]
    n_mode = lax.axis_size("mode")
    n_fc = lax.axis_size("fc")
    n_qp = lax.axis_size("qp")
    groups = n_mode * n_fc
    group = modes // groups
    pairs = own_pairs * n_qp
    share = ceil_div(group, n_qp)
    here = lax.axis_index("qp")
    if share % 6 == 0 and share > 6:
        chunks = ((0, 6), (6, share - 6))
    else:
        chunks = ((0, share),)

    part_rows = modes // n_fc
    part = lax.dynamic_slice_in_dim(
        grid_vectors, lax.axis_index("fc") * part_rows, part_rows, axis=1
    )
    lane = jnp.arange(modes)[None]
    small = jnp.where(lane == 0, partner[:, None], jnp.where(lane == 1, weights[:, None], 0))
    side = jnp.stack([partner_frequencies, small.astype(BF16)], axis=1)
    side = jnp.pad(side, ((0, 0), (0, 14), (0, 0)))
    pack = lax.all_gather(jnp.concatenate([part, side], axis=1), ("qp", "fc"), axis=0)
    pack = pack.reshape(n_qp, n_fc, own_pairs, part_rows + 16, modes)

    sent = project(
        here.astype(jnp.int32)[None], home_vectors, force_table, groups, n_qp, group, share, chunks
    )
    moved = [
        lax.all_to_all(x, ("mode", "fc"), split_axis=0, concat_axis=0, tiled=True) for x in sent
    ]

    own = lax.axis_index(("mode", "fc"))
    home = home_freqs.astype(F32).reshape(groups, group)
    home = jnp.pad(home, ((0, 0), (0, share * n_qp - group)), constant_values=1.0)
    home = lax.dynamic_slice(home, (own, here * share), (1, share)).reshape(share)

    shared = arrange(pack)
    parts, widths = [], []
    for (first, count), block in zip(chunks, moved):
        found = coupling(
            shared[0], shared[1], home[first : first + count], *shared[2:], block
        )
        back = lax.all_to_all(
            found.reshape(n_qp, own_pairs, found.shape[1], modes),
            "qp",
            split_axis=0,
            concat_axis=0,
            tiled=True,
        )
        widths.append(back[:, 0, count, :count])
        parts.append(back[:, :, :count, :])
    widths = jnp.concatenate(widths, axis=1).reshape(n_qp * share)[:group]
    collision = jnp.transpose(jnp.concatenate(parts, axis=2), (0, 2, 1, 3))
    collision = collision.reshape(n_qp * share, own_pairs, modes)[:group]
    return (widths, collision)


def solution(mesh):
    placed = (
        P("grp", None),
        P("grp"),
        P("qp", None, None),
        P("qp", None),
        P(None, ("mode", "fc")),
        P(("grp", "qp")),
        P(("grp", "qp")),
    )
    return jax.shard_map(
        local,
        mesh=mesh,
        in_specs=placed,
        out_specs=(P(("grp", "mode", "fc")), P(("mode", "fc"), ("grp", "qp"), None)),
        check_vma=False,
    )
```

```python
import functools
import math

import jax
import jax.numpy as jnp
from jax import lax
from jax.experimental import pallas as pl
from jax.experimental.pallas import tpu as pltpu
from jax.sharding import PartitionSpec as P

thermal_reservoir_kelvin = 1.0
smearing = 0.25

MAIN = 256
TILE = 128
F32 = jnp.float32
BF16 = jnp.bfloat16


def ceil_div(a, b):
    return -(-a // b)


def occupy(energy):
    return 1.0 / (jnp.exp(energy / thermal_reservoir_kelvin) - 1.0)


def dot_nn(a, b):
    return lax.dot_general(a, b, (((1,), (0,)), ((), ())), preferred_element_type=F32)


def dot_nt(a, b):
    return lax.dot_general(a, b, (((1,), (1,)), ((), ())), preferred_element_type=F32)


def slots_of(count, modes):
    return count + ceil_div(count, MAIN // (modes - MAIN))


def project_kernel(groups, n_qp, group, chunks, here_ref, home_ref, force_ref, *refs):
    outs = refs[: len(chunks)]
    rows_ref, main_ref, rest_ref = refs[len(chunks) :]
    modes = home_ref.shape[0]
    lines = rows_ref.shape[0]
    share = lines // groups
    rest = modes - MAIN
    per_slot = MAIN // rest
    depth = outs[0].shape[2]
    step = pl.program_id(0)
    here = force_ref.shape[1] // modes

    @pl.when(step == 0)
    def _():
        line = lax.broadcasted_iota(jnp.int32, (lines, modes), 0)
        column = lax.broadcasted_iota(jnp.int32, (lines, modes), 1)
        own = here_ref[0] * share + line % share
        wanted = (line // share) * group + own
        select = jnp.logical_and(column == wanted, own < group).astype(BF16)
        rows_ref[...] = dot_nt(select, home_ref[...]).astype(BF16)

    result = dot_nn(rows_ref[...], force_ref[...])
    for c in range(here):
        row = pl.multiple_of((step * here + c) * lines, 8)
        piece = result[:, c * modes : (c + 1) * modes]
        main_ref[0, pl.ds(row, lines), :] = piece[:, :TILE]
        main_ref[1, pl.ds(row, lines), :] = piece[:, TILE:MAIN]
        rest_ref[pl.ds(row, lines), :] = jnp.concatenate(
            [piece[:, MAIN:], jnp.zeros((lines, TILE - rest), F32)], axis=1
        )

    @pl.when(step == pl.num_programs(0) - 1)
    def _():
        lane = lax.broadcasted_iota(jnp.int32, (depth, TILE), 1)
        for (first, count), out_ref in zip(chunks, outs):
            for t in range(groups):
                base = t * share + first
                for r in range(count):
                    for h in range(2):
                        out_ref[t, r, :, h * TILE : (h + 1) * TILE] = main_ref[
                            h, pl.ds(base + r, depth, stride=lines), :
                        ].astype(BF16)
                for g in range(ceil_div(count, per_slot)):
                    for h in range(2):
                        packed = jnp.zeros((depth, TILE), F32)
                        for b in range(per_slot // 2):
                            r = g * per_slot + h * (per_slot // 2) + b
                            if r < count:
                                piece = rest_ref[pl.ds(base + r, depth, stride=lines), :]
                                if b > 0:
                                    piece = pltpu.roll(piece, b * rest, 1)
                                packed = jnp.where(lane // rest == b, piece, packed)
                        out_ref[t, count + g, :, h * TILE : (h + 1) * TILE] = packed.astype(BF16)


def project(here, home_vectors, force_table, groups, n_qp, group, share, chunks):
    modes = home_vectors.shape[0]
    lines = groups * share
    depth = force_table.shape[1] // modes
    per_step = 8 if depth % 8 == 0 else 4
    steps = depth // per_step
    shapes = [(groups, slots_of(count, modes), depth, MAIN) for _, count in chunks]
    return pl.pallas_call(
        functools.partial(project_kernel, groups, n_qp, group, chunks),
        grid=(steps,),
        in_specs=[
            pl.BlockSpec(memory_space=pltpu.SMEM),
            pl.BlockSpec((modes, modes), lambda i: (0, 0)),
            pl.BlockSpec((modes, per_step * modes), lambda i: (0, i)),
        ],
        out_specs=[pl.BlockSpec(shape, lambda i: (0, 0, 0, 0)) for shape in shapes],
        out_shape=[jax.ShapeDtypeStruct(shape, BF16) for shape in shapes],
        scratch_shapes=[
            pltpu.VMEM((lines, modes), BF16),
            pltpu.VMEM((2, depth * lines, TILE), F32),
            pltpu.VMEM((depth * lines, TILE), F32),
        ],
        compiler_params=pltpu.CompilerParams(vmem_limit_bytes=56 << 20),
        name="project",
    )(here, home_vectors, force_table)


def identity(size):
    return (
        lax.broadcasted_iota(jnp.int32, (size, size), 0)
        == lax.broadcasted_iota(jnp.int32, (size, size), 1)
    ).astype(BF16)


def arrange_kernel(
    pack_ref, partner_ref, weight_ref, grid_ref, grid_t_ref, freq_row_ref, freq_col_ref
):
    owners, parts, each, rows, modes = pack_ref.shape
    half = modes // parts
    rest = modes - MAIN
    eye = identity(modes)
    source = lax.broadcasted_iota(jnp.int32, (modes, MAIN + TILE), 0)
    place = lax.broadcasted_iota(jnp.int32, (modes, MAIN + TILE), 1)
    wanted = jnp.where(place < MAIN, place, MAIN + (place - MAIN) % rest)
    spread = (source == wanted).astype(BF16)
    lane = lax.broadcasted_iota(jnp.int32, freq_col_ref.shape, 1)
    lane16 = lax.broadcasted_iota(jnp.int32, (16, modes), 1)
    line16 = lax.broadcasted_iota(jnp.int32, (16, modes), 0)
    freq_col_ref[...] = jnp.zeros_like(freq_col_ref)

    def one(q, carry):
        for s in range(each):
            x = q * each + s
            for part in range(parts):
                grid_ref[x, part * half : (part + 1) * half, :] = pack_ref[q, part, s, :half, :]
            grid_t_ref[x] = dot_nt(eye, grid_ref[x]).astype(BF16)
            side = pack_ref[q, 0, s, half : half + 16, :]
            freq_row_ref[x] = dot_nn(side, spread)[0:1, :]
            column = dot_nt(eye, side)[:, 0:1]
            freq_col_ref[...] = jnp.where(lane == x, column, freq_col_ref[...])
            wide = side.astype(F32)
            for spot, ref in ((0, partner_ref), (1, weight_ref)):
                found = jnp.sum(
                    jnp.where(jnp.logical_and(line16 == 1, lane16 == spot), wide, 0.0)
                )
                ref[x] = found.astype(ref.dtype)
        return carry

    lax.fori_loop(0, owners, one, 0)


def arrange(pack):
    owners, parts, each, _, modes = pack.shape
    pairs = owners * each
    smem = pl.BlockSpec(memory_space=pltpu.SMEM)
    vmem = pl.BlockSpec(memory_space=pltpu.VMEM)
    return pl.pallas_call(
        arrange_kernel,
        in_specs=[vmem],
        out_specs=[smem, smem, vmem, vmem, vmem, vmem],
        out_shape=[
            jax.ShapeDtypeStruct((pairs,), jnp.int32),
            jax.ShapeDtypeStruct((pairs,), F32),
            jax.ShapeDtypeStruct((pairs, modes, modes), BF16),
            jax.ShapeDtypeStruct((pairs, modes, modes), BF16),
            jax.ShapeDtypeStruct((pairs, 1, MAIN + TILE), F32),
            jax.ShapeDtypeStruct((modes, TILE), F32),
        ],
        compiler_params=pltpu.CompilerParams(vmem_limit_bytes=56 << 20),
        name="arrange",
    )(pack)


def interleave(heavy, light):
    done = 0
    for i, task in enumerate(heavy):
        task()
        upto = (i + 1) * len(light) // len(heavy)
        while done < upto:
            light[done]()
            done += 1
    while done < len(light):
        light[done]()
        done += 1


def coupling_kernel(
    share,
    block,
    partner_ref,
    weight_ref,
    home_ref,
    grid_ref,
    grid_t_ref,
    freq_row_ref,
    freq_col_ref,
    home_row_ref,
    moved_ref,
    out_ref,
    turned_ref,
    grid_rest_ref,
    inner_rest_ref,
    gather_ref,
    pick_ref,
    rest_value_ref,
    *work,
):
    inners, values, tabs, sums, firsts = (work[2 * i : 2 * i + 2] for i in range(5))
    pairs = grid_ref.shape[0]
    modes = grid_ref.shape[2]
    rest = modes - MAIN
    sources, depth = moved_ref.shape[0], moved_ref.shape[2]
    per_slot = MAIN // rest
    rest_lanes = home_row_ref.shape[1]
    s2 = smearing * smearing
    steps = share // block

    for x in range(pairs):
        grid_rest_ref[x * rest : (x + 1) * rest, :] = grid_t_ref[x, MAIN:, :]
    eye = identity(modes)
    if share * rest < rest_lanes:
        inner_rest_ref[...] = jnp.zeros_like(inner_rest_ref)
    for r in range(share):
        slot, spot = share + r // per_slot, r % per_slot
        half, spot = spot // (per_slot // 2), spot % (per_slot // 2)
        for s in range(sources):
            gather_ref[s * depth : (s + 1) * depth, :MAIN] = moved_ref[s, r].astype(F32)
            tail = moved_ref[s, slot, :, half * TILE : (half + 1) * TILE].astype(F32)
            if spot > 0:
                tail = pltpu.roll(tail, TILE - spot * rest, 1)
            gather_ref[s * depth : (s + 1) * depth, MAIN:] = tail[:, :rest]
        whole = gather_ref[...].astype(BF16)
        turned_ref[r * modes : (r + 1) * modes, :] = dot_nt(eye, whole).astype(BF16)
        found = dot_nn(grid_rest_ref[...], whole).astype(BF16)
        for x in range(pairs):
            inner_rest_ref[x, r * rest : (r + 1) * rest, :] = found[x * rest : (x + 1) * rest, :]

    row_id = lax.broadcasted_iota(jnp.int32, pick_ref.shape, 0)
    col_id = lax.broadcasted_iota(jnp.int32, pick_ref.shape, 1)
    branch = jnp.where(
        row_id < share * TILE, row_id // TILE, (row_id - share * TILE) // rest
    )
    pick_ref[...] = (branch == col_id).astype(BF16)
    for ref in (out_ref, *sums, *firsts):
        ref[...] = jnp.zeros_like(ref)

    def contract_first(x, r, b, into):
        def task():
            found = dot_nn(turned_ref[r * modes : (r + 1) * modes, :], grid_ref[x, :, :MAIN])
            into[:, b * MAIN : (b + 1) * MAIN] = found.astype(BF16)

        return task

    def contract_second(x, b, source, into):
        lanes = slice(b * MAIN, (b + 1) * MAIN)

        def task():
            into[:, lanes] = dot_nn(grid_t_ref[partner_ref[x]], source[:, lanes])

        return task

    def line_shapes(v, t, w, c1, c2):
        p = v * v
        d = t[0] - w
        e = t[1] - c1
        return (
            (p * t[2]) * pl.reciprocal(d * d + s2, approx=True),
            (p * t[3]) * pl.reciprocal(e * e + c2, approx=True),
        )

    def weigh(step, source, tab, sum_ref, first_ref):
        state = {}

        def begin():
            state["w"] = [home_ref[step * block + b] for b in range(block)]
            state["c1"] = [w * w - s2 for w in state["w"]]
            state["c2"] = [(4.0 * s2) * (w * w) for w in state["w"]]
            state["total"] = [jnp.zeros((8, MAIN), F32) for _ in range(block)]

        def rows(n):
            def task():
                if n == 0:
                    begin()
                t = [tab[k, n : n + 16, :MAIN] for k in range(4)]
                for b in range(block):
                    v = source[n : n + 16, b * MAIN : (b + 1) * MAIN]
                    f, u = line_shapes(v, t, state["w"][b], state["c1"][b], state["c2"][b])
                    state["total"][b] = state["total"][b] + (f[:8] + f[8:])
                    r = step * block + b
                    sum_ref[n : n + 16, r * TILE : (r + 1) * TILE] = (
                        u[:, :TILE] + u[:, TILE:]
                    ).astype(BF16)
                if n + 16 == modes:
                    for b in range(block):
                        r = step * block + b
                        line = jnp.sum(state["total"][b], axis=0, keepdims=True)
                        first_ref[r : r + 1, :MAIN] = line * (1.0 / state["w"][b])

            return task

        return [rows(n) for n in range(0, modes, 16)]

    def contract_rest(x):
        def task():
            rest_value_ref[...] = dot_nt(grid_t_ref[partner_ref[x]], inner_rest_ref[x])

        return task

    def weigh_rest(tab, sum_ref, first_ref):
        def tile(start):
            lanes = slice(start, start + TILE)
            spot = share * TILE + start
            state = {}

            def rows(n):
                def task():
                    if n == 0:
                        state["total"] = jnp.zeros((8, TILE), F32)
                        state["w"] = home_row_ref[0:1, lanes]
                        state["c1"] = home_row_ref[1:2, lanes]
                        state["c2"] = home_row_ref[2:3, lanes]
                    for k in range(n, n + 48, 16):
                        t = [tab[i, k : k + 16, MAIN:] for i in range(4)]
                        f, u = line_shapes(
                            rest_value_ref[k : k + 16, lanes], t, state["w"], state["c1"], state["c2"]
                        )
                        state["total"] = state["total"] + (f[:8] + f[8:])
                        sum_ref[k : k + 16, spot : spot + TILE] = u.astype(BF16)
                    if n + 48 == modes:
                        line = jnp.sum(state["total"], axis=0, keepdims=True)
                        line = line * home_row_ref[3:4, lanes]
                        for b in range(TILE // rest):
                            r = start // rest + b
                            if r < share:
                                first_ref[r : r + 1, MAIN:] = line[:, b * rest : (b + 1) * rest]

                return task

            return [rows(n) for n in range(0, modes, 48)]

        return [task for start in range(0, rest_lanes, TILE) for task in tile(start)]

    def tables(x, tab):
        state = {}

        def begin():
            w1 = freq_row_ref[x]
            spots = lax.broadcasted_iota(jnp.int32, freq_col_ref.shape, 1)
            w2 = jnp.sum(
                jnp.where(spots == partner_ref[x], freq_col_ref[...], 0.0), axis=1, keepdims=True
            )
            state["w"] = (w1, w2)
            state["o"] = (occupy(w1), occupy(w2))
            scale = weight_ref[x] * (smearing / math.pi / modes)
            state["i"] = (scale / w1, 1.0 / w2)

        def rows(n):
            def task():
                if n == 0:
                    begin()
                part = slice(n, n + 48)
                (w1, w2), (o1, o2), (i1, i2) = state["w"], state["o"], state["i"]
                w2, o2, i2 = w2[part], o2[part], i2[part]
                a = w1 - w2
                both = i1 * i2
                tab[0, part, :] = w1 + w2
                tab[1, part, :] = a * a
                tab[2, part, :] = (1.0 + o1 + o2) * both
                tab[3, part, :] = (4.0 * a) * (o2 - o1) * both

            return task

        return [rows(n) for n in range(0, modes, 48)]

    def finish(x, target, sum_ref, first_ref):
        second = dot_nn(sum_ref[...], pick_ref[...])
        out_ref[x, :share, :] += first_ref[:share, :]
        out_ref[target, :share, :] += second.T[:share, :]

    for task in tables(0, tabs[0]):
        task()
    for g in range(2):
        for b in range(block):
            x, step = jnp.int32(g // steps), g % steps
            contract_first(x, step * block + b, b, inners[g])()
    for b in range(block):
        contract_second(jnp.int32(0), b, inners[0], values[0])()

    def two_pairs(i, carry):
        for e in range(2):
            x = i * 2 + e

            def later(g):
                return jnp.minimum(i * 2 + g // steps, pairs - 1), g % steps

            before = jnp.maximum(x - 1, 0)
            target = partner_ref[before]
            finish_sum, finish_first = sums[1 - e], firsts[1 - e]
            extra = weigh_rest(tabs[e], sums[e], firsts[e])
            extra = extra + tables(jnp.minimum(x + 1, pairs - 1), tabs[1 - e])
            contract_rest(x)()
            for s in range(steps):
                g = e * steps + s
                heavy = []
                for b in range(block):
                    x1, _ = later(g + 1)
                    heavy.append(contract_second(x1, b, inners[(g + 1) % 2], values[(g + 1) % 2]))
                for b in range(block):
                    x2, step2 = later(g + 2)
                    heavy.append(contract_first(x2, step2 * block + b, b, inners[g % 2]))
                light = weigh(s, values[g % 2], tabs[e], sums[e], firsts[e])
                light = light + extra[s * len(extra) // steps : (s + 1) * len(extra) // steps]
                interleave(heavy, light)
            finish(before, target, finish_sum, finish_first)
        return carry

    lax.fori_loop(0, pairs // 2, two_pairs, 0)
    finish(pairs - 1, partner_ref[pairs - 1], sums[1], firsts[1])

    totals = jnp.zeros(out_ref.shape[1:], F32)
    for y in range(pairs):
        totals = totals + out_ref[y]
    widths = jnp.sum(totals, axis=1, keepdims=True) * (1.0 / (pairs * modes))
    spread = jnp.where(
        lax.broadcasted_iota(jnp.int32, totals.shape, 0)
        == lax.broadcasted_iota(jnp.int32, totals.shape, 1),
        widths,
        0.0,
    )
    out_ref[:, share, :] = jnp.broadcast_to(
        jnp.sum(spread, axis=0, keepdims=True), (pairs, modes)
    )


def coupling(partner, weights, home, grid, grid_t, freq_rows, freq_cols, moved):
    pairs, modes = grid.shape[0], grid.shape[2]
    share = home.shape[0]
    rest = modes - MAIN
    rest_lanes = ceil_div(share * rest, TILE) * TILE
    row = jnp.repeat(home, rest)
    row = jnp.pad(row, (0, rest_lanes - share * rest), constant_values=1.0)
    s2 = smearing * smearing
    home_row = jnp.stack([row, row * row - s2, (4.0 * s2) * (row * row), 1.0 / row])
    padded = (share // 8 + 1) * 8
    smem = pl.BlockSpec(memory_space=pltpu.SMEM)
    vmem = pl.BlockSpec(memory_space=pltpu.VMEM)
    tiles = share + rest_lanes // TILE
    block = 3 if share % 3 == 0 else 1
    assert pairs % 2 == 0
    return pl.pallas_call(
        functools.partial(coupling_kernel, share, block),
        in_specs=[smem, smem, smem, vmem, vmem, vmem, vmem, vmem, vmem],
        out_specs=vmem,
        out_shape=jax.ShapeDtypeStruct((pairs, padded, modes), F32),
        scratch_shapes=[
            pltpu.VMEM((share * modes, modes), BF16),
            pltpu.VMEM((pairs * rest, modes), BF16),
            pltpu.VMEM((pairs, rest_lanes, modes), BF16),
            pltpu.VMEM((modes, modes), F32),
            pltpu.VMEM((tiles * TILE, TILE), BF16),
            pltpu.VMEM((modes, rest_lanes), F32),
        ]
        + [pltpu.VMEM((modes, block * MAIN), BF16)] * 2
        + [pltpu.VMEM((modes, block * MAIN), F32)] * 2
        + [pltpu.VMEM((4, modes, MAIN + TILE), F32)] * 2
        + [pltpu.VMEM((modes, tiles * TILE), BF16)] * 2
        + [pltpu.VMEM((padded, modes), F32)] * 2,
        compiler_params=pltpu.CompilerParams(vmem_limit_bytes=56 << 20),
        cost_estimate=pl.CostEstimate(
            flops=4 * share * pairs * modes**3,
            bytes_accessed=8 * share * modes * modes,
            transcendentals=2 * share * pairs * modes**2,
        ),
        name="coupling",
    )(partner, weights, home, grid, grid_t, freq_rows, freq_cols, home_row, moved)


def local(
    home_vectors, home_freqs, grid_vectors, partner_frequencies, force_table, partner, weights
):
    own_pairs = partner.shape[0]
    modes = home_vectors.shape[0]
    n_mode = lax.axis_size("mode")
    n_fc = lax.axis_size("fc")
    n_qp = lax.axis_size("qp")
    groups = n_mode * n_fc
    group = modes // groups
    pairs = own_pairs * n_qp
    share = ceil_div(group, n_qp)
    here = lax.axis_index("qp")
    if share % 6 == 0 and share > 6:
        chunks = ((0, 6), (6, share - 6))
    else:
        chunks = ((0, share),)

    part_rows = modes // n_fc
    part = lax.dynamic_slice_in_dim(
        grid_vectors, lax.axis_index("fc") * part_rows, part_rows, axis=1
    )
    lane = jnp.arange(modes)[None]
    small = jnp.where(lane == 0, partner[:, None], jnp.where(lane == 1, weights[:, None], 0))
    side = jnp.stack([partner_frequencies, small.astype(BF16)], axis=1)
    side = jnp.pad(side, ((0, 0), (0, 14), (0, 0)))
    pack = lax.all_gather(jnp.concatenate([part, side], axis=1), ("qp", "fc"), axis=0)
    pack = pack.reshape(n_qp, n_fc, own_pairs, part_rows + 16, modes)

    sent = project(
        here.astype(jnp.int32)[None], home_vectors, force_table, groups, n_qp, group, share, chunks
    )
    moved = [
        lax.all_to_all(x, ("mode", "fc"), split_axis=0, concat_axis=0, tiled=True) for x in sent
    ]

    own = lax.axis_index(("mode", "fc"))
    home = home_freqs.astype(F32).reshape(groups, group)
    home = jnp.pad(home, ((0, 0), (0, share * n_qp - group)), constant_values=1.0)
    home = lax.dynamic_slice(home, (own, here * share), (1, share)).reshape(share)

    shared = arrange(pack)
    parts, widths = [], []
    for (first, count), block in zip(chunks, moved):
        found = coupling(
            shared[0], shared[1], home[first : first + count], *shared[2:], block
        )
        back = lax.all_to_all(
            found.reshape(n_qp, own_pairs, found.shape[1], modes),
            "qp",
            split_axis=0,
            concat_axis=0,
            tiled=True,
        )
        widths.append(back[:, 0, count, :count])
        parts.append(back[:, :, :count, :])
    widths = jnp.concatenate(widths, axis=1).reshape(n_qp * share)[:group]
    collision = jnp.transpose(jnp.concatenate(parts, axis=2), (0, 2, 1, 3))
    collision = collision.reshape(n_qp * share, own_pairs, modes)[:group]
    return (widths, collision)


def solution(mesh):
    placed = (
        P("grp", None),
        P("grp"),
        P("qp", None, None),
        P("qp", None),
        P(None, ("mode", "fc")),
        P(("grp", "qp")),
        P(("grp", "qp")),
    )
    return jax.shard_map(
        local,
        mesh=mesh,
        in_specs=placed,
        out_specs=(P(("grp", "mode", "fc")), P(("mode", "fc"), ("grp", "qp"), None)),
        check_vma=False,
    )
```

```python
import functools
import math

import jax
import jax.numpy as jnp
from jax import lax
from jax.experimental import pallas as pl
from jax.experimental.pallas import tpu as pltpu
from jax.sharding import PartitionSpec as P

thermal_reservoir_kelvin = 1.0
smearing = 0.25

MAIN = 256
TILE = 128
F32 = jnp.float32
BF16 = jnp.bfloat16


def ceil_div(a, b):
    return -(-a // b)


def grant(shapes):
    total = 0
    for shape, dtype in shapes:
        rows, lanes = shape[-2:]
        size = ceil_div(rows, 16) * 16 * ceil_div(lanes, TILE) * TILE * jnp.dtype(dtype).itemsize
        total += math.prod(shape[:-2]) * size
    return total + total // 8 + (4 << 20)


def occupy(energy):
    return 1.0 / (jnp.exp(energy / thermal_reservoir_kelvin) - 1.0)


def dot_nn(a, b):
    return lax.dot_general(a, b, (((1,), (0,)), ((), ())), preferred_element_type=F32)


def dot_nt(a, b):
    return lax.dot_general(a, b, (((1,), (1,)), ((), ())), preferred_element_type=F32)


def slots_of(count, modes):
    return count + ceil_div(count, MAIN // (modes - MAIN))


def project_kernel(groups, n_qp, group, chunks, here_ref, home_ref, force_ref, *refs):
    outs = refs[: len(chunks)]
    rows_ref, main_ref, rest_ref = refs[len(chunks) :]
    modes = home_ref.shape[0]
    lines = rows_ref.shape[0]
    share = lines // groups
    rest = modes - MAIN
    per_slot = MAIN // rest
    depth = outs[0].shape[2]
    step = pl.program_id(0)
    here = force_ref.shape[1] // modes

    @pl.when(step == 0)
    def _():
        line = lax.broadcasted_iota(jnp.int32, (lines, modes), 0)
        column = lax.broadcasted_iota(jnp.int32, (lines, modes), 1)
        own = here_ref[0] * share + line % share
        wanted = (line // share) * group + own
        select = jnp.logical_and(column == wanted, own < group).astype(BF16)
        rows_ref[...] = dot_nt(select, home_ref[...]).astype(BF16)

    result = dot_nn(rows_ref[...], force_ref[...])
    for c in range(here):
        row = pl.multiple_of((step * here + c) * lines, 8)
        piece = result[:, c * modes : (c + 1) * modes]
        main_ref[0, pl.ds(row, lines), :] = piece[:, :TILE]
        main_ref[1, pl.ds(row, lines), :] = piece[:, TILE:MAIN]
        rest_ref[pl.ds(row, lines), :] = jnp.concatenate(
            [piece[:, MAIN:], jnp.zeros((lines, TILE - rest), F32)], axis=1
        )

    @pl.when(step == pl.num_programs(0) - 1)
    def _():
        lane = lax.broadcasted_iota(jnp.int32, (depth, TILE), 1)
        for (first, count), out_ref in zip(chunks, outs):
            for t in range(groups):
                base = t * share + first
                for r in range(count):
                    for h in range(2):
                        out_ref[t, r, :, h * TILE : (h + 1) * TILE] = main_ref[
                            h, pl.ds(base + r, depth, stride=lines), :
                        ].astype(BF16)
                for g in range(ceil_div(count, per_slot)):
                    for h in range(2):
                        packed = jnp.zeros((depth, TILE), F32)
                        for b in range(per_slot // 2):
                            r = g * per_slot + h * (per_slot // 2) + b
                            if r < count:
                                piece = rest_ref[pl.ds(base + r, depth, stride=lines), :]
                                if b > 0:
                                    piece = pltpu.roll(piece, b * rest, 1)
                                packed = jnp.where(lane // rest == b, piece, packed)
                        out_ref[t, count + g, :, h * TILE : (h + 1) * TILE] = packed.astype(BF16)


def project(here, home_vectors, force_table, groups, n_qp, group, share, chunks):
    modes = home_vectors.shape[0]
    lines = groups * share
    depth = force_table.shape[1] // modes
    per_step = 8 if depth % 8 == 0 else 4
    steps = depth // per_step
    shapes = [(groups, slots_of(count, modes), depth, MAIN) for _, count in chunks]
    return pl.pallas_call(
        functools.partial(project_kernel, groups, n_qp, group, chunks),
        grid=(steps,),
        in_specs=[
            pl.BlockSpec(memory_space=pltpu.SMEM),
            pl.BlockSpec((modes, modes), lambda i: (0, 0)),
            pl.BlockSpec((modes, per_step * modes), lambda i: (0, i)),
        ],
        out_specs=[pl.BlockSpec(shape, lambda i: (0, 0, 0, 0)) for shape in shapes],
        out_shape=[jax.ShapeDtypeStruct(shape, BF16) for shape in shapes],
        scratch_shapes=[
            pltpu.VMEM((lines, modes), BF16),
            pltpu.VMEM((2, depth * lines, TILE), F32),
            pltpu.VMEM((depth * lines, TILE), F32),
        ],
        compiler_params=pltpu.CompilerParams(vmem_limit_bytes=grant(
                [((modes, per_step * modes), BF16)] * 2
                + [(shape, BF16) for shape in shapes] * 2
                + [((3 * depth * lines, TILE), F32), ((4 * lines, per_step * modes), F32)]
            )),
        name="project",
    )(here, home_vectors, force_table)


def identity(size):
    return (
        lax.broadcasted_iota(jnp.int32, (size, size), 0)
        == lax.broadcasted_iota(jnp.int32, (size, size), 1)
    ).astype(BF16)


def arrange_kernel(
    pack_ref, partner_ref, weight_ref, grid_ref, grid_t_ref, freq_row_ref, freq_col_ref
):
    owners, parts, each, rows, modes = pack_ref.shape
    half = modes // parts
    rest = modes - MAIN
    eye = identity(modes)
    source = lax.broadcasted_iota(jnp.int32, (modes, MAIN + TILE), 0)
    place = lax.broadcasted_iota(jnp.int32, (modes, MAIN + TILE), 1)
    wanted = jnp.where(place < MAIN, place, MAIN + (place - MAIN) % rest)
    spread = (source == wanted).astype(BF16)
    lane = lax.broadcasted_iota(jnp.int32, freq_col_ref.shape, 1)
    lane16 = lax.broadcasted_iota(jnp.int32, (16, modes), 1)
    line16 = lax.broadcasted_iota(jnp.int32, (16, modes), 0)
    freq_col_ref[...] = jnp.zeros_like(freq_col_ref)

    def one(q, carry):
        for s in range(each):
            x = q * each + s
            for part in range(parts):
                grid_ref[x, part * half : (part + 1) * half, :] = pack_ref[q, part, s, :half, :]
            grid_t_ref[x] = dot_nt(eye, grid_ref[x]).astype(BF16)
            side = pack_ref[q, 0, s, half : half + 16, :]
            freq_row_ref[x] = dot_nn(side, spread)[0:1, :]
            column = dot_nt(eye, side)[:, 0:1]
            freq_col_ref[...] = jnp.where(lane == x, column, freq_col_ref[...])
            wide = side.astype(F32)
            for spot, ref in ((0, partner_ref), (1, weight_ref)):
                found = jnp.sum(
                    jnp.where(jnp.logical_and(line16 == 1, lane16 == spot), wide, 0.0)
                )
                ref[x] = found.astype(ref.dtype)
        return carry

    lax.fori_loop(0, owners, one, 0)


def arrange(pack):
    owners, parts, each, _, modes = pack.shape
    pairs = owners * each
    smem = pl.BlockSpec(memory_space=pltpu.SMEM)
    vmem = pl.BlockSpec(memory_space=pltpu.VMEM)
    return pl.pallas_call(
        arrange_kernel,
        in_specs=[vmem],
        out_specs=[smem, smem, vmem, vmem, vmem, vmem],
        out_shape=[
            jax.ShapeDtypeStruct((pairs,), jnp.int32),
            jax.ShapeDtypeStruct((pairs,), F32),
            jax.ShapeDtypeStruct((pairs, modes, modes), BF16),
            jax.ShapeDtypeStruct((pairs, modes, modes), BF16),
            jax.ShapeDtypeStruct((pairs, 1, MAIN + TILE), F32),
            jax.ShapeDtypeStruct((modes, TILE), F32),
        ],
        compiler_params=pltpu.CompilerParams(vmem_limit_bytes=grant(
                [(pack.shape, BF16)] + [((pairs, modes, modes), BF16)] * 2 + [((pairs, 8, modes), F32)]
            )),
        name="arrange",
    )(pack)


def interleave(heavy, light):
    done = 0
    for i, task in enumerate(heavy):
        task()
        upto = (i + 1) * len(light) // len(heavy)
        while done < upto:
            light[done]()
            done += 1
    while done < len(light):
        light[done]()
        done += 1


def coupling_kernel(
    share,
    block,
    partner_ref,
    weight_ref,
    home_ref,
    grid_ref,
    grid_t_ref,
    freq_row_ref,
    freq_col_ref,
    home_row_ref,
    moved_ref,
    out_ref,
    turned_ref,
    grid_rest_ref,
    inner_rest_ref,
    pick_ref,
    rest_value_ref,
    *work,
):
    gathers, inners, values, tabs, sums, rest_sums, firsts = (
        work[2 * i : 2 * i + 2] for i in range(7)
    )
    pairs = grid_ref.shape[0]
    modes = grid_ref.shape[2]
    rest = modes - MAIN
    sources, depth = moved_ref.shape[0], moved_ref.shape[2]
    per_slot = MAIN // rest
    rest_lanes = home_row_ref.shape[1]
    s2 = smearing * smearing
    steps = share // block

    for x in range(pairs):
        grid_rest_ref[x * rest : (x + 1) * rest, :] = grid_t_ref[x, MAIN:, :]
    eye = identity(modes)
    if share * rest < rest_lanes:
        inner_rest_ref[...] = jnp.zeros_like(inner_rest_ref)
    for r in range(share):
        slot, spot = share + r // per_slot, r % per_slot
        half, spot = spot // (per_slot // 2), spot % (per_slot // 2)
        gather_ref = gathers[r % 2]
        for s in range(sources):
            gather_ref[s * depth : (s + 1) * depth, :MAIN] = moved_ref[s, r].astype(F32)
            tail = moved_ref[s, slot, :, half * TILE : (half + 1) * TILE].astype(F32)
            if spot > 0:
                tail = pltpu.roll(tail, TILE - spot * rest, 1)
            gather_ref[s * depth : (s + 1) * depth, MAIN:] = tail[:, :rest]
        whole = gather_ref[...].astype(BF16)
        turned_ref[r * modes : (r + 1) * modes, :] = dot_nt(eye, whole).astype(BF16)
        found = dot_nn(grid_rest_ref[...], whole).astype(BF16)
        for x in range(pairs):
            inner_rest_ref[x, r * rest : (r + 1) * rest, :] = found[x * rest : (x + 1) * rest, :]

    row_id = lax.broadcasted_iota(jnp.int32, pick_ref.shape, 0)
    col_id = lax.broadcasted_iota(jnp.int32, pick_ref.shape, 1)
    pick_ref[...] = (row_id // rest == col_id).astype(BF16)
    for ref in (out_ref, *sums, *rest_sums, *firsts):
        ref[...] = jnp.zeros_like(ref)

    def contract_first(x, r, b, into):
        def task():
            found = dot_nn(turned_ref[r * modes : (r + 1) * modes, :], grid_ref[x, :, :MAIN])
            into[:, b * MAIN : (b + 1) * MAIN] = found.astype(BF16)

        return task

    def contract_second(x, b, source, into):
        lanes = slice(b * MAIN, (b + 1) * MAIN)

        def task():
            into[:, lanes] = dot_nn(grid_t_ref[partner_ref[x]], source[:, lanes])

        return task

    def line_shapes(v, t, w, c1, c2):
        p = v * v
        d = t[0] - w
        e = t[1] - c1
        return (
            (p * t[2]) * pl.reciprocal(d * d + s2, approx=True),
            (p * t[3]) * pl.reciprocal(e * e + c2, approx=True),
        )

    def weigh(step, source, tab, sum_ref, first_ref):
        state = {}

        def begin():
            state["w"] = [home_ref[step * block + b] for b in range(block)]
            state["c1"] = [w * w - s2 for w in state["w"]]
            state["c2"] = [(4.0 * s2) * (w * w) for w in state["w"]]
            state["total"] = [jnp.zeros((8, MAIN), F32) for _ in range(block)]

        def rows(n):
            def task():
                if n == 0:
                    begin()
                t = [tab[k, n : n + 16, :MAIN] for k in range(4)]
                for b in range(block):
                    v = source[n : n + 16, b * MAIN : (b + 1) * MAIN]
                    f, u = line_shapes(v, t, state["w"][b], state["c1"][b], state["c2"][b])
                    state["total"][b] = state["total"][b] + (f[:8] + f[8:])
                    r = step * block + b
                    sum_ref[n : n + 16, r : r + 1] = jnp.sum(
                        u[:, :TILE] + u[:, TILE:], axis=1, keepdims=True
                    )
                if n + 16 == modes:
                    for b in range(block):
                        r = step * block + b
                        line = jnp.sum(state["total"][b], axis=0, keepdims=True)
                        first_ref[r : r + 1, :MAIN] = line * (1.0 / state["w"][b])

            return task

        return [rows(n) for n in range(0, modes, 16)]

    def contract_rest(x):
        def task():
            rest_value_ref[...] = dot_nt(grid_t_ref[partner_ref[x]], inner_rest_ref[x])

        return task

    def weigh_rest(tab, sum_ref, first_ref):
        def tile(start):
            lanes = slice(start, start + TILE)
            state = {}

            def rows(n):
                def task():
                    if n == 0:
                        state["total"] = jnp.zeros((8, TILE), F32)
                        state["w"] = home_row_ref[0:1, lanes]
                        state["c1"] = home_row_ref[1:2, lanes]
                        state["c2"] = home_row_ref[2:3, lanes]
                    for k in range(n, n + 48, 16):
                        t = [tab[i, k : k + 16, MAIN:] for i in range(4)]
                        f, u = line_shapes(
                            rest_value_ref[k : k + 16, lanes], t, state["w"], state["c1"], state["c2"]
                        )
                        state["total"] = state["total"] + (f[:8] + f[8:])
                        sum_ref[k : k + 16, lanes] = u.astype(BF16)
                    if n + 48 == modes:
                        line = jnp.sum(state["total"], axis=0, keepdims=True)
                        line = line * home_row_ref[3:4, lanes]
                        for b in range(TILE // rest):
                            r = start // rest + b
                            if r < share:
                                first_ref[r : r + 1, MAIN:] = line[:, b * rest : (b + 1) * rest]

                return task

            return [rows(n) for n in range(0, modes, 48)]

        return [task for start in range(0, rest_lanes, TILE) for task in tile(start)]

    def tables(x, tab):
        state = {}

        def begin():
            w1 = freq_row_ref[x]
            spots = lax.broadcasted_iota(jnp.int32, freq_col_ref.shape, 1)
            w2 = jnp.sum(
                jnp.where(spots == partner_ref[x], freq_col_ref[...], 0.0), axis=1, keepdims=True
            )
            state["w"] = (w1, w2)
            state["o"] = (occupy(w1), occupy(w2))
            scale = weight_ref[x] * (smearing / math.pi / modes)
            state["i"] = (scale / w1, 1.0 / w2)

        def rows(n):
            def task():
                if n == 0:
                    begin()
                part = slice(n, n + 48)
                (w1, w2), (o1, o2), (i1, i2) = state["w"], state["o"], state["i"]
                w2, o2, i2 = w2[part], o2[part], i2[part]
                a = w1 - w2
                both = i1 * i2
                tab[0, part, :] = w1 + w2
                tab[1, part, :] = a * a
                tab[2, part, :] = (1.0 + o1 + o2) * both
                tab[3, part, :] = (4.0 * a) * (o2 - o1) * both

            return task

        return [rows(n) for n in range(0, modes, 48)]

    def finish(x, target, sum_ref, rest_sum_ref, first_ref):
        second = sum_ref[...] + dot_nn(rest_sum_ref[...], pick_ref[...])
        out_ref[x, :share, :] += first_ref[:share, :]
        out_ref[target, :share, :] += second.T[:share, :]

    for task in tables(0, tabs[0]):
        task()
    for g in range(2):
        for b in range(block):
            x, step = jnp.int32(g // steps), g % steps
            contract_first(x, step * block + b, b, inners[g])()
    for b in range(block):
        contract_second(jnp.int32(0), b, inners[0], values[0])()

    def two_pairs(i, carry):
        for e in range(2):
            x = i * 2 + e

            def later(g):
                return jnp.minimum(i * 2 + g // steps, pairs - 1), g % steps

            before = jnp.maximum(x - 1, 0)
            target = partner_ref[before]
            extra = weigh_rest(tabs[e], rest_sums[e], firsts[e])
            extra = extra + tables(jnp.minimum(x + 1, pairs - 1), tabs[1 - e])
            contract_rest(x)()
            for s in range(steps):
                g = e * steps + s
                heavy = []
                for b in range(block):
                    x1, _ = later(g + 1)
                    heavy.append(contract_second(x1, b, inners[(g + 1) % 2], values[(g + 1) % 2]))
                for b in range(block):
                    x2, step2 = later(g + 2)
                    heavy.append(contract_first(x2, step2 * block + b, b, inners[g % 2]))
                light = weigh(s, values[g % 2], tabs[e], sums[e], firsts[e])
                light = light + extra[s * len(extra) // steps : (s + 1) * len(extra) // steps]
                interleave(heavy, light)
            finish(before, target, sums[1 - e], rest_sums[1 - e], firsts[1 - e])
        return carry

    lax.fori_loop(0, pairs // 2, two_pairs, 0)
    finish(pairs - 1, partner_ref[pairs - 1], sums[1], rest_sums[1], firsts[1])

    totals = jnp.zeros(out_ref.shape[1:], F32)
    for y in range(pairs):
        totals = totals + out_ref[y]
    widths = jnp.sum(totals, axis=1, keepdims=True) * (1.0 / (pairs * modes))
    spread = jnp.where(
        lax.broadcasted_iota(jnp.int32, totals.shape, 0)
        == lax.broadcasted_iota(jnp.int32, totals.shape, 1),
        widths,
        0.0,
    )
    out_ref[:, share, :] = jnp.broadcast_to(
        jnp.sum(spread, axis=0, keepdims=True), (pairs, modes)
    )


def coupling(partner, weights, home, grid, grid_t, freq_rows, freq_cols, moved):
    pairs, modes = grid.shape[0], grid.shape[2]
    share = home.shape[0]
    rest = modes - MAIN
    rest_lanes = ceil_div(share * rest, TILE) * TILE
    row = jnp.repeat(home, rest)
    row = jnp.pad(row, (0, rest_lanes - share * rest), constant_values=1.0)
    s2 = smearing * smearing
    home_row = jnp.stack([row, row * row - s2, (4.0 * s2) * (row * row), 1.0 / row])
    padded = (share // 8 + 1) * 8
    smem = pl.BlockSpec(memory_space=pltpu.SMEM)
    vmem = pl.BlockSpec(memory_space=pltpu.VMEM)
    block = 3 if share % 3 == 0 else 1
    assert pairs % 2 == 0
    scratch = (
        [
            pltpu.VMEM((share * modes, modes), BF16),
            pltpu.VMEM((pairs * rest, modes), BF16),
            pltpu.VMEM((pairs, rest_lanes, modes), BF16),
            pltpu.VMEM((rest_lanes, TILE), BF16),
            pltpu.VMEM((modes, rest_lanes), F32),
        ]
        + [pltpu.VMEM((modes, modes), F32)] * 2
        + [pltpu.VMEM((modes, block * MAIN), BF16)] * 2
        + [pltpu.VMEM((modes, block * MAIN), F32)] * 2
        + [pltpu.VMEM((4, modes, MAIN + TILE), F32)] * 2
        + [pltpu.VMEM((modes, TILE), F32)] * 2
        + [pltpu.VMEM((modes, rest_lanes), BF16)] * 2
        + [pltpu.VMEM((padded, modes), F32)] * 2
    )
    held = [(x.shape, x.dtype) for x in (grid, grid_t, freq_rows, freq_cols, moved)]
    held += [(x.shape, x.dtype) for x in scratch] + [((pairs, padded, modes), F32)] * 2
    return pl.pallas_call(
        functools.partial(coupling_kernel, share, block),
        in_specs=[smem, smem, smem, vmem, vmem, vmem, vmem, vmem, vmem],
        out_specs=vmem,
        out_shape=jax.ShapeDtypeStruct((pairs, padded, modes), F32),
        scratch_shapes=scratch,
        compiler_params=pltpu.CompilerParams(vmem_limit_bytes=grant(held)),
        cost_estimate=pl.CostEstimate(
            flops=4 * share * pairs * modes**3,
            bytes_accessed=8 * share * modes * modes,
            transcendentals=2 * share * pairs * modes**2,
        ),
        name="coupling",
    )(partner, weights, home, grid, grid_t, freq_rows, freq_cols, home_row, moved)


def local(
    home_vectors, home_freqs, grid_vectors, partner_frequencies, force_table, partner, weights
):
    own_pairs = partner.shape[0]
    modes = home_vectors.shape[0]
    n_mode = lax.axis_size("mode")
    n_fc = lax.axis_size("fc")
    n_qp = lax.axis_size("qp")
    groups = n_mode * n_fc
    group = modes // groups
    pairs = own_pairs * n_qp
    share = ceil_div(group, n_qp)
    here = lax.axis_index("qp")
    if share % 6 == 0 and share > 6:
        chunks = ((0, share - 6), (share - 6, 6))
    else:
        chunks = ((0, share),)

    part_rows = modes // n_fc
    part = lax.dynamic_slice_in_dim(
        grid_vectors, lax.axis_index("fc") * part_rows, part_rows, axis=1
    )
    lane = jnp.arange(modes)[None]
    small = jnp.where(lane == 0, partner[:, None], jnp.where(lane == 1, weights[:, None], 0))
    side = jnp.stack([partner_frequencies, small.astype(BF16)], axis=1)
    side = jnp.pad(side, ((0, 0), (0, 14), (0, 0)))
    pack = lax.all_gather(jnp.concatenate([part, side], axis=1), ("qp", "fc"), axis=0)
    pack = pack.reshape(n_qp, n_fc, own_pairs, part_rows + 16, modes)

    sent = project(
        here.astype(jnp.int32)[None], home_vectors, force_table, groups, n_qp, group, share, chunks
    )
    moved = [
        lax.all_to_all(x, ("mode", "fc"), split_axis=0, concat_axis=0, tiled=True) for x in sent
    ]

    own = lax.axis_index(("mode", "fc"))
    home = home_freqs.astype(F32).reshape(groups, group)
    home = jnp.pad(home, ((0, 0), (0, share * n_qp - group)), constant_values=1.0)
    home = lax.dynamic_slice(home, (own, here * share), (1, share)).reshape(share)

    shared = arrange(pack)
    parts, widths = [], []
    for (first, count), block in zip(chunks, moved):
        found = coupling(
            shared[0], shared[1], home[first : first + count], *shared[2:], block
        )
        back = lax.all_to_all(
            found.reshape(n_qp, own_pairs, found.shape[1], modes),
            "qp",
            split_axis=0,
            concat_axis=0,
            tiled=True,
        )
        widths.append(back[:, 0, count, :count])
        parts.append(back[:, :, :count, :])
    widths = jnp.concatenate(widths, axis=1).reshape(n_qp * share)[:group]
    collision = jnp.transpose(jnp.concatenate(parts, axis=2), (0, 2, 1, 3))
    collision = collision.reshape(n_qp * share, own_pairs, modes)[:group]
    return (widths, collision)


def solution(mesh):
    placed = (
        P("grp", None),
        P("grp"),
        P("qp", None, None),
        P("qp", None),
        P(None, ("mode", "fc")),
        P(("grp", "qp")),
        P(("grp", "qp")),
    )
    return jax.shard_map(
        local,
        mesh=mesh,
        in_specs=placed,
        out_specs=(P(("grp", "mode", "fc")), P(("mode", "fc"), ("grp", "qp"), None)),
        check_vma=False,
    )
```

```python
import functools
import math

import jax
import jax.numpy as jnp
from jax import lax
from jax.experimental import pallas as pl
from jax.experimental.pallas import tpu as pltpu
from jax.sharding import PartitionSpec as P

thermal_reservoir_kelvin = 1.0
smearing = 0.25

MAIN = 256
TILE = 128
F32 = jnp.float32
BF16 = jnp.bfloat16


def ceil_div(a, b):
    return -(-a // b)


VMEM_BYTES = 56 << 20


def occupy(energy):
    return 1.0 / (jnp.exp(energy / thermal_reservoir_kelvin) - 1.0)


def dot_nn(a, b):
    return lax.dot_general(a, b, (((1,), (0,)), ((), ())), preferred_element_type=F32)


def dot_nt(a, b):
    return lax.dot_general(a, b, (((1,), (1,)), ((), ())), preferred_element_type=F32)


def slots_of(count, modes):
    return count + ceil_div(count, MAIN // (modes - MAIN))


def project_kernel(groups, n_qp, group, chunks, here_ref, home_ref, force_ref, *refs):
    outs = refs[: len(chunks)]
    rows_ref, main_ref, rest_ref = refs[len(chunks) :]
    modes = home_ref.shape[0]
    lines = rows_ref.shape[0]
    share = lines // groups
    rest = modes - MAIN
    per_slot = MAIN // rest
    depth = outs[0].shape[2]
    step = pl.program_id(0)
    here = force_ref.shape[1] // modes
    pitch = lines + 1

    @pl.when(step == 0)
    def _():
        line = lax.broadcasted_iota(jnp.int32, (lines, modes), 0)
        column = lax.broadcasted_iota(jnp.int32, (lines, modes), 1)
        own = here_ref[0] * share + line % share
        wanted = (line // share) * group + own
        select = jnp.logical_and(column == wanted, own < group).astype(BF16)
        rows_ref[...] = dot_nt(select, home_ref[...]).astype(BF16)

    result = dot_nn(rows_ref[...], force_ref[...])
    for c in range(here):
        row = (step * here + c) * pitch
        piece = result[:, c * modes : (c + 1) * modes]
        main_ref[0, pl.ds(row, lines), :] = piece[:, :TILE]
        main_ref[1, pl.ds(row, lines), :] = piece[:, TILE:MAIN]
        rest_ref[pl.ds(row, lines), :] = jnp.concatenate(
            [piece[:, MAIN:], jnp.zeros((lines, TILE - rest), F32)], axis=1
        )

    @pl.when(step == pl.num_programs(0) - 1)
    def _():
        lane = lax.broadcasted_iota(jnp.int32, (depth, TILE), 1)
        for (first, count), out_ref in zip(chunks, outs):
            for t in range(groups):
                base = t * share + first
                for r in range(count):
                    for h in range(2):
                        out_ref[t, r, :, h * TILE : (h + 1) * TILE] = main_ref[
                            h, pl.ds(base + r, depth, stride=pitch), :
                        ].astype(BF16)
                for g in range(ceil_div(count, per_slot)):
                    for h in range(2):
                        packed = jnp.zeros((depth, TILE), F32)
                        for b in range(per_slot // 2):
                            r = g * per_slot + h * (per_slot // 2) + b
                            if r < count:
                                piece = rest_ref[pl.ds(base + r, depth, stride=pitch), :]
                                if b > 0:
                                    piece = pltpu.roll(piece, b * rest, 1)
                                packed = jnp.where(lane // rest == b, piece, packed)
                        out_ref[t, count + g, :, h * TILE : (h + 1) * TILE] = packed.astype(BF16)


def project(here, home_vectors, force_table, groups, n_qp, group, share, chunks):
    modes = home_vectors.shape[0]
    lines = groups * share
    depth = force_table.shape[1] // modes
    per_step = 8 if depth % 8 == 0 else 4
    steps = depth // per_step
    shapes = [(groups, slots_of(count, modes), depth, MAIN) for _, count in chunks]
    return pl.pallas_call(
        functools.partial(project_kernel, groups, n_qp, group, chunks),
        grid=(steps,),
        in_specs=[
            pl.BlockSpec(memory_space=pltpu.SMEM),
            pl.BlockSpec((modes, modes), lambda i: (0, 0)),
            pl.BlockSpec((modes, per_step * modes), lambda i: (0, i)),
        ],
        out_specs=[pl.BlockSpec(shape, lambda i: (0, 0, 0, 0)) for shape in shapes],
        out_shape=[jax.ShapeDtypeStruct(shape, BF16) for shape in shapes],
        scratch_shapes=[
            pltpu.VMEM((lines, modes), BF16),
            pltpu.VMEM((2, (depth + 1) * (lines + 1), TILE), F32),
            pltpu.VMEM(((depth + 1) * (lines + 1), TILE), F32),
        ],
        compiler_params=pltpu.CompilerParams(vmem_limit_bytes=VMEM_BYTES),
        name="project",
    )(here, home_vectors, force_table)


def identity(size):
    return (
        lax.broadcasted_iota(jnp.int32, (size, size), 0)
        == lax.broadcasted_iota(jnp.int32, (size, size), 1)
    ).astype(BF16)


def pack_kernel(part_ref, partner_ref, weight_ref, grid_ref, freq_ref, out_ref):
    own_pairs, modes, _ = grid_ref.shape
    rest = modes - MAIN
    lines = rest // 2
    part = part_ref[0]
    line = lax.broadcasted_iota(jnp.int32, (lines, modes), 0)
    column = lax.broadcasted_iota(jnp.int32, (lines, modes), 1)
    select = (column == MAIN + part * lines + line).astype(BF16)
    freqs = freq_ref[...].astype(F32)
    blank = jnp.zeros((own_pairs, TILE - rest), F32)
    freq_tiles = (
        freqs[:, :TILE],
        freqs[:, TILE:MAIN],
        jnp.concatenate([freqs[:, MAIN:], blank], axis=1),
    )
    line16 = lax.broadcasted_iota(jnp.int32, (16, TILE), 0)
    lane16 = lax.broadcasted_iota(jnp.int32, (16, TILE), 1)
    for s in range(own_pairs):
        for p in range(2):

            @pl.when(part == p)
            def _():
                out_ref[s, :modes, :] = grid_ref[s, :, p * TILE : (p + 1) * TILE]

        turned = dot_nt(select, grid_ref[s])
        turned = (
            turned[:, :TILE],
            turned[:, TILE:MAIN],
            jnp.concatenate([turned[:, MAIN:], jnp.zeros((lines, TILE - rest), F32)], axis=1),
        )
        for h in range(3):
            start = modes + h * lines
            out_ref[s, start : start + lines, :] = turned[h].astype(BF16)
        pair = partner_ref[s].astype(F32)
        weight = weight_ref[s].astype(F32)
        side = jnp.where(lane16 == 0, pair, jnp.where(lane16 == 1, weight, 0.0))
        side = jnp.where(line16 == 3, side, 0.0)
        for h in range(3):
            side = jnp.where(line16 == h, freq_tiles[h][s : s + 1], side)
        start = modes + 3 * lines
        out_ref[s, start : start + 16, :] = side.astype(BF16)


def pack_own(part, partner, weights, grid_vectors, partner_frequencies):
    own_pairs, modes, _ = grid_vectors.shape
    smem = pl.BlockSpec(memory_space=pltpu.SMEM)
    vmem = pl.BlockSpec(memory_space=pltpu.VMEM)
    rows = modes + 3 * (modes - MAIN) // 2 + 16
    return pl.pallas_call(
        pack_kernel,
        in_specs=[smem, smem, smem, vmem, vmem],
        out_specs=vmem,
        out_shape=jax.ShapeDtypeStruct((own_pairs, rows, TILE), BF16),
        compiler_params=pltpu.CompilerParams(vmem_limit_bytes=VMEM_BYTES),
        name="pack_own",
    )(part, partner, weights, grid_vectors, partner_frequencies)


def arrange_kernel(
    pack_ref, partner_ref, weight_ref, grid_ref, grid_t_ref, freq_row_ref, freq_col_ref
):
    owners, parts, each, rows, _ = pack_ref.shape
    modes = grid_ref.shape[1]
    rest = modes - MAIN
    lines = rest // parts
    eye = identity(MAIN)
    source = lax.broadcasted_iota(jnp.int32, (TILE, TILE), 0)
    place = lax.broadcasted_iota(jnp.int32, (TILE, TILE), 1)
    spread = (source == place % rest).astype(BF16)
    eye_tile = (source == place).astype(BF16)
    lane = lax.broadcasted_iota(jnp.int32, (TILE, freq_col_ref.shape[1]), 1)
    line16 = lax.broadcasted_iota(jnp.int32, (16, TILE), 0)
    lane16 = lax.broadcasted_iota(jnp.int32, (16, TILE), 1)
    freq_col_ref[...] = jnp.zeros_like(freq_col_ref)

    def one(q, carry):
        for s in range(each):
            x = q * each + s
            for part in range(parts):
                grid_ref[x, :, part * TILE : (part + 1) * TILE] = pack_ref[q, part, s, :modes, :]
                for h in range(3):
                    start, width = modes + h * lines, min(TILE, modes - h * TILE)
                    piece = pack_ref[q, part, s, start : start + lines, :]
                    grid_t_ref[
                        x, MAIN + part * lines : MAIN + (part + 1) * lines, h * TILE : h * TILE + width
                    ] = piece[:, :width]
            grid_t_ref[x, :MAIN, :] = dot_nt(eye, grid_ref[x]).astype(BF16)
            side = pack_ref[q, 0, s, modes + 3 * lines : modes + 3 * lines + 16, :]
            wide = side.astype(F32)
            freq_row_ref[x, :, :TILE] = wide[0:1]
            freq_row_ref[x, :, TILE:MAIN] = wide[1:2]
            freq_row_ref[x, :, MAIN:] = dot_nn(side, spread)[2:3]
            columns = dot_nt(eye_tile, side)
            for h in range(3):
                width = min(TILE, modes - h * TILE)
                here = slice(h * TILE, h * TILE + width)
                freq_col_ref[here, :] = jnp.where(
                    lane[:width] == x, columns[:width, h : h + 1], freq_col_ref[here, :]
                )
            for spot, ref in ((0, partner_ref), (1, weight_ref)):
                found = jnp.sum(
                    jnp.where(jnp.logical_and(line16 == 3, lane16 == spot), wide, 0.0)
                )
                ref[x] = found.astype(ref.dtype)
        return carry

    lax.fori_loop(0, owners, one, 0)


def arrange(pack, modes):
    owners, parts, each, _, _ = pack.shape
    pairs = owners * each
    smem = pl.BlockSpec(memory_space=pltpu.SMEM)
    vmem = pl.BlockSpec(memory_space=pltpu.VMEM)
    return pl.pallas_call(
        arrange_kernel,
        in_specs=[vmem],
        out_specs=[smem, smem, vmem, vmem, vmem, vmem],
        out_shape=[
            jax.ShapeDtypeStruct((pairs,), jnp.int32),
            jax.ShapeDtypeStruct((pairs,), F32),
            jax.ShapeDtypeStruct((pairs, modes, MAIN), BF16),
            jax.ShapeDtypeStruct((pairs, modes, modes), BF16),
            jax.ShapeDtypeStruct((pairs, 1, MAIN + TILE), F32),
            jax.ShapeDtypeStruct((modes, TILE), F32),
        ],
        compiler_params=pltpu.CompilerParams(vmem_limit_bytes=VMEM_BYTES),
        name="arrange",
    )(pack)


def interleave(heavy, light):
    done = 0
    for i, task in enumerate(heavy):
        task()
        upto = (i + 1) * len(light) // len(heavy)
        while done < upto:
            light[done]()
            done += 1
    while done < len(light):
        light[done]()
        done += 1


def coupling_kernel(
    share,
    block,
    partner_ref,
    weight_ref,
    home_ref,
    grid_ref,
    grid_t_ref,
    freq_row_ref,
    freq_col_ref,
    home_row_ref,
    moved_ref,
    out_ref,
    turned_ref,
    grid_rest_ref,
    inner_rest_ref,
    pick_ref,
    rest_value_ref,
    *work,
):
    gathers, inners, values, tabs, sums, rest_sums, firsts = (
        work[2 * i : 2 * i + 2] for i in range(7)
    )
    pairs = grid_ref.shape[0]
    modes = grid_ref.shape[1]
    rest = modes - MAIN
    sources, depth = moved_ref.shape[0], moved_ref.shape[2]
    per_slot = MAIN // rest
    rest_lanes = home_row_ref.shape[1]
    s2 = smearing * smearing
    steps = share // block

    for x in range(pairs):
        grid_rest_ref[x * rest : (x + 1) * rest, :] = grid_t_ref[x, MAIN:, :]
    eye = identity(modes)
    if share * rest < rest_lanes:
        inner_rest_ref[...] = jnp.zeros_like(inner_rest_ref)
    for r in range(share):
        slot, spot = share + r // per_slot, r % per_slot
        half, spot = spot // (per_slot // 2), spot % (per_slot // 2)
        gather_ref = gathers[r % 2]
        for s in range(sources):
            gather_ref[s * depth : (s + 1) * depth, :MAIN] = moved_ref[s, r].astype(F32)
            tail = moved_ref[s, slot, :, half * TILE : (half + 1) * TILE].astype(F32)
            if spot > 0:
                tail = pltpu.roll(tail, TILE - spot * rest, 1)
            gather_ref[s * depth : (s + 1) * depth, MAIN:] = tail[:, :rest]
        whole = gather_ref[...].astype(BF16)
        turned_ref[r * modes : (r + 1) * modes, :] = dot_nt(eye, whole).astype(BF16)
        found = dot_nn(grid_rest_ref[...], whole).astype(BF16)
        for x in range(pairs):
            inner_rest_ref[x, r * rest : (r + 1) * rest, :] = found[x * rest : (x + 1) * rest, :]

    row_id = lax.broadcasted_iota(jnp.int32, pick_ref.shape, 0)
    col_id = lax.broadcasted_iota(jnp.int32, pick_ref.shape, 1)
    pick_ref[...] = (row_id // rest == col_id).astype(BF16)
    for ref in (out_ref, *sums, *rest_sums, *firsts):
        ref[...] = jnp.zeros_like(ref)

    def contract_first(x, r, b, into):
        def task():
            found = dot_nn(turned_ref[r * modes : (r + 1) * modes, :], grid_ref[x])
            into[:, b * MAIN : (b + 1) * MAIN] = found.astype(BF16)

        return task

    def contract_second(x, b, source, into):
        lanes = slice(b * MAIN, (b + 1) * MAIN)

        def task():
            into[:, lanes] = dot_nn(grid_t_ref[partner_ref[x]], source[:, lanes])

        return task

    def line_shapes(v, t, w, c1, c2):
        p = v * v
        d = t[0] - w
        e = t[1] - c1
        return (
            (p * t[2]) * pl.reciprocal(d * d + s2, approx=True),
            (p * t[3]) * pl.reciprocal(e * e + c2, approx=True),
        )

    def weigh(step, source, tab, sum_ref, first_ref):
        state = {}

        def begin():
            state["w"] = [home_ref[step * block + b] for b in range(block)]
            state["c1"] = [w * w - s2 for w in state["w"]]
            state["c2"] = [(4.0 * s2) * (w * w) for w in state["w"]]
            state["total"] = [jnp.zeros((8, MAIN), F32) for _ in range(block)]

        def rows(n):
            def task():
                if n == 0:
                    begin()
                t = [tab[k, n : n + 16, :MAIN] for k in range(4)]
                for b in range(block):
                    v = source[n : n + 16, b * MAIN : (b + 1) * MAIN]
                    f, u = line_shapes(v, t, state["w"][b], state["c1"][b], state["c2"][b])
                    state["total"][b] = state["total"][b] + (f[:8] + f[8:])
                    r = step * block + b
                    sum_ref[n : n + 16, r : r + 1] = jnp.sum(
                        u[:, :TILE] + u[:, TILE:], axis=1, keepdims=True
                    )
                if n + 16 == modes:
                    for b in range(block):
                        r = step * block + b
                        line = jnp.sum(state["total"][b], axis=0, keepdims=True)
                        first_ref[r : r + 1, :MAIN] = line * (1.0 / state["w"][b])

            return task

        return [rows(n) for n in range(0, modes, 16)]

    def contract_rest(x):
        def task():
            rest_value_ref[...] = dot_nt(grid_t_ref[partner_ref[x]], inner_rest_ref[x])

        return task

    def weigh_rest(tab, sum_ref, first_ref):
        def tile(start):
            lanes = slice(start, start + TILE)
            state = {}

            def rows(n):
                def task():
                    if n == 0:
                        state["total"] = jnp.zeros((8, TILE), F32)
                        state["w"] = home_row_ref[0:1, lanes]
                        state["c1"] = home_row_ref[1:2, lanes]
                        state["c2"] = home_row_ref[2:3, lanes]
                    for k in range(n, n + 48, 16):
                        t = [tab[i, k : k + 16, MAIN:] for i in range(4)]
                        f, u = line_shapes(
                            rest_value_ref[k : k + 16, lanes], t, state["w"], state["c1"], state["c2"]
                        )
                        state["total"] = state["total"] + (f[:8] + f[8:])
                        sum_ref[k : k + 16, lanes] = u.astype(BF16)
                    if n + 48 == modes:
                        line = jnp.sum(state["total"], axis=0, keepdims=True)
                        line = line * home_row_ref[3:4, lanes]
                        for b in range(TILE // rest):
                            r = start // rest + b
                            if r < share:
                                first_ref[r : r + 1, MAIN:] = line[:, b * rest : (b + 1) * rest]

                return task

            return [rows(n) for n in range(0, modes, 48)]

        return [task for start in range(0, rest_lanes, TILE) for task in tile(start)]

    def tables(x, tab):
        state = {}

        def begin():
            w1 = freq_row_ref[x]
            spots = lax.broadcasted_iota(jnp.int32, freq_col_ref.shape, 1)
            w2 = jnp.sum(
                jnp.where(spots == partner_ref[x], freq_col_ref[...], 0.0), axis=1, keepdims=True
            )
            state["w"] = (w1, w2)
            state["o"] = (occupy(w1), occupy(w2))
            scale = weight_ref[x] * (smearing / math.pi / modes)
            state["i"] = (scale / w1, 1.0 / w2)

        def rows(n):
            def task():
                if n == 0:
                    begin()
                part = slice(n, n + 48)
                (w1, w2), (o1, o2), (i1, i2) = state["w"], state["o"], state["i"]
                w2, o2, i2 = w2[part], o2[part], i2[part]
                a = w1 - w2
                both = i1 * i2
                tab[0, part, :] = w1 + w2
                tab[1, part, :] = a * a
                tab[2, part, :] = (1.0 + o1 + o2) * both
                tab[3, part, :] = (4.0 * a) * (o2 - o1) * both

            return task

        return [rows(n) for n in range(0, modes, 48)]

    def collect(sum_ref, rest_sum_ref, state):
        def task():
            second = sum_ref[...] + dot_nn(rest_sum_ref[...], pick_ref[...])
            state["second"] = second.T[:share, :]

        return task

    def deliver(x, target, state, first_ref):
        out_ref[x, :share, :] += first_ref[:share, :]
        out_ref[target, :share, :] += state["second"]

    for task in tables(0, tabs[0]):
        task()
    for g in range(2):
        for b in range(block):
            x, step = jnp.int32(g // steps), g % steps
            contract_first(x, step * block + b, b, inners[g])()
    for b in range(block):
        contract_second(jnp.int32(0), b, inners[0], values[0])()

    def two_pairs(i, carry):
        for e in range(2):
            x = i * 2 + e

            def later(g):
                return jnp.minimum(i * 2 + g // steps, pairs - 1), g % steps

            before = jnp.maximum(x - 1, 0)
            target = partner_ref[before]
            extra = weigh_rest(tabs[e], rest_sums[e], firsts[e])
            extra = extra + tables(jnp.minimum(x + 1, pairs - 1), tabs[1 - e])
            contract_rest(x)()
            done = {}
            for s in range(steps):
                g = e * steps + s
                heavy = []
                for b in range(block):
                    x1, _ = later(g + 1)
                    heavy.append(contract_second(x1, b, inners[(g + 1) % 2], values[(g + 1) % 2]))
                for b in range(block):
                    x2, step2 = later(g + 2)
                    heavy.append(contract_first(x2, step2 * block + b, b, inners[g % 2]))
                light = weigh(s, values[g % 2], tabs[e], sums[e], firsts[e])
                light = light + extra[s * len(extra) // steps : (s + 1) * len(extra) // steps]
                if s == 0:
                    heavy.insert(1, collect(sums[1 - e], rest_sums[1 - e], done))
                interleave(heavy, light)
            deliver(before, target, done, firsts[1 - e])
        return carry

    lax.fori_loop(0, pairs // 2, two_pairs, 0)
    last = {}
    collect(sums[1], rest_sums[1], last)()
    deliver(pairs - 1, partner_ref[pairs - 1], last, firsts[1])

    totals = jnp.zeros(out_ref.shape[1:], F32)
    for y in range(pairs):
        totals = totals + out_ref[y]
    widths = jnp.sum(totals, axis=1, keepdims=True) * (1.0 / (pairs * modes))
    spread = jnp.where(
        lax.broadcasted_iota(jnp.int32, totals.shape, 0)
        == lax.broadcasted_iota(jnp.int32, totals.shape, 1),
        widths,
        0.0,
    )
    out_ref[:, share, :] = jnp.broadcast_to(
        jnp.sum(spread, axis=0, keepdims=True), (pairs, modes)
    )


def coupling(partner, weights, home, grid, grid_t, freq_rows, freq_cols, moved):
    pairs, modes = grid.shape[0], grid.shape[1]
    share = home.shape[0]
    rest = modes - MAIN
    rest_lanes = ceil_div(share * rest, TILE) * TILE
    row = jnp.repeat(home, rest)
    row = jnp.pad(row, (0, rest_lanes - share * rest), constant_values=1.0)
    s2 = smearing * smearing
    home_row = jnp.stack([row, row * row - s2, (4.0 * s2) * (row * row), 1.0 / row])
    padded = (share // 8 + 1) * 8
    smem = pl.BlockSpec(memory_space=pltpu.SMEM)
    vmem = pl.BlockSpec(memory_space=pltpu.VMEM)
    block = 3 if share % 3 == 0 else 1
    assert pairs % 2 == 0
    scratch = (
        [
            pltpu.VMEM((share * modes, modes), BF16),
            pltpu.VMEM((pairs * rest, modes), BF16),
            pltpu.VMEM((pairs, rest_lanes, modes), BF16),
            pltpu.VMEM((rest_lanes, TILE), BF16),
            pltpu.VMEM((modes, rest_lanes), F32),
        ]
        + [pltpu.VMEM((modes, modes), F32)] * 2
        + [pltpu.VMEM((modes, block * MAIN), BF16)] * 2
        + [pltpu.VMEM((modes, block * MAIN), F32)] * 2
        + [pltpu.VMEM((4, modes, MAIN + TILE), F32)] * 2
        + [pltpu.VMEM((modes, TILE), F32)] * 2
        + [pltpu.VMEM((modes, rest_lanes), BF16)] * 2
        + [pltpu.VMEM((padded, modes), F32)] * 2
    )
    return pl.pallas_call(
        functools.partial(coupling_kernel, share, block),
        in_specs=[smem, smem, smem, vmem, vmem, vmem, vmem, vmem, vmem],
        out_specs=vmem,
        out_shape=jax.ShapeDtypeStruct((pairs, padded, modes), F32),
        scratch_shapes=scratch,
        compiler_params=pltpu.CompilerParams(vmem_limit_bytes=VMEM_BYTES),
        cost_estimate=pl.CostEstimate(
            flops=4 * share * pairs * modes**3,
            bytes_accessed=8 * share * modes * modes,
            transcendentals=2 * share * pairs * modes**2,
        ),
        name="coupling",
    )(partner, weights, home, grid, grid_t, freq_rows, freq_cols, home_row, moved)


def local(
    home_vectors, home_freqs, grid_vectors, partner_frequencies, force_table, partner, weights
):
    own_pairs = partner.shape[0]
    modes = home_vectors.shape[0]
    n_mode = lax.axis_size("mode")
    n_fc = lax.axis_size("fc")
    n_qp = lax.axis_size("qp")
    groups = n_mode * n_fc
    group = modes // groups
    pairs = own_pairs * n_qp
    share = ceil_div(group, n_qp)
    here = lax.axis_index("qp")
    if share % 6 == 0 and share > 6:
        chunks = ((0, 6), (6, share - 6))
    else:
        chunks = ((0, share),)

    assert n_fc * TILE == MAIN
    own_part = lax.axis_index("fc").astype(jnp.int32)[None]
    pack = pack_own(own_part, partner, weights, grid_vectors, partner_frequencies)
    pack = lax.all_gather(pack, ("qp", "fc"), axis=0)
    pack = pack.reshape(n_qp, n_fc, own_pairs, pack.shape[2], TILE)

    sent = project(
        here.astype(jnp.int32)[None], home_vectors, force_table, groups, n_qp, group, share, chunks
    )
    moved = [
        lax.all_to_all(x, ("mode", "fc"), split_axis=0, concat_axis=0, tiled=True) for x in sent
    ]

    own = lax.axis_index(("mode", "fc"))
    home = home_freqs.astype(F32).reshape(groups, group)
    home = jnp.pad(home, ((0, 0), (0, share * n_qp - group)), constant_values=1.0)
    home = lax.dynamic_slice(home, (own, here * share), (1, share)).reshape(share)

    shared = arrange(pack, modes)
    parts, widths = [], []
    for (first, count), block in zip(chunks, moved):
        found = coupling(
            shared[0], shared[1], home[first : first + count], *shared[2:], block
        )
        back = lax.all_to_all(
            found.reshape(n_qp, own_pairs, found.shape[1], modes),
            "qp",
            split_axis=0,
            concat_axis=0,
            tiled=True,
        )
        widths.append(back[:, 0, count, :count])
        parts.append(back[:, :, :count, :])
    widths = jnp.concatenate(widths, axis=1).reshape(n_qp * share)[:group]
    collision = jnp.transpose(jnp.concatenate(parts, axis=2), (0, 2, 1, 3))
    collision = collision.reshape(n_qp * share, own_pairs, modes)[:group]
    return (widths, collision)


def solution(mesh):
    placed = (
        P("grp", None),
        P("grp"),
        P("qp", None, None),
        P("qp", None),
        P(None, ("mode", "fc")),
        P(("grp", "qp")),
        P(("grp", "qp")),
    )
    return jax.shard_map(
        local,
        mesh=mesh,
        in_specs=placed,
        out_specs=(P(("grp", "mode", "fc")), P(("mode", "fc"), ("grp", "qp"), None)),
        check_vma=False,
    )
```

```python
import functools
import math

import jax
import jax.numpy as jnp
from jax import lax
from jax.experimental import pallas as pl
from jax.experimental.pallas import tpu as pltpu
from jax.sharding import PartitionSpec as P

thermal_reservoir_kelvin = 1.0
smearing = 0.25

MAIN = 256
TILE = 128
F32 = jnp.float32
BF16 = jnp.bfloat16


def ceil_div(a, b):
    return -(-a // b)


VMEM_BYTES = 56 << 20


def occupy(energy):
    return 1.0 / (jnp.exp(energy / thermal_reservoir_kelvin) - 1.0)


def dot_nn(a, b):
    return lax.dot_general(a, b, (((1,), (0,)), ((), ())), preferred_element_type=F32)


def dot_nt(a, b):
    return lax.dot_general(a, b, (((1,), (1,)), ((), ())), preferred_element_type=F32)


def slots_of(count, modes):
    return count + ceil_div(count, MAIN // (modes - MAIN))


def project_kernel(groups, n_qp, group, chunks, here_ref, home_ref, force_ref, *refs):
    outs = refs[: len(chunks)]
    rows_ref, main_ref, rest_ref = refs[len(chunks) :]
    modes = home_ref.shape[0]
    lines = rows_ref.shape[0]
    share = lines // groups
    rest = modes - MAIN
    per_slot = MAIN // rest
    depth = outs[0].shape[2]
    step = pl.program_id(0)
    here = force_ref.shape[1] // modes
    pitch = lines + 1

    @pl.when(step == 0)
    def _():
        line = lax.broadcasted_iota(jnp.int32, (lines, modes), 0)
        column = lax.broadcasted_iota(jnp.int32, (lines, modes), 1)
        own = here_ref[0] * share + line % share
        wanted = (line // share) * group + own
        select = jnp.logical_and(column == wanted, own < group).astype(BF16)
        rows_ref[...] = dot_nt(select, home_ref[...]).astype(BF16)

    result = dot_nn(rows_ref[...], force_ref[...])
    for c in range(here):
        row = (step * here + c) * pitch
        piece = result[:, c * modes : (c + 1) * modes]
        main_ref[0, pl.ds(row, lines), :] = piece[:, :TILE]
        main_ref[1, pl.ds(row, lines), :] = piece[:, TILE:MAIN]
        rest_ref[pl.ds(row, lines), :] = jnp.concatenate(
            [piece[:, MAIN:], jnp.zeros((lines, TILE - rest), F32)], axis=1
        )

    @pl.when(step == pl.num_programs(0) - 1)
    def _():
        lane = lax.broadcasted_iota(jnp.int32, (depth, TILE), 1)
        for (first, count), out_ref in zip(chunks, outs):
            for t in range(groups):
                base = t * share + first
                for r in range(count):
                    for h in range(2):
                        out_ref[t, r, :, h * TILE : (h + 1) * TILE] = main_ref[
                            h, pl.ds(base + r, depth, stride=pitch), :
                        ].astype(BF16)
                for g in range(ceil_div(count, per_slot)):
                    for h in range(2):
                        packed = jnp.zeros((depth, TILE), F32)
                        for b in range(per_slot // 2):
                            r = g * per_slot + h * (per_slot // 2) + b
                            if r < count:
                                piece = rest_ref[pl.ds(base + r, depth, stride=pitch), :]
                                if b > 0:
                                    piece = pltpu.roll(piece, b * rest, 1)
                                packed = jnp.where(lane // rest == b, piece, packed)
                        out_ref[t, count + g, :, h * TILE : (h + 1) * TILE] = packed.astype(BF16)


def project(here, home_vectors, force_table, groups, n_qp, group, share, chunks):
    modes = home_vectors.shape[0]
    lines = groups * share
    depth = force_table.shape[1] // modes
    per_step = 8 if depth % 8 == 0 else 4
    steps = depth // per_step
    shapes = [(groups, slots_of(count, modes), depth, MAIN) for _, count in chunks]
    return pl.pallas_call(
        functools.partial(project_kernel, groups, n_qp, group, chunks),
        grid=(steps,),
        in_specs=[
            pl.BlockSpec(memory_space=pltpu.SMEM),
            pl.BlockSpec((modes, modes), lambda i: (0, 0)),
            pl.BlockSpec((modes, per_step * modes), lambda i: (0, i)),
        ],
        out_specs=[pl.BlockSpec(shape, lambda i: (0, 0, 0, 0)) for shape in shapes],
        out_shape=[jax.ShapeDtypeStruct(shape, BF16) for shape in shapes],
        scratch_shapes=[
            pltpu.VMEM((lines, modes), BF16),
            pltpu.VMEM((2, (depth + 1) * (lines + 1), TILE), F32),
            pltpu.VMEM(((depth + 1) * (lines + 1), TILE), F32),
        ],
        compiler_params=pltpu.CompilerParams(vmem_limit_bytes=VMEM_BYTES),
        name="project",
    )(here, home_vectors, force_table)


def identity(size):
    return (
        lax.broadcasted_iota(jnp.int32, (size, size), 0)
        == lax.broadcasted_iota(jnp.int32, (size, size), 1)
    ).astype(BF16)


def pack_kernel(part_ref, partner_ref, weight_ref, grid_ref, freq_ref, out_ref):
    own_pairs, modes, _ = grid_ref.shape
    rest = modes - MAIN
    lines = rest // 2
    part = part_ref[0]
    line = lax.broadcasted_iota(jnp.int32, (lines, modes), 0)
    column = lax.broadcasted_iota(jnp.int32, (lines, modes), 1)
    select = (column == MAIN + part * lines + line).astype(BF16)
    freqs = freq_ref[...].astype(F32)
    blank = jnp.zeros((own_pairs, TILE - rest), F32)
    freq_tiles = (
        freqs[:, :TILE],
        freqs[:, TILE:MAIN],
        jnp.concatenate([freqs[:, MAIN:], blank], axis=1),
    )
    line16 = lax.broadcasted_iota(jnp.int32, (16, TILE), 0)
    lane16 = lax.broadcasted_iota(jnp.int32, (16, TILE), 1)
    for s in range(own_pairs):
        for p in range(2):

            @pl.when(part == p)
            def _():
                out_ref[s, :modes, :] = grid_ref[s, :, p * TILE : (p + 1) * TILE]

        turned = dot_nt(select, grid_ref[s])
        turned = (
            turned[:, :TILE],
            turned[:, TILE:MAIN],
            jnp.concatenate([turned[:, MAIN:], jnp.zeros((lines, TILE - rest), F32)], axis=1),
        )
        for h in range(3):
            start = modes + h * lines
            out_ref[s, start : start + lines, :] = turned[h].astype(BF16)
        pair = partner_ref[s].astype(F32)
        weight = weight_ref[s].astype(F32)
        side = jnp.where(lane16 == 0, pair, jnp.where(lane16 == 1, weight, 0.0))
        side = jnp.where(line16 == 3, side, 0.0)
        for h in range(3):
            side = jnp.where(line16 == h, freq_tiles[h][s : s + 1], side)
        start = modes + 3 * lines
        out_ref[s, start : start + 16, :] = side.astype(BF16)


def pack_own(part, partner, weights, grid_vectors, partner_frequencies):
    own_pairs, modes, _ = grid_vectors.shape
    smem = pl.BlockSpec(memory_space=pltpu.SMEM)
    vmem = pl.BlockSpec(memory_space=pltpu.VMEM)
    rows = modes + 3 * (modes - MAIN) // 2 + 16
    return pl.pallas_call(
        pack_kernel,
        in_specs=[smem, smem, smem, vmem, vmem],
        out_specs=vmem,
        out_shape=jax.ShapeDtypeStruct((own_pairs, rows, TILE), BF16),
        compiler_params=pltpu.CompilerParams(vmem_limit_bytes=VMEM_BYTES),
        name="pack_own",
    )(part, partner, weights, grid_vectors, partner_frequencies)


def arrange_kernel(
    pack_ref, partner_ref, weight_ref, grid_ref, grid_t_ref, freq_row_ref, freq_col_ref
):
    owners, parts, each, rows, _ = pack_ref.shape
    modes = grid_ref.shape[1]
    rest = modes - MAIN
    lines = rest // parts
    eye = identity(MAIN)
    source = lax.broadcasted_iota(jnp.int32, (TILE, TILE), 0)
    place = lax.broadcasted_iota(jnp.int32, (TILE, TILE), 1)
    spread = (source == place % rest).astype(BF16)
    eye_tile = (source == place).astype(BF16)
    lane = lax.broadcasted_iota(jnp.int32, (TILE, freq_col_ref.shape[1]), 1)
    line16 = lax.broadcasted_iota(jnp.int32, (16, TILE), 0)
    lane16 = lax.broadcasted_iota(jnp.int32, (16, TILE), 1)
    freq_col_ref[...] = jnp.zeros_like(freq_col_ref)

    def one(q, carry):
        for s in range(each):
            x = q * each + s
            for part in range(parts):
                grid_ref[x, :, part * TILE : (part + 1) * TILE] = pack_ref[q, part, s, :modes, :]
                for h in range(3):
                    start = modes + h * lines
                    grid_t_ref[
                        x,
                        MAIN + part * lines : MAIN + (part + 1) * lines,
                        h * TILE : (h + 1) * TILE,
                    ] = pack_ref[q, part, s, start : start + lines, :]
            grid_t_ref[x, :MAIN, MAIN:] = jnp.zeros((MAIN, TILE), BF16)
            grid_t_ref[x, :MAIN, :modes] = dot_nt(eye, grid_ref[x]).astype(BF16)
            side = pack_ref[q, 0, s, modes + 3 * lines : modes + 3 * lines + 16, :]
            wide = side.astype(F32)
            freq_row_ref[x, :, :TILE] = wide[0:1]
            freq_row_ref[x, :, TILE:MAIN] = wide[1:2]
            freq_row_ref[x, :, MAIN:] = dot_nn(side, spread)[2:3]
            columns = dot_nt(eye_tile, side)
            for h in range(3):
                width = min(TILE, modes - h * TILE)
                here = slice(h * TILE, h * TILE + width)
                freq_col_ref[here, :] = jnp.where(
                    lane[:width] == x, columns[:width, h : h + 1], freq_col_ref[here, :]
                )
            for spot, ref in ((0, partner_ref), (1, weight_ref)):
                found = jnp.sum(
                    jnp.where(jnp.logical_and(line16 == 3, lane16 == spot), wide, 0.0)
                )
                ref[x] = found.astype(ref.dtype)
        return carry

    lax.fori_loop(0, owners, one, 0)


def arrange(pack, modes):
    owners, parts, each, _, _ = pack.shape
    pairs = owners * each
    smem = pl.BlockSpec(memory_space=pltpu.SMEM)
    vmem = pl.BlockSpec(memory_space=pltpu.VMEM)
    return pl.pallas_call(
        arrange_kernel,
        in_specs=[vmem],
        out_specs=[smem, smem, vmem, vmem, vmem, vmem],
        out_shape=[
            jax.ShapeDtypeStruct((pairs,), jnp.int32),
            jax.ShapeDtypeStruct((pairs,), F32),
            jax.ShapeDtypeStruct((pairs, modes, MAIN), BF16),
            jax.ShapeDtypeStruct((pairs, modes, MAIN + TILE), BF16),
            jax.ShapeDtypeStruct((pairs, 1, MAIN + TILE), F32),
            jax.ShapeDtypeStruct((modes, TILE), F32),
        ],
        compiler_params=pltpu.CompilerParams(vmem_limit_bytes=VMEM_BYTES),
        name="arrange",
    )(pack)


def interleave(heavy, light):
    done = 0
    for i, task in enumerate(heavy):
        task()
        upto = (i + 1) * len(light) // len(heavy)
        while done < upto:
            light[done]()
            done += 1
    while done < len(light):
        light[done]()
        done += 1


def coupling_kernel(
    share,
    block,
    partner_ref,
    weight_ref,
    home_ref,
    grid_ref,
    grid_t_ref,
    freq_row_ref,
    freq_col_ref,
    home_row_ref,
    moved_ref,
    out_ref,
    turned_ref,
    grid_rest_ref,
    inner_rest_ref,
    pick_ref,
    rest_value_ref,
    force_rest_ref,
    *work,
):
    gathers, inners, lefts, wides, values, tabs, sums, rest_sums, firsts = (
        work[2 * i : 2 * i + 2] for i in range(9)
    )
    pairs = grid_ref.shape[0]
    modes = grid_ref.shape[1]
    rest = modes - MAIN
    sources, depth = moved_ref.shape[0], moved_ref.shape[2]
    per_slot = MAIN // rest
    per_tile = TILE // rest
    rest_lanes = home_row_ref.shape[1]
    s2 = smearing * smearing
    steps = share // block

    for x in range(pairs):
        grid_rest_ref[x * rest : (x + 1) * rest, :] = grid_t_ref[x, MAIN:, :modes]
    eye = identity(modes)
    force_rest_ref[...] = jnp.zeros_like(force_rest_ref)
    if share * rest < rest_lanes:
        inner_rest_ref[...] = jnp.zeros_like(inner_rest_ref)
    for r in range(share):
        slot, spot = share + r // per_slot, r % per_slot
        half, spot = spot // (per_slot // 2), spot % (per_slot // 2)
        gather_ref = gathers[r % 2]
        for s in range(sources):
            gather_ref[s * depth : (s + 1) * depth, :MAIN] = moved_ref[s, r].astype(F32)
            tail = moved_ref[s, slot, :, half * TILE : (half + 1) * TILE].astype(F32)
            if spot > 0:
                tail = pltpu.roll(tail, TILE - spot * rest, 1)
            gather_ref[s * depth : (s + 1) * depth, MAIN:] = tail[:, :rest]
        whole = gather_ref[...].astype(BF16)
        turned_ref[r * modes : (r + 1) * modes, :] = dot_nt(eye, whole[:MAIN]).astype(BF16)
        line = (r // block * per_tile + r % block) * rest
        force_rest_ref[line : line + rest, :] = whole[MAIN:]
        found = dot_nn(grid_rest_ref[...], whole).astype(BF16)
        for x in range(pairs):
            inner_rest_ref[x, r * rest : (r + 1) * rest, :] = found[x * rest : (x + 1) * rest, :]

    row_id = lax.broadcasted_iota(jnp.int32, pick_ref.shape, 0)
    col_id = lax.broadcasted_iota(jnp.int32, pick_ref.shape, 1)
    pick_ref[...] = (row_id // rest == col_id).astype(BF16)
    for ref in (out_ref, *inners, *sums, *rest_sums, *firsts):
        ref[...] = jnp.zeros_like(ref)

    def contract_wide(x, into):
        def task():
            left = grid_t_ref[partner_ref[x], :, :modes]
            into[...] = dot_nt(left, force_rest_ref[...]).astype(BF16)

        return task

    def contract_first(x, r, b, into):
        def task():
            lanes = slice(b * MAIN, (b + 1) * MAIN)
            found = dot_nn(turned_ref[r * modes : (r + 1) * modes, :], grid_ref[x, :MAIN, :])
            into[:modes, lanes] = found.astype(BF16)
            start = MAIN + TILE + b * rest
            into[start : start + rest, lanes] = grid_ref[x, MAIN:, :]

        return task

    def prepare_second(x, step, wide, left):
        def task():
            left[:, : MAIN + TILE] = grid_t_ref[partner_ref[x]]
            left[:, MAIN + TILE :] = wide[:, step * TILE : (step + 1) * TILE]

        return task

    def contract_second(b, left, source, into):
        lanes = slice(b * MAIN, (b + 1) * MAIN)

        def task():
            into[:, lanes] = dot_nn(left[...], source[:, lanes])

        return task

    def line_shapes(v, t, w, c1, c2):
        p = v * v
        d = t[0] - w
        e = t[1] - c1
        return (
            (p * t[2]) * pl.reciprocal(d * d + s2, approx=True),
            (p * t[3]) * pl.reciprocal(e * e + c2, approx=True),
        )

    def weigh(step, source, tab, sum_ref, first_ref):
        state = {}

        def begin():
            state["w"] = [home_ref[step * block + b] for b in range(block)]
            state["c1"] = [w * w - s2 for w in state["w"]]
            state["c2"] = [(4.0 * s2) * (w * w) for w in state["w"]]
            state["total"] = [jnp.zeros((8, MAIN), F32) for _ in range(block)]

        def rows(n):
            def task():
                if n == 0:
                    begin()
                t = [tab[k, n : n + 16, :MAIN] for k in range(4)]
                for b in range(block):
                    v = source[n : n + 16, b * MAIN : (b + 1) * MAIN]
                    f, u = line_shapes(v, t, state["w"][b], state["c1"][b], state["c2"][b])
                    state["total"][b] = state["total"][b] + (f[:8] + f[8:])
                    r = step * block + b
                    sum_ref[n : n + 16, r : r + 1] = jnp.sum(
                        u[:, :TILE] + u[:, TILE:], axis=1, keepdims=True
                    )
                if n + 16 == modes:
                    for b in range(block):
                        r = step * block + b
                        line = jnp.sum(state["total"][b], axis=0, keepdims=True)
                        first_ref[r : r + 1, :MAIN] = line * (1.0 / state["w"][b])

            return task

        return [rows(n) for n in range(0, modes, 16)]

    def contract_rest(x):
        def task():
            rest_value_ref[...] = dot_nt(
                grid_t_ref[partner_ref[x], :, :modes], inner_rest_ref[x]
            )

        return task

    def weigh_rest(tab, sum_ref, first_ref):
        def tile(start):
            lanes = slice(start, start + TILE)
            state = {}

            def rows(n):
                def task():
                    if n == 0:
                        state["total"] = jnp.zeros((8, TILE), F32)
                        state["w"] = home_row_ref[0:1, lanes]
                        state["c1"] = home_row_ref[1:2, lanes]
                        state["c2"] = home_row_ref[2:3, lanes]
                    for k in range(n, n + 48, 16):
                        t = [tab[i, k : k + 16, MAIN:] for i in range(4)]
                        f, u = line_shapes(
                            rest_value_ref[k : k + 16, lanes], t, state["w"], state["c1"], state["c2"]
                        )
                        state["total"] = state["total"] + (f[:8] + f[8:])
                        sum_ref[k : k + 16, lanes] = u.astype(BF16)
                    if n + 48 == modes:
                        line = jnp.sum(state["total"], axis=0, keepdims=True)
                        line = line * home_row_ref[3:4, lanes]
                        for b in range(TILE // rest):
                            r = start // rest + b
                            if r < share:
                                first_ref[r : r + 1, MAIN:] = line[:, b * rest : (b + 1) * rest]

                return task

            return [rows(n) for n in range(0, modes, 48)]

        return [task for start in range(0, rest_lanes, TILE) for task in tile(start)]

    def tables(x, tab):
        state = {}

        def begin():
            w1 = freq_row_ref[x]
            spots = lax.broadcasted_iota(jnp.int32, freq_col_ref.shape, 1)
            w2 = jnp.sum(
                jnp.where(spots == partner_ref[x], freq_col_ref[...], 0.0), axis=1, keepdims=True
            )
            state["w"] = (w1, w2)
            state["o"] = (occupy(w1), occupy(w2))
            scale = weight_ref[x] * (smearing / math.pi / modes)
            state["i"] = (scale / w1, 1.0 / w2)

        def rows(n):
            def task():
                if n == 0:
                    begin()
                part = slice(n, n + 48)
                (w1, w2), (o1, o2), (i1, i2) = state["w"], state["o"], state["i"]
                w2, o2, i2 = w2[part], o2[part], i2[part]
                a = w1 - w2
                both = i1 * i2
                tab[0, part, :] = w1 + w2
                tab[1, part, :] = a * a
                tab[2, part, :] = (1.0 + o1 + o2) * both
                tab[3, part, :] = (4.0 * a) * (o2 - o1) * both

            return task

        return [rows(n) for n in range(0, modes, 48)]

    def collect(sum_ref, rest_sum_ref, state):
        def task():
            second = sum_ref[...] + dot_nn(rest_sum_ref[...], pick_ref[...])
            state["second"] = second.T[:share, :]

        return task

    def deliver(x, target, state, first_ref):
        out_ref[x, :share, :] += first_ref[:share, :]
        out_ref[target, :share, :] += state["second"]

    for task in tables(0, tabs[0]):
        task()
    for g in range(2):
        for b in range(block):
            x, step = jnp.int32(g // steps), g % steps
            contract_first(x, step * block + b, b, inners[g])()
    contract_wide(jnp.int32(0), wides[0])()
    prepare_second(jnp.int32(0), 0, wides[0], lefts[0])()
    for b in range(block):
        contract_second(b, lefts[0], inners[0], values[0])()

    def two_pairs(i, carry):
        for e in range(2):
            x = i * 2 + e

            def later(g):
                return jnp.minimum(i * 2 + g // steps, pairs - 1), g % steps

            before = jnp.maximum(x - 1, 0)
            target = partner_ref[before]
            extra = weigh_rest(tabs[e], rest_sums[e], firsts[e])
            extra = extra + tables(jnp.minimum(x + 1, pairs - 1), tabs[1 - e])
            contract_rest(x)()
            done = {}
            for s in range(steps):
                g = e * steps + s
                heavy = []
                if s == 0:
                    contract_wide(jnp.minimum(x + 1, pairs - 1), wides[1 - e])()
                x1, step1 = later(g + 1)
                odd = (g + 1) % 2
                prepare_second(x1, step1, wides[(g + 1) // steps % 2], lefts[odd])()
                for b in range(block):
                    heavy.append(contract_second(b, lefts[odd], inners[odd], values[odd]))
                for b in range(block):
                    x2, step2 = later(g + 2)
                    heavy.append(contract_first(x2, step2 * block + b, b, inners[g % 2]))
                light = weigh(s, values[g % 2], tabs[e], sums[e], firsts[e])
                light = light + extra[s * len(extra) // steps : (s + 1) * len(extra) // steps]
                if s == 0:
                    heavy.insert(1, collect(sums[1 - e], rest_sums[1 - e], done))
                interleave(heavy, light)
            deliver(before, target, done, firsts[1 - e])
        return carry

    lax.fori_loop(0, pairs // 2, two_pairs, 0)
    last = {}
    collect(sums[1], rest_sums[1], last)()
    deliver(pairs - 1, partner_ref[pairs - 1], last, firsts[1])

    totals = jnp.zeros(out_ref.shape[1:], F32)
    for y in range(pairs):
        totals = totals + out_ref[y]
    widths = jnp.sum(totals, axis=1, keepdims=True) * (1.0 / (pairs * modes))
    spread = jnp.where(
        lax.broadcasted_iota(jnp.int32, totals.shape, 0)
        == lax.broadcasted_iota(jnp.int32, totals.shape, 1),
        widths,
        0.0,
    )
    out_ref[:, share, :] = jnp.broadcast_to(
        jnp.sum(spread, axis=0, keepdims=True), (pairs, modes)
    )


def coupling(partner, weights, home, grid, grid_t, freq_rows, freq_cols, moved):
    pairs, modes = grid.shape[0], grid.shape[1]
    share = home.shape[0]
    rest = modes - MAIN
    rest_lanes = ceil_div(share * rest, TILE) * TILE
    row = jnp.repeat(home, rest)
    row = jnp.pad(row, (0, rest_lanes - share * rest), constant_values=1.0)
    s2 = smearing * smearing
    home_row = jnp.stack([row, row * row - s2, (4.0 * s2) * (row * row), 1.0 / row])
    padded = (share // 8 + 1) * 8
    smem = pl.BlockSpec(memory_space=pltpu.SMEM)
    vmem = pl.BlockSpec(memory_space=pltpu.VMEM)
    block = 3 if share % 3 == 0 else 1
    assert pairs % 2 == 0
    scratch = (
        [
            pltpu.VMEM((share * modes, MAIN), BF16),
            pltpu.VMEM((pairs * rest, modes), BF16),
            pltpu.VMEM((pairs, rest_lanes, modes), BF16),
            pltpu.VMEM((rest_lanes, TILE), BF16),
            pltpu.VMEM((modes, rest_lanes), F32),
            pltpu.VMEM((share // block * TILE, modes), BF16),
        ]
        + [pltpu.VMEM((modes, modes), F32)] * 2
        + [pltpu.VMEM((2 * MAIN, block * MAIN), BF16)] * 2
        + [pltpu.VMEM((modes, 2 * MAIN), BF16)] * 2
        + [pltpu.VMEM((modes, share // block * TILE), BF16)] * 2
        + [pltpu.VMEM((modes, block * MAIN), F32)] * 2
        + [pltpu.VMEM((4, modes, MAIN + TILE), F32)] * 2
        + [pltpu.VMEM((modes, TILE), F32)] * 2
        + [pltpu.VMEM((modes, rest_lanes), BF16)] * 2
        + [pltpu.VMEM((padded, modes), F32)] * 2
    )
    return pl.pallas_call(
        functools.partial(coupling_kernel, share, block),
        in_specs=[smem, smem, smem, vmem, vmem, vmem, vmem, vmem, vmem],
        out_specs=vmem,
        out_shape=jax.ShapeDtypeStruct((pairs, padded, modes), F32),
        scratch_shapes=scratch,
        compiler_params=pltpu.CompilerParams(vmem_limit_bytes=VMEM_BYTES),
        cost_estimate=pl.CostEstimate(
            flops=4 * share * pairs * modes**3,
            bytes_accessed=8 * share * modes * modes,
            transcendentals=2 * share * pairs * modes**2,
        ),
        name="coupling",
    )(partner, weights, home, grid, grid_t, freq_rows, freq_cols, home_row, moved)


def local(
    home_vectors, home_freqs, grid_vectors, partner_frequencies, force_table, partner, weights
):
    own_pairs = partner.shape[0]
    modes = home_vectors.shape[0]
    n_mode = lax.axis_size("mode")
    n_fc = lax.axis_size("fc")
    n_qp = lax.axis_size("qp")
    groups = n_mode * n_fc
    group = modes // groups
    pairs = own_pairs * n_qp
    share = ceil_div(group, n_qp)
    here = lax.axis_index("qp")
    if share % 6 == 0 and share > 6:
        chunks = ((0, 6), (6, share - 6))
    else:
        chunks = ((0, share),)

    assert n_fc * TILE == MAIN
    own_part = lax.axis_index("fc").astype(jnp.int32)[None]
    pack = pack_own(own_part, partner, weights, grid_vectors, partner_frequencies)
    pack = lax.all_gather(pack, ("qp", "fc"), axis=0)
    pack = pack.reshape(n_qp, n_fc, own_pairs, pack.shape[2], TILE)

    sent = project(
        here.astype(jnp.int32)[None], home_vectors, force_table, groups, n_qp, group, share, chunks
    )
    moved = [
        lax.all_to_all(x, ("mode", "fc"), split_axis=0, concat_axis=0, tiled=True) for x in sent
    ]

    own = lax.axis_index(("mode", "fc"))
    home = home_freqs.astype(F32).reshape(groups, group)
    home = jnp.pad(home, ((0, 0), (0, share * n_qp - group)), constant_values=1.0)
    home = lax.dynamic_slice(home, (own, here * share), (1, share)).reshape(share)

    shared = arrange(pack, modes)
    parts, widths = [], []
    for (first, count), block in zip(chunks, moved):
        found = coupling(
            shared[0], shared[1], home[first : first + count], *shared[2:], block
        )
        back = lax.all_to_all(
            found.reshape(n_qp, own_pairs, found.shape[1], modes),
            "qp",
            split_axis=0,
            concat_axis=0,
            tiled=True,
        )
        widths.append(back[:, 0, count, :count])
        parts.append(back[:, :, :count, :])
    widths = jnp.concatenate(widths, axis=1).reshape(n_qp * share)[:group]
    collision = jnp.transpose(jnp.concatenate(parts, axis=2), (0, 2, 1, 3))
    collision = collision.reshape(n_qp * share, own_pairs, modes)[:group]
    return (widths, collision)


def solution(mesh):
    placed = (
        P("grp", None),
        P("grp"),
        P("qp", None, None),
        P("qp", None),
        P(None, ("mode", "fc")),
        P(("grp", "qp")),
        P(("grp", "qp")),
    )
    return jax.shard_map(
        local,
        mesh=mesh,
        in_specs=placed,
        out_specs=(P(("grp", "mode", "fc")), P(("mode", "fc"), ("grp", "qp"), None)),
        check_vma=False,
    )
```

```python
import functools
import math

import jax
import jax.numpy as jnp
from jax import lax
from jax.experimental import pallas as pl
from jax.experimental.pallas import tpu as pltpu
from jax.sharding import PartitionSpec as P

thermal_reservoir_kelvin = 1.0
smearing = 0.25

MAIN = 256
TILE = 128
F32 = jnp.float32
BF16 = jnp.bfloat16


def ceil_div(a, b):
    return -(-a // b)


VMEM_BYTES = 56 << 20


def occupy(energy):
    return 1.0 / (jnp.exp(energy / thermal_reservoir_kelvin) - 1.0)


def dot_nn(a, b):
    return lax.dot_general(a, b, (((1,), (0,)), ((), ())), preferred_element_type=F32)


def dot_nt(a, b):
    return lax.dot_general(a, b, (((1,), (1,)), ((), ())), preferred_element_type=F32)


def slots_of(count, modes):
    return count + ceil_div(count, MAIN // (modes - MAIN))


def project_kernel(groups, n_qp, group, chunks, here_ref, home_ref, force_ref, *refs):
    outs = refs[: len(chunks)]
    rows_ref, main_ref, rest_ref = refs[len(chunks) :]
    modes = home_ref.shape[0]
    lines = rows_ref.shape[0]
    share = lines // groups
    rest = modes - MAIN
    per_slot = MAIN // rest
    depth = outs[0].shape[2]
    step = pl.program_id(0)
    here = force_ref.shape[1] // modes
    pitch = lines + 1

    @pl.when(step == 0)
    def _():
        line = lax.broadcasted_iota(jnp.int32, (lines, modes), 0)
        column = lax.broadcasted_iota(jnp.int32, (lines, modes), 1)
        own = here_ref[0] * share + line % share
        wanted = (line // share) * group + own
        select = jnp.logical_and(column == wanted, own < group).astype(BF16)
        rows_ref[...] = dot_nt(select, home_ref[...]).astype(BF16)

    result = dot_nn(rows_ref[...], force_ref[...])
    for c in range(here):
        row = (step * here + c) * pitch
        piece = result[:, c * modes : (c + 1) * modes]
        main_ref[0, pl.ds(row, lines), :] = piece[:, :TILE]
        main_ref[1, pl.ds(row, lines), :] = piece[:, TILE:MAIN]
        rest_ref[pl.ds(row, lines), :] = jnp.concatenate(
            [piece[:, MAIN:], jnp.zeros((lines, TILE - rest), F32)], axis=1
        )

    @pl.when(step == pl.num_programs(0) - 1)
    def _():
        lane = lax.broadcasted_iota(jnp.int32, (depth, TILE), 1)
        for (first, count), out_ref in zip(chunks, outs):
            for t in range(groups):
                base = t * share + first
                for r in range(count):
                    for h in range(2):
                        out_ref[t, r, :, h * TILE : (h + 1) * TILE] = main_ref[
                            h, pl.ds(base + r, depth, stride=pitch), :
                        ].astype(BF16)
                for g in range(ceil_div(count, per_slot)):
                    for h in range(2):
                        packed = jnp.zeros((depth, TILE), F32)
                        for b in range(per_slot // 2):
                            r = g * per_slot + h * (per_slot // 2) + b
                            if r < count:
                                piece = rest_ref[pl.ds(base + r, depth, stride=pitch), :]
                                if b > 0:
                                    piece = pltpu.roll(piece, b * rest, 1)
                                packed = jnp.where(lane // rest == b, piece, packed)
                        out_ref[t, count + g, :, h * TILE : (h + 1) * TILE] = packed.astype(BF16)


def project(here, home_vectors, force_table, groups, n_qp, group, share, chunks):
    modes = home_vectors.shape[0]
    lines = groups * share
    depth = force_table.shape[1] // modes
    per_step = 8 if depth % 8 == 0 else 4
    steps = depth // per_step
    shapes = [(groups, slots_of(count, modes), depth, MAIN) for _, count in chunks]
    return pl.pallas_call(
        functools.partial(project_kernel, groups, n_qp, group, chunks),
        grid=(steps,),
        in_specs=[
            pl.BlockSpec(memory_space=pltpu.SMEM),
            pl.BlockSpec((modes, modes), lambda i: (0, 0)),
            pl.BlockSpec((modes, per_step * modes), lambda i: (0, i)),
        ],
        out_specs=[pl.BlockSpec(shape, lambda i: (0, 0, 0, 0)) for shape in shapes],
        out_shape=[jax.ShapeDtypeStruct(shape, BF16) for shape in shapes],
        scratch_shapes=[
            pltpu.VMEM((lines, modes), BF16),
            pltpu.VMEM((2, (depth + 1) * (lines + 1), TILE), F32),
            pltpu.VMEM(((depth + 1) * (lines + 1), TILE), F32),
        ],
        compiler_params=pltpu.CompilerParams(vmem_limit_bytes=VMEM_BYTES),
        name="project",
    )(here, home_vectors, force_table)


def identity(size):
    return (
        lax.broadcasted_iota(jnp.int32, (size, size), 0)
        == lax.broadcasted_iota(jnp.int32, (size, size), 1)
    ).astype(BF16)


def pack_kernel(part_ref, partner_ref, weight_ref, grid_ref, freq_ref, out_ref):
    own_pairs, modes, _ = grid_ref.shape
    rest = modes - MAIN
    lines = rest // 2
    part = part_ref[0]
    line = lax.broadcasted_iota(jnp.int32, (lines, modes), 0)
    column = lax.broadcasted_iota(jnp.int32, (lines, modes), 1)
    select = (column == MAIN + part * lines + line).astype(BF16)
    freqs = freq_ref[...].astype(F32)
    blank = jnp.zeros((own_pairs, TILE - rest), F32)
    freq_tiles = (
        freqs[:, :TILE],
        freqs[:, TILE:MAIN],
        jnp.concatenate([freqs[:, MAIN:], blank], axis=1),
    )
    line16 = lax.broadcasted_iota(jnp.int32, (16, TILE), 0)
    lane16 = lax.broadcasted_iota(jnp.int32, (16, TILE), 1)
    for s in range(own_pairs):
        for p in range(2):

            @pl.when(part == p)
            def _():
                out_ref[s, :modes, :] = grid_ref[s, :, p * TILE : (p + 1) * TILE]

        turned = dot_nt(select, grid_ref[s])
        turned = (
            turned[:, :TILE],
            turned[:, TILE:MAIN],
            jnp.concatenate([turned[:, MAIN:], jnp.zeros((lines, TILE - rest), F32)], axis=1),
        )
        for h in range(3):
            start = modes + h * lines
            out_ref[s, start : start + lines, :] = turned[h].astype(BF16)
        pair = partner_ref[s].astype(F32)
        weight = weight_ref[s].astype(F32)
        side = jnp.where(lane16 == 0, pair, jnp.where(lane16 == 1, weight, 0.0))
        side = jnp.where(line16 == 3, side, 0.0)
        for h in range(3):
            side = jnp.where(line16 == h, freq_tiles[h][s : s + 1], side)
        start = modes + 3 * lines
        out_ref[s, start : start + 16, :] = side.astype(BF16)


def pack_own(part, partner, weights, grid_vectors, partner_frequencies):
    own_pairs, modes, _ = grid_vectors.shape
    smem = pl.BlockSpec(memory_space=pltpu.SMEM)
    vmem = pl.BlockSpec(memory_space=pltpu.VMEM)
    rows = modes + 3 * (modes - MAIN) // 2 + 16
    return pl.pallas_call(
        pack_kernel,
        in_specs=[smem, smem, smem, vmem, vmem],
        out_specs=vmem,
        out_shape=jax.ShapeDtypeStruct((own_pairs, rows, TILE), BF16),
        compiler_params=pltpu.CompilerParams(vmem_limit_bytes=VMEM_BYTES),
        name="pack_own",
    )(part, partner, weights, grid_vectors, partner_frequencies)


def arrange_kernel(
    pack_ref, partner_ref, weight_ref, grid_ref, grid_t_ref, freq_row_ref, freq_col_ref
):
    owners, parts, each, rows, _ = pack_ref.shape
    modes = grid_ref.shape[1]
    rest = modes - MAIN
    lines = rest // parts
    eye = identity(MAIN)
    source = lax.broadcasted_iota(jnp.int32, (TILE, TILE), 0)
    place = lax.broadcasted_iota(jnp.int32, (TILE, TILE), 1)
    spread = (source == place % rest).astype(BF16)
    eye_tile = (source == place).astype(BF16)
    lane = lax.broadcasted_iota(jnp.int32, (TILE, freq_col_ref.shape[1]), 1)
    line16 = lax.broadcasted_iota(jnp.int32, (16, TILE), 0)
    lane16 = lax.broadcasted_iota(jnp.int32, (16, TILE), 1)
    freq_col_ref[...] = jnp.zeros_like(freq_col_ref)

    def one(q, carry):
        for s in range(each):
            x = q * each + s
            for part in range(parts):
                grid_ref[x, :, part * TILE : (part + 1) * TILE] = pack_ref[q, part, s, :modes, :]
                for h in range(3):
                    start, width = modes + h * lines, min(TILE, modes - h * TILE)
                    piece = pack_ref[q, part, s, start : start + lines, :]
                    grid_t_ref[
                        x, MAIN + part * lines : MAIN + (part + 1) * lines, h * TILE : h * TILE + width
                    ] = piece[:, :width]
            grid_t_ref[x, :MAIN, :] = dot_nt(eye, grid_ref[x]).astype(BF16)
            side = pack_ref[q, 0, s, modes + 3 * lines : modes + 3 * lines + 16, :]
            wide = side.astype(F32)
            freq_row_ref[x, :, :TILE] = wide[0:1]
            freq_row_ref[x, :, TILE:MAIN] = wide[1:2]
            freq_row_ref[x, :, MAIN:] = dot_nn(side, spread)[2:3]
            columns = dot_nt(eye_tile, side)
            for h in range(3):
                width = min(TILE, modes - h * TILE)
                here = slice(h * TILE, h * TILE + width)
                freq_col_ref[here, :] = jnp.where(
                    lane[:width] == x, columns[:width, h : h + 1], freq_col_ref[here, :]
                )
            for spot, ref in ((0, partner_ref), (1, weight_ref)):
                found = jnp.sum(
                    jnp.where(jnp.logical_and(line16 == 3, lane16 == spot), wide, 0.0)
                )
                ref[x] = found.astype(ref.dtype)
        return carry

    lax.fori_loop(0, owners, one, 0, unroll=owners <= 4)


def arrange(pack, modes):
    owners, parts, each, _, _ = pack.shape
    pairs = owners * each
    smem = pl.BlockSpec(memory_space=pltpu.SMEM)
    vmem = pl.BlockSpec(memory_space=pltpu.VMEM)
    return pl.pallas_call(
        arrange_kernel,
        in_specs=[vmem],
        out_specs=[smem, smem, vmem, vmem, vmem, vmem],
        out_shape=[
            jax.ShapeDtypeStruct((pairs,), jnp.int32),
            jax.ShapeDtypeStruct((pairs,), F32),
            jax.ShapeDtypeStruct((pairs, modes, MAIN), BF16),
            jax.ShapeDtypeStruct((pairs, modes, modes), BF16),
            jax.ShapeDtypeStruct((pairs, 1, MAIN + TILE), F32),
            jax.ShapeDtypeStruct((modes, TILE), F32),
        ],
        compiler_params=pltpu.CompilerParams(vmem_limit_bytes=VMEM_BYTES),
        name="arrange",
    )(pack)


def interleave(heavy, light):
    done = 0
    for i, task in enumerate(heavy):
        task()
        upto = (i + 1) * len(light) // len(heavy)
        while done < upto:
            light[done]()
            done += 1
    while done < len(light):
        light[done]()
        done += 1


def coupling_kernel(
    share,
    block,
    behind,
    partner_ref,
    weight_ref,
    home_ref,
    grid_ref,
    grid_t_ref,
    freq_row_ref,
    freq_col_ref,
    home_row_ref,
    moved_ref,
    *refs,
):
    earlier_ref = refs[0] if behind else None
    (
        out_ref,
        turned_ref,
        grid_rest_ref,
        inner_rest_ref,
        pick_ref,
        rest_value_ref,
        *work,
    ) = refs[1:] if behind else refs
    gathers, inners, values, tabs, sums, rest_sums, firsts = (
        work[2 * i : 2 * i + 2] for i in range(7)
    )
    pairs = grid_ref.shape[0]
    modes = grid_ref.shape[1]
    rest = modes - MAIN
    sources, depth = moved_ref.shape[0], moved_ref.shape[2]
    per_slot = MAIN // rest
    rest_lanes = home_row_ref.shape[1]
    s2 = smearing * smearing
    steps = share // block

    for x in range(pairs):
        grid_rest_ref[x * rest : (x + 1) * rest, :] = grid_t_ref[x, MAIN:, :]
    eye = identity(modes)
    if share * rest < rest_lanes:
        inner_rest_ref[...] = jnp.zeros_like(inner_rest_ref)
    for r in range(share):
        slot, spot = share + r // per_slot, r % per_slot
        half, spot = spot // (per_slot // 2), spot % (per_slot // 2)
        gather_ref = gathers[r % 2]
        for s in range(sources):
            gather_ref[s * depth : (s + 1) * depth, :MAIN] = moved_ref[s, r].astype(F32)
            tail = moved_ref[s, slot, :, half * TILE : (half + 1) * TILE].astype(F32)
            if spot > 0:
                tail = pltpu.roll(tail, TILE - spot * rest, 1)
            gather_ref[s * depth : (s + 1) * depth, MAIN:] = tail[:, :rest]
        whole = gather_ref[...].astype(BF16)
        turned_ref[r * modes : (r + 1) * modes, :] = dot_nt(eye, whole).astype(BF16)
        found = dot_nn(grid_rest_ref[...], whole).astype(BF16)
        for x in range(pairs):
            inner_rest_ref[x, r * rest : (r + 1) * rest, :] = found[x * rest : (x + 1) * rest, :]

    row_id = lax.broadcasted_iota(jnp.int32, pick_ref.shape, 0)
    col_id = lax.broadcasted_iota(jnp.int32, pick_ref.shape, 1)
    pick_ref[...] = (row_id // rest == col_id).astype(BF16)
    for ref in (out_ref, *sums, *rest_sums, *firsts):
        ref[...] = jnp.zeros_like(ref)

    def contract_first(x, r, b, into):
        def task():
            found = dot_nn(turned_ref[r * modes : (r + 1) * modes, :], grid_ref[x])
            into[:, b * MAIN : (b + 1) * MAIN] = found.astype(BF16)

        return task

    def contract_second(x, b, source, into):
        lanes = slice(b * MAIN, (b + 1) * MAIN)

        def task():
            into[:, lanes] = dot_nn(grid_t_ref[partner_ref[x]], source[:, lanes])

        return task

    def line_shapes(v, t, w, c1, c2):
        d = t[0] - w
        e = t[1] - c1
        d = d * d + s2
        e = e * e + c2
        p = (v * v) * pl.reciprocal(d * e, approx=True)
        return (t[2] * e) * p, (t[3] * d) * p

    def weigh(step, source, tab, sum_ref, first_ref):
        state = {}

        def begin():
            state["w"] = [home_ref[step * block + b] for b in range(block)]
            state["c1"] = [w * w - s2 for w in state["w"]]
            state["c2"] = [(4.0 * s2) * (w * w) for w in state["w"]]
            state["total"] = [jnp.zeros((8, MAIN), F32) for _ in range(block)]

        def rows(n):
            def task():
                if n == 0:
                    begin()
                t = [tab[k, n : n + 16, :MAIN] for k in range(4)]
                for b in range(block):
                    v = source[n : n + 16, b * MAIN : (b + 1) * MAIN]
                    f, u = line_shapes(v, t, state["w"][b], state["c1"][b], state["c2"][b])
                    state["total"][b] = state["total"][b] + (f[:8] + f[8:])
                    r = step * block + b
                    sum_ref[n : n + 16, r : r + 1] = jnp.sum(
                        u[:, :TILE] + u[:, TILE:], axis=1, keepdims=True
                    )
                if n + 16 == modes:
                    for b in range(block):
                        r = step * block + b
                        line = jnp.sum(state["total"][b], axis=0, keepdims=True)
                        first_ref[r : r + 1, :MAIN] = line * (1.0 / state["w"][b])

            return task

        return [rows(n) for n in range(0, modes, 16)]

    def contract_rest(x):
        def task():
            rest_value_ref[...] = dot_nt(grid_t_ref[partner_ref[x]], inner_rest_ref[x])

        return task

    def weigh_rest(tab, sum_ref, first_ref):
        def tile(start):
            lanes = slice(start, start + TILE)
            state = {}

            def rows(n):
                def task():
                    if n == 0:
                        state["total"] = jnp.zeros((8, TILE), F32)
                        state["w"] = home_row_ref[0:1, lanes]
                        state["c1"] = home_row_ref[1:2, lanes]
                        state["c2"] = home_row_ref[2:3, lanes]
                    for k in range(n, n + 48, 16):
                        t = [tab[i, k : k + 16, MAIN:] for i in range(4)]
                        f, u = line_shapes(
                            rest_value_ref[k : k + 16, lanes], t, state["w"], state["c1"], state["c2"]
                        )
                        state["total"] = state["total"] + (f[:8] + f[8:])
                        sum_ref[k : k + 16, lanes] = u.astype(BF16)
                    if n + 48 == modes:
                        line = jnp.sum(state["total"], axis=0, keepdims=True)
                        line = line * home_row_ref[3:4, lanes]
                        for b in range(TILE // rest):
                            r = start // rest + b
                            if r < share:
                                first_ref[r : r + 1, MAIN:] = line[:, b * rest : (b + 1) * rest]

                return task

            return [rows(n) for n in range(0, modes, 48)]

        return [task for start in range(0, rest_lanes, TILE) for task in tile(start)]

    def tables(x, tab):
        state = {}

        def begin():
            w1 = freq_row_ref[x]
            spots = lax.broadcasted_iota(jnp.int32, freq_col_ref.shape, 1)
            w2 = jnp.sum(
                jnp.where(spots == partner_ref[x], freq_col_ref[...], 0.0), axis=1, keepdims=True
            )
            state["w"] = (w1, w2)
            state["o"] = (occupy(w1), occupy(w2))
            scale = weight_ref[x] * (smearing / math.pi / modes)
            state["i"] = (scale / w1, 1.0 / w2)

        def rows(n):
            def task():
                if n == 0:
                    begin()
                part = slice(n, n + 48)
                (w1, w2), (o1, o2), (i1, i2) = state["w"], state["o"], state["i"]
                w2, o2, i2 = w2[part], o2[part], i2[part]
                a = w1 - w2
                both = i1 * i2
                tab[0, part, :] = w1 + w2
                tab[1, part, :] = a * a
                tab[2, part, :] = (1.0 + o1 + o2) * both
                tab[3, part, :] = (4.0 * a) * (o2 - o1) * both

            return task

        return [rows(n) for n in range(0, modes, 48)]

    def collect(sum_ref, rest_sum_ref, state):
        def task():
            second = sum_ref[...] + dot_nn(rest_sum_ref[...], pick_ref[...])
            state["second"] = second.T[:share, :]

        return task

    def deliver(x, target, state, first_ref):
        out_ref[x, :share, :] += first_ref[:share, :]
        out_ref[target, :share, :] += state["second"]

    for task in tables(0, tabs[0]):
        task()
    for g in range(2):
        for b in range(block):
            x, step = jnp.int32(g // steps), g % steps
            contract_first(x, step * block + b, b, inners[g])()
    for b in range(block):
        contract_second(jnp.int32(0), b, inners[0], values[0])()

    def two_pairs(i, carry):
        for e in range(2):
            x = i * 2 + e

            def later(g):
                return jnp.minimum(i * 2 + g // steps, pairs - 1), g % steps

            before = jnp.maximum(x - 1, 0)
            target = partner_ref[before]
            extra = weigh_rest(tabs[e], rest_sums[e], firsts[e])
            extra = extra + tables(jnp.minimum(x + 1, pairs - 1), tabs[1 - e])
            contract_rest(x)()
            done = {}
            for s in range(steps):
                g = e * steps + s
                heavy = []
                for b in range(block):
                    x1, _ = later(g + 1)
                    heavy.append(contract_second(x1, b, inners[(g + 1) % 2], values[(g + 1) % 2]))
                for b in range(block):
                    x2, step2 = later(g + 2)
                    heavy.append(contract_first(x2, step2 * block + b, b, inners[g % 2]))
                light = weigh(s, values[g % 2], tabs[e], sums[e], firsts[e])
                light = light + extra[s * len(extra) // steps : (s + 1) * len(extra) // steps]
                if s == 0:
                    heavy.insert(1, collect(sums[1 - e], rest_sums[1 - e], done))
                interleave(heavy, light)
            deliver(before, target, done, firsts[1 - e])
        return carry

    lax.fori_loop(0, pairs // 2, two_pairs, 0)
    last = {}
    collect(sums[1], rest_sums[1], last)()
    deliver(pairs - 1, partner_ref[pairs - 1], last, firsts[1])

    if behind is None:
        return
    row = share
    if behind:
        place = ceil_div(share, 8) * 8
        out_ref[:, place:, :] = earlier_ref[...]
        row = place + behind
    totals = jnp.zeros(out_ref.shape[1:], F32)
    for y in range(pairs):
        totals = totals + out_ref[y]
    widths = jnp.sum(totals, axis=1, keepdims=True) * (1.0 / (pairs * modes))
    spread = jnp.where(
        lax.broadcasted_iota(jnp.int32, totals.shape, 0)
        == lax.broadcasted_iota(jnp.int32, totals.shape, 1),
        widths,
        0.0,
    )
    out_ref[:, row, :] = jnp.broadcast_to(jnp.sum(spread, axis=0, keepdims=True), (pairs, modes))


def coupling(behind, partner, weights, home, grid, grid_t, freq_rows, freq_cols, moved, *earlier):
    pairs, modes = grid.shape[0], grid.shape[1]
    share = home.shape[0]
    rest = modes - MAIN
    rest_lanes = ceil_div(share * rest, TILE) * TILE
    row = jnp.repeat(home, rest)
    row = jnp.pad(row, (0, rest_lanes - share * rest), constant_values=1.0)
    s2 = smearing * smearing
    home_row = jnp.stack([row, row * row - s2, (4.0 * s2) * (row * row), 1.0 / row])
    padded = (share // 8 + 1) * 8
    if behind:
        padded = ceil_div(share, 8) * 8 + earlier[0].shape[1]
    smem = pl.BlockSpec(memory_space=pltpu.SMEM)
    vmem = pl.BlockSpec(memory_space=pltpu.VMEM)
    block = 3 if share % 3 == 0 else 1
    assert pairs % 2 == 0
    scratch = (
        [
            pltpu.VMEM((share * modes, modes), BF16),
            pltpu.VMEM((pairs * rest, modes), BF16),
            pltpu.VMEM((pairs, rest_lanes, modes), BF16),
            pltpu.VMEM((rest_lanes, TILE), BF16),
            pltpu.VMEM((modes, rest_lanes), F32),
        ]
        + [pltpu.VMEM((modes, modes), F32)] * 2
        + [pltpu.VMEM((modes, block * MAIN), BF16)] * 2
        + [pltpu.VMEM((modes, block * MAIN), F32)] * 2
        + [pltpu.VMEM((4, modes, MAIN + TILE), F32)] * 2
        + [pltpu.VMEM((modes, TILE), F32)] * 2
        + [pltpu.VMEM((modes, rest_lanes), BF16)] * 2
        + [pltpu.VMEM((padded, modes), F32)] * 2
    )
    return pl.pallas_call(
        functools.partial(coupling_kernel, share, block, behind),
        in_specs=[smem] * 3 + [vmem] * (6 + len(earlier)),
        out_specs=vmem,
        out_shape=jax.ShapeDtypeStruct((pairs, padded, modes), F32),
        scratch_shapes=scratch,
        compiler_params=pltpu.CompilerParams(vmem_limit_bytes=VMEM_BYTES),
        cost_estimate=pl.CostEstimate(
            flops=4 * share * pairs * modes**3,
            bytes_accessed=8 * share * modes * modes,
            transcendentals=2 * share * pairs * modes**2,
        ),
        name="coupling",
    )(partner, weights, home, grid, grid_t, freq_rows, freq_cols, home_row, moved, *earlier)


def local(
    home_vectors, home_freqs, grid_vectors, partner_frequencies, force_table, partner, weights
):
    own_pairs = partner.shape[0]
    modes = home_vectors.shape[0]
    n_mode = lax.axis_size("mode")
    n_fc = lax.axis_size("fc")
    n_qp = lax.axis_size("qp")
    groups = n_mode * n_fc
    group = modes // groups
    pairs = own_pairs * n_qp
    share = ceil_div(group, n_qp)
    here = lax.axis_index("qp")
    if share % 6 == 0 and share > 6:
        chunks = ((0, 6), (6, share - 6))
    else:
        chunks = ((0, share),)

    assert n_fc * TILE == MAIN
    own_part = lax.axis_index("fc").astype(jnp.int32)[None]
    pack = pack_own(own_part, partner, weights, grid_vectors, partner_frequencies)
    pack = lax.all_gather(pack, ("qp", "fc"), axis=0)
    pack = pack.reshape(n_qp, n_fc, own_pairs, pack.shape[2], TILE)

    sent = project(
        here.astype(jnp.int32)[None], home_vectors, force_table, groups, n_qp, group, share, chunks
    )
    moved = [
        lax.all_to_all(x, ("mode", "fc"), split_axis=0, concat_axis=0, tiled=True) for x in sent
    ]

    own = lax.axis_index(("mode", "fc"))
    home = home_freqs.astype(F32).reshape(groups, group)
    home = jnp.pad(home, ((0, 0), (0, share * n_qp - group)), constant_values=1.0)
    home = lax.dynamic_slice(home, (own, here * share), (1, share)).reshape(share)

    shared = arrange(pack, modes)
    found = ()
    for at, ((first, count), block) in enumerate(zip(chunks, moved)):
        behind = None if at + 1 < len(chunks) else 0 if at == 0 else chunks[0][1]
        found = (
            coupling(
                behind, shared[0], shared[1], home[first : first + count], *shared[2:], block, *found
            ),
        )
    padded = found[0].shape[1]
    back = lax.all_to_all(
        found[0].reshape(n_qp, own_pairs, padded, modes),
        "qp",
        split_axis=0,
        concat_axis=0,
        tiled=True,
    )
    last = chunks[-1][1]
    places = [(0, last)]
    if len(chunks) > 1:
        places.insert(0, (ceil_div(last, 8) * 8, chunks[0][1]))
    row = places[0][0] + places[0][1]
    widths = jnp.concatenate([back[:, 0, row, a : a + c] for a, c in places], axis=1)
    widths = widths.reshape(n_qp * share)[:group]
    parts = [back[:, :, a : a + c, :] for a, c in places]
    collision = jnp.transpose(jnp.concatenate(parts, axis=2), (0, 2, 1, 3))
    collision = collision.reshape(n_qp * share, own_pairs, modes)[:group]
    return (widths, collision)


def solution(mesh):
    placed = (
        P("grp", None),
        P("grp"),
        P("qp", None, None),
        P("qp", None),
        P(None, ("mode", "fc")),
        P(("grp", "qp")),
        P(("grp", "qp")),
    )
    return jax.shard_map(
        local,
        mesh=mesh,
        in_specs=placed,
        out_specs=(P(("grp", "mode", "fc")), P(("mode", "fc"), ("grp", "qp"), None)),
        check_vma=False,
    )
```

```python
import functools
import math

import jax
import jax.numpy as jnp
from jax import lax
from jax.experimental import pallas as pl
from jax.experimental.pallas import tpu as pltpu
from jax.sharding import PartitionSpec as P

thermal_reservoir_kelvin = 1.0
smearing = 0.25

MAIN = 256
TILE = 128
F32 = jnp.float32
BF16 = jnp.bfloat16


def ceil_div(a, b):
    return -(-a // b)


VMEM_BYTES = 56 << 20


def occupy(energy):
    return 1.0 / (jnp.exp(energy / thermal_reservoir_kelvin) - 1.0)


def dot_nn(a, b):
    return lax.dot_general(a, b, (((1,), (0,)), ((), ())), preferred_element_type=F32)


def dot_nt(a, b):
    return lax.dot_general(a, b, (((1,), (1,)), ((), ())), preferred_element_type=F32)


def slots_of(count, modes):
    return count + ceil_div(count, MAIN // (modes - MAIN))


STREAMS = 3


def project_kernel(groups, group, share, first, count, here_ref, home_ref, *refs):
    force_refs, (out_ref, rows_ref, main_ref, rest_ref) = refs[:STREAMS], refs[STREAMS:]
    modes = home_ref.shape[0]
    lines = groups * count
    rest = modes - MAIN
    per_slot = MAIN // rest
    depth = out_ref.shape[2]
    step = pl.program_id(0)
    here = force_refs[0].shape[1] // modes
    pitch = lines + 1

    @pl.when(step == 0)
    def _():
        line = lax.broadcasted_iota(jnp.int32, (lines, modes), 0)
        column = lax.broadcasted_iota(jnp.int32, (lines, modes), 1)
        own = here_ref[0] * share + first + line % count
        wanted = (line // count) * group + own
        select = jnp.logical_and(column == wanted, own < group).astype(BF16)
        rows_ref[...] = dot_nt(select, home_ref[...]).astype(BF16)

    force = jnp.concatenate([ref[...] for ref in force_refs], axis=0)
    result = dot_nn(rows_ref[...], force)
    for c in range(here):
        row = (step * here + c) * pitch
        piece = result[:, c * modes : (c + 1) * modes]
        main_ref[0, pl.ds(row, lines), :] = piece[:, :TILE]
        main_ref[1, pl.ds(row, lines), :] = piece[:, TILE:MAIN]
        rest_ref[pl.ds(row, lines), :] = jnp.concatenate(
            [piece[:, MAIN:], jnp.zeros((lines, TILE - rest), F32)], axis=1
        )

    @pl.when(step == pl.num_programs(0) - 1)
    def _():
        lane = lax.broadcasted_iota(jnp.int32, (depth, TILE), 1)
        for t in range(groups):
            base = t * count
            for r in range(count):
                for h in range(2):
                    out_ref[t, r, :, h * TILE : (h + 1) * TILE] = main_ref[
                        h, pl.ds(base + r, depth, stride=pitch), :
                    ].astype(BF16)
            for g in range(ceil_div(count, per_slot)):
                for h in range(2):
                    packed = jnp.zeros((depth, TILE), F32)
                    for b in range(per_slot // 2):
                        r = g * per_slot + h * (per_slot // 2) + b
                        if r < count:
                            piece = rest_ref[pl.ds(base + r, depth, stride=pitch), :]
                            if b > 0:
                                piece = pltpu.roll(piece, b * rest, 1)
                            packed = jnp.where(lane // rest == b, piece, packed)
                    out_ref[t, count + g, :, h * TILE : (h + 1) * TILE] = packed.astype(BF16)


def project(here, home_vectors, force_table, groups, group, share, first, count):
    modes = home_vectors.shape[0]
    lines = groups * count
    depth = force_table.shape[1] // modes
    per_step = 8 if depth % 8 == 0 else 4
    rows = modes // STREAMS
    shape = (groups, slots_of(count, modes), depth, MAIN)

    def stream(k):
        return pl.BlockSpec((rows, per_step * modes), lambda i: (k, i))

    return pl.pallas_call(
        functools.partial(project_kernel, groups, group, share, first, count),
        grid=(depth // per_step,),
        in_specs=[
            pl.BlockSpec(memory_space=pltpu.SMEM),
            pl.BlockSpec((modes, modes), lambda i: (0, 0)),
        ]
        + [stream(k) for k in range(STREAMS)],
        out_specs=pl.BlockSpec(shape, lambda i: (0, 0, 0, 0)),
        out_shape=jax.ShapeDtypeStruct(shape, BF16),
        scratch_shapes=[
            pltpu.VMEM((lines, modes), BF16),
            pltpu.VMEM((2, (depth + 1) * (lines + 1), TILE), F32),
            pltpu.VMEM(((depth + 1) * (lines + 1), TILE), F32),
        ],
        compiler_params=pltpu.CompilerParams(vmem_limit_bytes=VMEM_BYTES),
        cost_estimate=pl.CostEstimate(
            flops=2 * lines * modes * modes * depth,
            bytes_accessed=2 * modes * modes * depth,
            transcendentals=0,
        ),
        name="project",
    )(here, home_vectors, *[force_table] * STREAMS)


def identity(size):
    return (
        lax.broadcasted_iota(jnp.int32, (size, size), 0)
        == lax.broadcasted_iota(jnp.int32, (size, size), 1)
    ).astype(BF16)


def pack_kernel(part_ref, partner_ref, weight_ref, grid_ref, freq_ref, upper_ref, lower_ref):
    own_pairs, modes, _ = grid_ref.shape
    rest = modes - MAIN
    lines = rest // 2
    cut = upper_ref.shape[1]
    part = part_ref[0]
    line = lax.broadcasted_iota(jnp.int32, (lines, modes), 0)
    column = lax.broadcasted_iota(jnp.int32, (lines, modes), 1)
    select = (column == MAIN + part * lines + line).astype(BF16)
    freqs = freq_ref[...].astype(F32)
    blank = jnp.zeros((own_pairs, TILE - rest), F32)
    freq_tiles = (
        freqs[:, :TILE],
        freqs[:, TILE:MAIN],
        jnp.concatenate([freqs[:, MAIN:], blank], axis=1),
    )
    line16 = lax.broadcasted_iota(jnp.int32, (16, TILE), 0)
    lane16 = lax.broadcasted_iota(jnp.int32, (16, TILE), 1)
    for s in range(own_pairs):
        for p in range(2):

            @pl.when(part == p)
            def _():
                upper_ref[s] = grid_ref[s, :cut, p * TILE : (p + 1) * TILE]
                lower_ref[s, : modes - cut, :] = grid_ref[s, cut:, p * TILE : (p + 1) * TILE]

        turned = dot_nt(select, grid_ref[s])
        turned = (
            turned[:, :TILE],
            turned[:, TILE:MAIN],
            jnp.concatenate([turned[:, MAIN:], jnp.zeros((lines, TILE - rest), F32)], axis=1),
        )
        for h in range(3):
            start = modes - cut + h * lines
            lower_ref[s, start : start + lines, :] = turned[h].astype(BF16)
        pair = partner_ref[s].astype(F32)
        weight = weight_ref[s].astype(F32)
        side = jnp.where(lane16 == 0, pair, jnp.where(lane16 == 1, weight, 0.0))
        side = jnp.where(line16 == 3, side, 0.0)
        for h in range(3):
            side = jnp.where(line16 == h, freq_tiles[h][s : s + 1], side)
        start = modes - cut + 3 * lines
        lower_ref[s, start : start + 16, :] = side.astype(BF16)


def pack_own(part, partner, weights, grid_vectors, partner_frequencies):
    own_pairs, modes, _ = grid_vectors.shape
    smem = pl.BlockSpec(memory_space=pltpu.SMEM)
    vmem = pl.BlockSpec(memory_space=pltpu.VMEM)
    rows = (modes + 3 * (modes - MAIN) // 2 + 16) // 2
    shape = jax.ShapeDtypeStruct((own_pairs, rows, TILE), BF16)
    return pl.pallas_call(
        pack_kernel,
        in_specs=[smem, smem, smem, vmem, vmem],
        out_specs=[vmem] * 2,
        out_shape=[shape] * 2,
        compiler_params=pltpu.CompilerParams(vmem_limit_bytes=VMEM_BYTES),
        name="pack_own",
    )(part, partner, weights, grid_vectors, partner_frequencies)


def arrange_kernel(
    upper_ref, lower_ref, partner_ref, weight_ref, grid_ref, grid_t_ref, freq_row_ref, freq_col_ref
):
    owners, parts, each, cut, _ = upper_ref.shape
    modes = grid_ref.shape[1]
    rest = modes - MAIN
    lines = rest // parts
    left = modes - cut
    eye = identity(MAIN)
    source = lax.broadcasted_iota(jnp.int32, (TILE, TILE), 0)
    place = lax.broadcasted_iota(jnp.int32, (TILE, TILE), 1)
    spread = (source == place % rest).astype(BF16)
    eye_tile = (source == place).astype(BF16)
    lane = lax.broadcasted_iota(jnp.int32, (TILE, freq_col_ref.shape[1]), 1)
    line16 = lax.broadcasted_iota(jnp.int32, (16, TILE), 0)
    lane16 = lax.broadcasted_iota(jnp.int32, (16, TILE), 1)
    freq_col_ref[...] = jnp.zeros_like(freq_col_ref)

    def one(q, carry):
        for s in range(each):
            x = q * each + s
            for part in range(parts):
                lanes = slice(part * TILE, (part + 1) * TILE)
                grid_ref[x, :cut, lanes] = upper_ref[q, part, s]
                grid_ref[x, cut:, lanes] = lower_ref[q, part, s, :left, :]
                for h in range(3):
                    start, width = left + h * lines, min(TILE, modes - h * TILE)
                    piece = lower_ref[q, part, s, start : start + lines, :]
                    grid_t_ref[
                        x, MAIN + part * lines : MAIN + (part + 1) * lines, h * TILE : h * TILE + width
                    ] = piece[:, :width]
            grid_t_ref[x, :MAIN, :] = dot_nt(eye, grid_ref[x]).astype(BF16)
            side = lower_ref[q, 0, s, left + 3 * lines : left + 3 * lines + 16, :]
            wide = side.astype(F32)
            freq_row_ref[x, :, :TILE] = wide[0:1]
            freq_row_ref[x, :, TILE:MAIN] = wide[1:2]
            freq_row_ref[x, :, MAIN:] = dot_nn(side, spread)[2:3]
            columns = dot_nt(eye_tile, side)
            for h in range(3):
                width = min(TILE, modes - h * TILE)
                here = slice(h * TILE, h * TILE + width)
                freq_col_ref[here, :] = jnp.where(
                    lane[:width] == x, columns[:width, h : h + 1], freq_col_ref[here, :]
                )
            for spot, ref in ((0, partner_ref), (1, weight_ref)):
                found = jnp.sum(
                    jnp.where(jnp.logical_and(line16 == 3, lane16 == spot), wide, 0.0)
                )
                ref[x] = found.astype(ref.dtype)
        return carry

    lax.fori_loop(0, owners, one, 0, unroll=owners <= 4)


def arrange(packs, modes):
    owners, parts, each, _, _ = packs[0].shape
    pairs = owners * each
    smem = pl.BlockSpec(memory_space=pltpu.SMEM)
    vmem = pl.BlockSpec(memory_space=pltpu.VMEM)
    return pl.pallas_call(
        arrange_kernel,
        in_specs=[vmem] * 2,
        out_specs=[smem, smem, vmem, vmem, vmem, vmem],
        out_shape=[
            jax.ShapeDtypeStruct((pairs,), jnp.int32),
            jax.ShapeDtypeStruct((pairs,), F32),
            jax.ShapeDtypeStruct((pairs, modes, MAIN), BF16),
            jax.ShapeDtypeStruct((pairs, modes, modes), BF16),
            jax.ShapeDtypeStruct((pairs, 1, MAIN + TILE), F32),
            jax.ShapeDtypeStruct((modes, TILE), F32),
        ],
        compiler_params=pltpu.CompilerParams(vmem_limit_bytes=VMEM_BYTES),
        name="arrange",
    )(*packs)


def interleave(heavy, light):
    done = 0
    for i, task in enumerate(heavy):
        task()
        upto = (i + 1) * len(light) // len(heavy)
        while done < upto:
            light[done]()
            done += 1
    while done < len(light):
        light[done]()
        done += 1


def coupling_kernel(
    share,
    block,
    partner_ref,
    weight_ref,
    home_ref,
    grid_ref,
    grid_t_ref,
    freq_row_ref,
    freq_col_ref,
    home_row_ref,
    moved_ref,
    out_ref,
    turned_ref,
    grid_rest_ref,
    inner_rest_ref,
    pick_ref,
    rest_value_ref,
    *work,
):
    gathers, inners, values, tabs, sums, rest_sums, firsts = (
        work[2 * i : 2 * i + 2] for i in range(7)
    )
    pairs = grid_ref.shape[0]
    modes = grid_ref.shape[1]
    rest = modes - MAIN
    sources, depth = moved_ref.shape[0], moved_ref.shape[2]
    per_slot = MAIN // rest
    rest_lanes = home_row_ref.shape[1]
    s2 = smearing * smearing
    steps = share // block

    for x in range(pairs):
        grid_rest_ref[x * rest : (x + 1) * rest, :] = grid_t_ref[x, MAIN:, :]
    eye = identity(modes)
    if share * rest < rest_lanes:
        inner_rest_ref[...] = jnp.zeros_like(inner_rest_ref)
    for r in range(share):
        slot, spot = share + r // per_slot, r % per_slot
        half, spot = spot // (per_slot // 2), spot % (per_slot // 2)
        gather_ref = gathers[r % 2]
        for s in range(sources):
            gather_ref[s * depth : (s + 1) * depth, :MAIN] = moved_ref[s, r].astype(F32)
            tail = moved_ref[s, slot, :, half * TILE : (half + 1) * TILE].astype(F32)
            if spot > 0:
                tail = pltpu.roll(tail, TILE - spot * rest, 1)
            gather_ref[s * depth : (s + 1) * depth, MAIN:] = tail[:, :rest]
        whole = gather_ref[...].astype(BF16)
        turned_ref[r * modes : (r + 1) * modes, :] = dot_nt(eye, whole).astype(BF16)
        found = dot_nn(grid_rest_ref[...], whole).astype(BF16)
        for x in range(pairs):
            inner_rest_ref[x, r * rest : (r + 1) * rest, :] = found[x * rest : (x + 1) * rest, :]

    row_id = lax.broadcasted_iota(jnp.int32, pick_ref.shape, 0)
    col_id = lax.broadcasted_iota(jnp.int32, pick_ref.shape, 1)
    pick_ref[...] = (row_id // rest == col_id).astype(BF16)
    for ref in (out_ref, *sums, *rest_sums, *firsts):
        ref[...] = jnp.zeros_like(ref)

    def contract_first(x, r, b, into):
        def task():
            found = dot_nn(turned_ref[r * modes : (r + 1) * modes, :], grid_ref[x])
            into[:, b * MAIN : (b + 1) * MAIN] = found.astype(BF16)

        return task

    def contract_second(x, b, source, into):
        lanes = slice(b * MAIN, (b + 1) * MAIN)

        def task():
            into[:, lanes] = dot_nn(grid_t_ref[partner_ref[x]], source[:, lanes])

        return task

    def line_shapes(v, t, w, c1, c2):
        p = v * v
        d = t[0] - w
        e = t[1] - c1
        return (
            (p * t[2]) * pl.reciprocal(d * d + s2, approx=True),
            (p * t[3]) * pl.reciprocal(e * e + c2, approx=True),
        )

    def weigh(step, source, tab, sum_ref, first_ref):
        state = {}

        def begin():
            state["w"] = [home_ref[step * block + b] for b in range(block)]
            state["c1"] = [w * w - s2 for w in state["w"]]
            state["c2"] = [(4.0 * s2) * (w * w) for w in state["w"]]
            state["total"] = [jnp.zeros((8, MAIN), F32) for _ in range(block)]

        def rows(n):
            def task():
                if n == 0:
                    begin()
                t = [tab[k, n : n + 16, :MAIN] for k in range(4)]
                for b in range(block):
                    v = source[n : n + 16, b * MAIN : (b + 1) * MAIN]
                    f, u = line_shapes(v, t, state["w"][b], state["c1"][b], state["c2"][b])
                    state["total"][b] = state["total"][b] + (f[:8] + f[8:])
                    r = step * block + b
                    sum_ref[n : n + 16, r : r + 1] = jnp.sum(
                        u[:, :TILE] + u[:, TILE:], axis=1, keepdims=True
                    )
                if n + 16 == modes:
                    for b in range(block):
                        r = step * block + b
                        line = jnp.sum(state["total"][b], axis=0, keepdims=True)
                        first_ref[r : r + 1, :MAIN] = line * (1.0 / state["w"][b])

            return task

        return [rows(n) for n in range(0, modes, 16)]

    def contract_rest(x):
        def task():
            rest_value_ref[...] = dot_nt(grid_t_ref[partner_ref[x]], inner_rest_ref[x])

        return task

    def weigh_rest(tab, sum_ref, first_ref):
        def tile(start):
            lanes = slice(start, start + TILE)
            state = {}

            def rows(n):
                def task():
                    if n == 0:
                        state["total"] = jnp.zeros((8, TILE), F32)
                        state["w"] = home_row_ref[0:1, lanes]
                        state["c1"] = home_row_ref[1:2, lanes]
                        state["c2"] = home_row_ref[2:3, lanes]
                    for k in range(n, n + 48, 16):
                        t = [tab[i, k : k + 16, MAIN:] for i in range(4)]
                        f, u = line_shapes(
                            rest_value_ref[k : k + 16, lanes], t, state["w"], state["c1"], state["c2"]
                        )
                        state["total"] = state["total"] + (f[:8] + f[8:])
                        sum_ref[k : k + 16, lanes] = u.astype(BF16)
                    if n + 48 == modes:
                        line = jnp.sum(state["total"], axis=0, keepdims=True)
                        line = line * home_row_ref[3:4, lanes]
                        for b in range(TILE // rest):
                            r = start // rest + b
                            if r < share:
                                first_ref[r : r + 1, MAIN:] = line[:, b * rest : (b + 1) * rest]

                return task

            return [rows(n) for n in range(0, modes, 48)]

        return [task for start in range(0, rest_lanes, TILE) for task in tile(start)]

    def tables(x, tab):
        state = {}

        def begin():
            w1 = freq_row_ref[x]
            spots = lax.broadcasted_iota(jnp.int32, freq_col_ref.shape, 1)
            w2 = jnp.sum(
                jnp.where(spots == partner_ref[x], freq_col_ref[...], 0.0), axis=1, keepdims=True
            )
            state["w"] = (w1, w2)
            state["o"] = (occupy(w1), occupy(w2))
            scale = weight_ref[x] * (smearing / math.pi / modes)
            state["i"] = (scale / w1, 1.0 / w2)

        def rows(n):
            def task():
                if n == 0:
                    begin()
                part = slice(n, n + 48)
                (w1, w2), (o1, o2), (i1, i2) = state["w"], state["o"], state["i"]
                w2, o2, i2 = w2[part], o2[part], i2[part]
                a = w1 - w2
                both = i1 * i2
                tab[0, part, :] = w1 + w2
                tab[1, part, :] = a * a
                tab[2, part, :] = (1.0 + o1 + o2) * both
                tab[3, part, :] = (4.0 * a) * (o2 - o1) * both

            return task

        return [rows(n) for n in range(0, modes, 48)]

    def collect(sum_ref, rest_sum_ref, state):
        def task():
            second = sum_ref[...] + dot_nn(rest_sum_ref[...], pick_ref[...])
            state["second"] = second.T[:share, :]

        return task

    def deliver(x, target, state, first_ref):
        out_ref[x, :share, :] += first_ref[:share, :]
        out_ref[target, :share, :] += state["second"]

    for task in tables(0, tabs[0]):
        task()
    for g in range(2):
        for b in range(block):
            x, step = jnp.int32(g // steps), g % steps
            contract_first(x, step * block + b, b, inners[g])()
    for b in range(block):
        contract_second(jnp.int32(0), b, inners[0], values[0])()

    def two_pairs(i, carry):
        for e in range(2):
            x = i * 2 + e

            def later(g):
                return jnp.minimum(i * 2 + g // steps, pairs - 1), g % steps

            before = jnp.maximum(x - 1, 0)
            target = partner_ref[before]
            extra = weigh_rest(tabs[e], rest_sums[e], firsts[e])
            extra = extra + tables(jnp.minimum(x + 1, pairs - 1), tabs[1 - e])
            contract_rest(x)()
            done = {}
            for s in range(steps):
                g = e * steps + s
                heavy = []
                for b in range(block):
                    x1, _ = later(g + 1)
                    heavy.append(contract_second(x1, b, inners[(g + 1) % 2], values[(g + 1) % 2]))
                for b in range(block):
                    x2, step2 = later(g + 2)
                    heavy.append(contract_first(x2, step2 * block + b, b, inners[g % 2]))
                light = weigh(s, values[g % 2], tabs[e], sums[e], firsts[e])
                light = light + extra[s * len(extra) // steps : (s + 1) * len(extra) // steps]
                if s == 0:
                    heavy.insert(1, collect(sums[1 - e], rest_sums[1 - e], done))
                interleave(heavy, light)
            deliver(before, target, done, firsts[1 - e])
        return carry

    lax.fori_loop(0, pairs // 2, two_pairs, 0)
    last = {}
    collect(sums[1], rest_sums[1], last)()
    deliver(pairs - 1, partner_ref[pairs - 1], last, firsts[1])

    totals = jnp.zeros(out_ref.shape[1:], F32)
    for y in range(pairs):
        totals = totals + out_ref[y]
    widths = jnp.sum(totals, axis=1, keepdims=True) * (1.0 / (pairs * modes))
    spread = jnp.where(
        lax.broadcasted_iota(jnp.int32, totals.shape, 0)
        == lax.broadcasted_iota(jnp.int32, totals.shape, 1),
        widths,
        0.0,
    )
    out_ref[:, share, :] = jnp.broadcast_to(
        jnp.sum(spread, axis=0, keepdims=True), (pairs, modes)
    )


def coupling(partner, weights, home, grid, grid_t, freq_rows, freq_cols, moved):
    pairs, modes = grid.shape[0], grid.shape[1]
    share = home.shape[0]
    rest = modes - MAIN
    rest_lanes = ceil_div(share * rest, TILE) * TILE
    row = jnp.repeat(home, rest)
    row = jnp.pad(row, (0, rest_lanes - share * rest), constant_values=1.0)
    s2 = smearing * smearing
    home_row = jnp.stack([row, row * row - s2, (4.0 * s2) * (row * row), 1.0 / row])
    padded = (share // 8 + 1) * 8
    smem = pl.BlockSpec(memory_space=pltpu.SMEM)
    vmem = pl.BlockSpec(memory_space=pltpu.VMEM)
    block = 3 if share % 3 == 0 else 1
    assert pairs % 2 == 0
    scratch = (
        [
            pltpu.VMEM((share * modes, modes), BF16),
            pltpu.VMEM((pairs * rest, modes), BF16),
            pltpu.VMEM((pairs, rest_lanes, modes), BF16),
            pltpu.VMEM((rest_lanes, TILE), BF16),
            pltpu.VMEM((modes, rest_lanes), F32),
        ]
        + [pltpu.VMEM((modes, modes), F32)] * 2
        + [pltpu.VMEM((modes, block * MAIN), BF16)] * 2
        + [pltpu.VMEM((modes, block * MAIN), F32)] * 2
        + [pltpu.VMEM((4, modes, MAIN + TILE), F32)] * 2
        + [pltpu.VMEM((modes, TILE), F32)] * 2
        + [pltpu.VMEM((modes, rest_lanes), BF16)] * 2
        + [pltpu.VMEM((padded, modes), F32)] * 2
    )
    return pl.pallas_call(
        functools.partial(coupling_kernel, share, block),
        in_specs=[smem, smem, smem, vmem, vmem, vmem, vmem, vmem, vmem],
        out_specs=vmem,
        out_shape=jax.ShapeDtypeStruct((pairs, padded, modes), F32),
        scratch_shapes=scratch,
        compiler_params=pltpu.CompilerParams(vmem_limit_bytes=VMEM_BYTES),
        cost_estimate=pl.CostEstimate(
            flops=4 * share * pairs * modes**3,
            bytes_accessed=8 * share * modes * modes,
            transcendentals=2 * share * pairs * modes**2,
        ),
        name="coupling",
    )(partner, weights, home, grid, grid_t, freq_rows, freq_cols, home_row, moved)


def local(
    home_vectors, home_freqs, grid_vectors, partner_frequencies, force_table, partner, weights
):
    own_pairs = partner.shape[0]
    modes = home_vectors.shape[0]
    n_mode = lax.axis_size("mode")
    n_fc = lax.axis_size("fc")
    n_qp = lax.axis_size("qp")
    groups = n_mode * n_fc
    group = modes // groups
    pairs = own_pairs * n_qp
    share = ceil_div(group, n_qp)
    here = lax.axis_index("qp")
    if share % 6 == 0 and share > 6:
        chunks = ((0, 6), (6, share - 6))
    else:
        chunks = ((0, share),)

    assert n_fc * TILE == MAIN
    own_part = lax.axis_index("fc").astype(jnp.int32)[None]
    packs = pack_own(own_part, partner, weights, grid_vectors, partner_frequencies)
    packs = [lax.all_gather(half, ("qp", "fc"), axis=0) for half in packs]
    packs = [half.reshape(n_qp, n_fc, own_pairs, half.shape[2], TILE) for half in packs]

    here_word = here.astype(jnp.int32)[None]
    moved = []
    for first, count in chunks:
        sent = project(here_word, home_vectors, force_table, groups, group, share, first, count)
        moved.append(
            lax.all_to_all(sent, ("mode", "fc"), split_axis=0, concat_axis=0, tiled=True)
        )

    own = lax.axis_index(("mode", "fc"))
    home = home_freqs.astype(F32).reshape(groups, group)
    home = jnp.pad(home, ((0, 0), (0, share * n_qp - group)), constant_values=1.0)
    home = lax.dynamic_slice(home, (own, here * share), (1, share)).reshape(share)

    shared = arrange(packs, modes)
    parts, widths = [], []
    for (first, count), block in zip(chunks, moved):
        found = coupling(
            shared[0], shared[1], home[first : first + count], *shared[2:], block
        )
        back = lax.all_to_all(
            found.reshape(n_qp, own_pairs, found.shape[1], modes),
            "qp",
            split_axis=0,
            concat_axis=0,
            tiled=True,
        )
        widths.append(back[:, 0, count, :count])
        parts.append(back[:, :, :count, :])
    widths = jnp.concatenate(widths, axis=1).reshape(n_qp * share)[:group]
    collision = jnp.transpose(jnp.concatenate(parts, axis=2), (0, 2, 1, 3))
    collision = collision.reshape(n_qp * share, own_pairs, modes)[:group]
    return (widths, collision)


def solution(mesh):
    placed = (
        P("grp", None),
        P("grp"),
        P("qp", None, None),
        P("qp", None),
        P(None, ("mode", "fc")),
        P(("grp", "qp")),
        P(("grp", "qp")),
    )
    return jax.shard_map(
        local,
        mesh=mesh,
        in_specs=placed,
        out_specs=(P(("grp", "mode", "fc")), P(("mode", "fc"), ("grp", "qp"), None)),
        check_vma=False,
    )
```

```python
import functools
import math

import jax
import jax.numpy as jnp
from jax import lax
from jax.experimental import pallas as pl
from jax.experimental.pallas import tpu as pltpu
from jax.sharding import PartitionSpec as P

thermal_reservoir_kelvin = 1.0
smearing = 0.25

MAIN = 256
TILE = 128
F32 = jnp.float32
BF16 = jnp.bfloat16


def ceil_div(a, b):
    return -(-a // b)


VMEM_BYTES = 56 << 20


def occupy(energy):
    return 1.0 / (jnp.exp(energy / thermal_reservoir_kelvin) - 1.0)


def dot_nn(a, b):
    return lax.dot_general(a, b, (((1,), (0,)), ((), ())), preferred_element_type=F32)


def dot_nt(a, b):
    return lax.dot_general(a, b, (((1,), (1,)), ((), ())), preferred_element_type=F32)


def slots_of(count, modes):
    return count + ceil_div(count, MAIN // (modes - MAIN))


STREAMS = 3


def project_kernel(groups, group, share, first, count, here_ref, home_ref, *refs):
    force_refs, (out_ref, rows_ref, main_ref, rest_ref) = refs[:STREAMS], refs[STREAMS:]
    modes = home_ref.shape[0]
    lines = groups * count
    rest = modes - MAIN
    per_slot = MAIN // rest
    depth = out_ref.shape[2]
    step = pl.program_id(0)
    here = force_refs[0].shape[1] // modes
    pitch = lines + 1

    @pl.when(step == 0)
    def _():
        line = lax.broadcasted_iota(jnp.int32, (lines, modes), 0)
        column = lax.broadcasted_iota(jnp.int32, (lines, modes), 1)
        own = here_ref[0] * share + first + line % count
        wanted = (line // count) * group + own
        select = jnp.logical_and(column == wanted, own < group).astype(BF16)
        rows_ref[...] = dot_nt(select, home_ref[...]).astype(BF16)

    force = jnp.concatenate([ref[...] for ref in force_refs], axis=0)
    result = dot_nn(rows_ref[...], force)
    for c in range(here):
        row = (step * here + c) * pitch
        piece = result[:, c * modes : (c + 1) * modes]
        main_ref[0, pl.ds(row, lines), :] = piece[:, :TILE]
        main_ref[1, pl.ds(row, lines), :] = piece[:, TILE:MAIN]
        rest_ref[pl.ds(row, lines), :] = jnp.concatenate(
            [piece[:, MAIN:], jnp.zeros((lines, TILE - rest), F32)], axis=1
        )

    @pl.when(step == pl.num_programs(0) - 1)
    def _():
        lane = lax.broadcasted_iota(jnp.int32, (depth, TILE), 1)
        for t in range(groups):
            base = t * count
            for r in range(count):
                for h in range(2):
                    out_ref[t, r, :, h * TILE : (h + 1) * TILE] = main_ref[
                        h, pl.ds(base + r, depth, stride=pitch), :
                    ].astype(BF16)
            for g in range(ceil_div(count, per_slot)):
                for h in range(2):
                    packed = jnp.zeros((depth, TILE), F32)
                    for b in range(per_slot // 2):
                        r = g * per_slot + h * (per_slot // 2) + b
                        if r < count:
                            piece = rest_ref[pl.ds(base + r, depth, stride=pitch), :]
                            if b > 0:
                                piece = pltpu.roll(piece, b * rest, 1)
                            packed = jnp.where(lane // rest == b, piece, packed)
                    out_ref[t, count + g, :, h * TILE : (h + 1) * TILE] = packed.astype(BF16)


def project(here, home_vectors, force_table, groups, group, share, first, count):
    modes = home_vectors.shape[0]
    lines = groups * count
    depth = force_table.shape[1] // modes
    per_step = 8 if depth % 8 == 0 else 4
    rows = modes // STREAMS
    shape = (groups, slots_of(count, modes), depth, MAIN)

    def stream(k):
        return pl.BlockSpec((rows, per_step * modes), lambda i: (k, i))

    return pl.pallas_call(
        functools.partial(project_kernel, groups, group, share, first, count),
        grid=(depth // per_step,),
        in_specs=[
            pl.BlockSpec(memory_space=pltpu.SMEM),
            pl.BlockSpec((modes, modes), lambda i: (0, 0)),
        ]
        + [stream(k) for k in range(STREAMS)],
        out_specs=pl.BlockSpec(shape, lambda i: (0, 0, 0, 0)),
        out_shape=jax.ShapeDtypeStruct(shape, BF16),
        scratch_shapes=[
            pltpu.VMEM((lines, modes), BF16),
            pltpu.VMEM((2, (depth + 1) * (lines + 1), TILE), F32),
            pltpu.VMEM(((depth + 1) * (lines + 1), TILE), F32),
        ],
        compiler_params=pltpu.CompilerParams(vmem_limit_bytes=VMEM_BYTES),
        cost_estimate=pl.CostEstimate(
            flops=2 * lines * modes * modes * depth,
            bytes_accessed=2 * modes * modes * depth,
            transcendentals=0,
        ),
        name="project",
    )(here, home_vectors, *[force_table] * STREAMS)


def identity(size):
    return (
        lax.broadcasted_iota(jnp.int32, (size, size), 0)
        == lax.broadcasted_iota(jnp.int32, (size, size), 1)
    ).astype(BF16)


def pack_kernel(part_ref, partner_ref, weight_ref, grid_ref, freq_ref, out_ref):
    own_pairs, modes, _ = grid_ref.shape
    rest = modes - MAIN
    lines = rest // 2
    part = part_ref[0]
    line = lax.broadcasted_iota(jnp.int32, (lines, modes), 0)
    column = lax.broadcasted_iota(jnp.int32, (lines, modes), 1)
    select = (column == MAIN + part * lines + line).astype(BF16)
    freqs = freq_ref[...].astype(F32)
    blank = jnp.zeros((own_pairs, TILE - rest), F32)
    freq_tiles = (
        freqs[:, :TILE],
        freqs[:, TILE:MAIN],
        jnp.concatenate([freqs[:, MAIN:], blank], axis=1),
    )
    line16 = lax.broadcasted_iota(jnp.int32, (16, TILE), 0)
    lane16 = lax.broadcasted_iota(jnp.int32, (16, TILE), 1)
    for s in range(own_pairs):
        for p in range(2):

            @pl.when(part == p)
            def _():
                out_ref[s, :modes, :] = grid_ref[s, :, p * TILE : (p + 1) * TILE]

        turned = dot_nt(select, grid_ref[s])
        turned = (
            turned[:, :TILE],
            turned[:, TILE:MAIN],
            jnp.concatenate([turned[:, MAIN:], jnp.zeros((lines, TILE - rest), F32)], axis=1),
        )
        for h in range(3):
            start = modes + h * lines
            out_ref[s, start : start + lines, :] = turned[h].astype(BF16)
        pair = partner_ref[s].astype(F32)
        weight = weight_ref[s].astype(F32)
        side = jnp.where(lane16 == 0, pair, jnp.where(lane16 == 1, weight, 0.0))
        side = jnp.where(line16 == 3, side, 0.0)
        for h in range(3):
            side = jnp.where(line16 == h, freq_tiles[h][s : s + 1], side)
        start = modes + 3 * lines
        out_ref[s, start : start + 16, :] = side.astype(BF16)


def pack_own(part, partner, weights, grid_vectors, partner_frequencies):
    own_pairs, modes, _ = grid_vectors.shape
    smem = pl.BlockSpec(memory_space=pltpu.SMEM)
    vmem = pl.BlockSpec(memory_space=pltpu.VMEM)
    rows = modes + 3 * (modes - MAIN) // 2 + 16
    return pl.pallas_call(
        pack_kernel,
        in_specs=[smem, smem, smem, vmem, vmem],
        out_specs=vmem,
        out_shape=jax.ShapeDtypeStruct((own_pairs, rows, TILE), BF16),
        compiler_params=pltpu.CompilerParams(vmem_limit_bytes=VMEM_BYTES),
        name="pack_own",
    )(part, partner, weights, grid_vectors, partner_frequencies)


def arrange_kernel(
    pack_ref, partner_ref, weight_ref, grid_ref, grid_t_ref, freq_row_ref, freq_col_ref
):
    owners, parts, each, rows, _ = pack_ref.shape
    modes = grid_ref.shape[1]
    rest = modes - MAIN
    lines = rest // parts
    eye = identity(MAIN)
    source = lax.broadcasted_iota(jnp.int32, (TILE, TILE), 0)
    place = lax.broadcasted_iota(jnp.int32, (TILE, TILE), 1)
    spread = (source == place % rest).astype(BF16)
    eye_tile = (source == place).astype(BF16)
    lane = lax.broadcasted_iota(jnp.int32, (TILE, freq_col_ref.shape[1]), 1)
    line16 = lax.broadcasted_iota(jnp.int32, (16, TILE), 0)
    lane16 = lax.broadcasted_iota(jnp.int32, (16, TILE), 1)
    freq_col_ref[...] = jnp.zeros_like(freq_col_ref)

    def one(q, carry):
        for s in range(each):
            x = q * each + s
            for part in range(parts):
                grid_ref[x, :, part * TILE : (part + 1) * TILE] = pack_ref[q, part, s, :modes, :]
                for h in range(3):
                    start = modes + h * lines
                    grid_t_ref[
                        x,
                        MAIN + part * lines : MAIN + (part + 1) * lines,
                        h * TILE : (h + 1) * TILE,
                    ] = pack_ref[q, part, s, start : start + lines, :]
            grid_t_ref[x, :MAIN, MAIN:] = jnp.zeros((MAIN, TILE), BF16)
            grid_t_ref[x, :MAIN, :modes] = dot_nt(eye, grid_ref[x]).astype(BF16)
            side = pack_ref[q, 0, s, modes + 3 * lines : modes + 3 * lines + 16, :]
            wide = side.astype(F32)
            freq_row_ref[x, :, :TILE] = wide[0:1]
            freq_row_ref[x, :, TILE:MAIN] = wide[1:2]
            freq_row_ref[x, :, MAIN:] = dot_nn(side, spread)[2:3]
            columns = dot_nt(eye_tile, side)
            for h in range(3):
                width = min(TILE, modes - h * TILE)
                here = slice(h * TILE, h * TILE + width)
                freq_col_ref[here, :] = jnp.where(
                    lane[:width] == x, columns[:width, h : h + 1], freq_col_ref[here, :]
                )
            for spot, ref in ((0, partner_ref), (1, weight_ref)):
                found = jnp.sum(
                    jnp.where(jnp.logical_and(line16 == 3, lane16 == spot), wide, 0.0)
                )
                ref[x] = found.astype(ref.dtype)
        return carry

    lax.fori_loop(0, owners, one, 0, unroll=owners <= 4)


def arrange(pack, modes):
    owners, parts, each, _, _ = pack.shape
    pairs = owners * each
    smem = pl.BlockSpec(memory_space=pltpu.SMEM)
    vmem = pl.BlockSpec(memory_space=pltpu.VMEM)
    return pl.pallas_call(
        arrange_kernel,
        in_specs=[vmem],
        out_specs=[smem, smem, vmem, vmem, vmem, vmem],
        out_shape=[
            jax.ShapeDtypeStruct((pairs,), jnp.int32),
            jax.ShapeDtypeStruct((pairs,), F32),
            jax.ShapeDtypeStruct((pairs, modes, MAIN), BF16),
            jax.ShapeDtypeStruct((pairs, modes, MAIN + TILE), BF16),
            jax.ShapeDtypeStruct((pairs, 1, MAIN + TILE), F32),
            jax.ShapeDtypeStruct((modes, TILE), F32),
        ],
        compiler_params=pltpu.CompilerParams(vmem_limit_bytes=VMEM_BYTES),
        name="arrange",
    )(pack)


def interleave(heavy, light):
    done = 0
    for i, task in enumerate(heavy):
        task()
        upto = (i + 1) * len(light) // len(heavy)
        while done < upto:
            light[done]()
            done += 1
    while done < len(light):
        light[done]()
        done += 1


def coupling_kernel(
    share,
    block,
    partner_ref,
    weight_ref,
    home_ref,
    grid_ref,
    grid_t_ref,
    freq_row_ref,
    freq_col_ref,
    home_row_ref,
    moved_ref,
    out_ref,
    turned_ref,
    grid_rest_ref,
    inner_rest_ref,
    pick_ref,
    rest_value_ref,
    force_rest_ref,
    *work,
):
    gathers, inners, lefts, wides, values, tabs, sums, rest_sums, firsts = (
        work[2 * i : 2 * i + 2] for i in range(9)
    )
    pairs = grid_ref.shape[0]
    modes = grid_ref.shape[1]
    rest = modes - MAIN
    sources, depth = moved_ref.shape[0], moved_ref.shape[2]
    per_slot = MAIN // rest
    per_tile = TILE // rest
    rest_lanes = home_row_ref.shape[1]
    s2 = smearing * smearing
    steps = share // block

    for x in range(pairs):
        grid_rest_ref[x * rest : (x + 1) * rest, :] = grid_t_ref[x, MAIN:, :modes]
    eye = identity(modes)
    force_rest_ref[...] = jnp.zeros_like(force_rest_ref)
    if share * rest < rest_lanes:
        inner_rest_ref[...] = jnp.zeros_like(inner_rest_ref)
    for r in range(share):
        slot, spot = share + r // per_slot, r % per_slot
        half, spot = spot // (per_slot // 2), spot % (per_slot // 2)
        gather_ref = gathers[r % 2]
        for s in range(sources):
            gather_ref[s * depth : (s + 1) * depth, :MAIN] = moved_ref[s, r].astype(F32)
            tail = moved_ref[s, slot, :, half * TILE : (half + 1) * TILE].astype(F32)
            if spot > 0:
                tail = pltpu.roll(tail, TILE - spot * rest, 1)
            gather_ref[s * depth : (s + 1) * depth, MAIN:] = tail[:, :rest]
        whole = gather_ref[...].astype(BF16)
        turned_ref[r * modes : (r + 1) * modes, :] = dot_nt(eye, whole[:MAIN]).astype(BF16)
        line = (r // block * per_tile + r % block) * rest
        force_rest_ref[line : line + rest, :] = whole[MAIN:]
        found = dot_nn(grid_rest_ref[...], whole).astype(BF16)
        for x in range(pairs):
            inner_rest_ref[x, r * rest : (r + 1) * rest, :] = found[x * rest : (x + 1) * rest, :]

    row_id = lax.broadcasted_iota(jnp.int32, pick_ref.shape, 0)
    col_id = lax.broadcasted_iota(jnp.int32, pick_ref.shape, 1)
    branch = jnp.where(
        row_id < share * TILE, row_id // TILE, (row_id - share * TILE) // rest
    )
    pick_ref[...] = (branch == col_id).astype(BF16)
    for ref in (out_ref, *inners, *sums, *rest_sums, *firsts):
        ref[...] = jnp.zeros_like(ref)

    def contract_wide(x, into):
        def task():
            left = grid_t_ref[partner_ref[x], :, :modes]
            into[...] = dot_nt(left, force_rest_ref[...]).astype(BF16)

        return task

    def contract_first(x, r, b, into):
        def task():
            lanes = slice(b * MAIN, (b + 1) * MAIN)
            found = dot_nn(turned_ref[r * modes : (r + 1) * modes, :], grid_ref[x, :MAIN, :])
            into[:modes, lanes] = found.astype(BF16)
            start = MAIN + TILE + b * rest
            into[start : start + rest, lanes] = grid_ref[x, MAIN:, :]

        return task

    def prepare_second(x, step, wide, left):
        def task():
            left[:, : MAIN + TILE] = grid_t_ref[partner_ref[x]]
            left[:, MAIN + TILE :] = wide[:, step * TILE : (step + 1) * TILE]

        return task

    def contract_second(b, left, source, into):
        lanes = slice(b * MAIN, (b + 1) * MAIN)

        def task():
            into[:, lanes] = dot_nn(left[...], source[:, lanes])

        return task

    def line_shapes(v, t, w, c1, c2):
        p = v * v
        d = t[0] - w
        e = t[1] - c1
        return (
            (p * t[2]) * pl.reciprocal(d * d + s2, approx=True),
            (p * t[3]) * pl.reciprocal(e * e + c2, approx=True),
        )

    def weigh(step, source, tab, sum_ref, first_ref):
        state = {}

        def begin():
            state["w"] = [home_ref[step * block + b] for b in range(block)]
            state["c1"] = [w * w - s2 for w in state["w"]]
            state["c2"] = [(4.0 * s2) * (w * w) for w in state["w"]]
            state["total"] = [jnp.zeros((8, MAIN), F32) for _ in range(block)]

        def rows(n):
            def task():
                if n == 0:
                    begin()
                t = [tab[k, n : n + 16, :MAIN] for k in range(4)]
                for b in range(block):
                    v = source[n : n + 16, b * MAIN : (b + 1) * MAIN]
                    f, u = line_shapes(v, t, state["w"][b], state["c1"][b], state["c2"][b])
                    state["total"][b] = state["total"][b] + (f[:8] + f[8:])
                    r = step * block + b
                    sum_ref[n : n + 16, r * TILE : (r + 1) * TILE] = (
                        u[:, :TILE] + u[:, TILE:]
                    ).astype(BF16)
                if n + 16 == modes:
                    for b in range(block):
                        r = step * block + b
                        line = jnp.sum(state["total"][b], axis=0, keepdims=True)
                        first_ref[r : r + 1, :MAIN] = line * (1.0 / state["w"][b])

            return task

        return [rows(n) for n in range(0, modes, 16)]

    def contract_rest(x):
        def task():
            rest_value_ref[...] = dot_nt(
                grid_t_ref[partner_ref[x], :, :modes], inner_rest_ref[x]
            )

        return task

    def weigh_rest(tab, sum_ref, first_ref):
        def tile(start):
            lanes = slice(start, start + TILE)
            state = {}

            def rows(n):
                def task():
                    if n == 0:
                        state["total"] = jnp.zeros((8, TILE), F32)
                        state["w"] = home_row_ref[0:1, lanes]
                        state["c1"] = home_row_ref[1:2, lanes]
                        state["c2"] = home_row_ref[2:3, lanes]
                    for k in range(n, n + 48, 16):
                        t = [tab[i, k : k + 16, MAIN:] for i in range(4)]
                        f, u = line_shapes(
                            rest_value_ref[k : k + 16, lanes], t, state["w"], state["c1"], state["c2"]
                        )
                        state["total"] = state["total"] + (f[:8] + f[8:])
                        sum_ref[k : k + 16, lanes] = u.astype(BF16)
                    if n + 48 == modes:
                        line = jnp.sum(state["total"], axis=0, keepdims=True)
                        line = line * home_row_ref[3:4, lanes]
                        for b in range(TILE // rest):
                            r = start // rest + b
                            if r < share:
                                first_ref[r : r + 1, MAIN:] = line[:, b * rest : (b + 1) * rest]

                return task

            return [rows(n) for n in range(0, modes, 48)]

        return [task for start in range(0, rest_lanes, TILE) for task in tile(start)]

    def tables(x, tab):
        state = {}

        def begin():
            w1 = freq_row_ref[x]
            spots = lax.broadcasted_iota(jnp.int32, freq_col_ref.shape, 1)
            w2 = jnp.sum(
                jnp.where(spots == partner_ref[x], freq_col_ref[...], 0.0), axis=1, keepdims=True
            )
            state["w"] = (w1, w2)
            state["o"] = (occupy(w1), occupy(w2))
            scale = weight_ref[x] * (smearing / math.pi / modes)
            state["i"] = (scale / w1, 1.0 / w2)

        def rows(n):
            def task():
                if n == 0:
                    begin()
                part = slice(n, n + 48)
                (w1, w2), (o1, o2), (i1, i2) = state["w"], state["o"], state["i"]
                w2, o2, i2 = w2[part], o2[part], i2[part]
                a = w1 - w2
                both = i1 * i2
                tab[0, part, :] = w1 + w2
                tab[1, part, :] = a * a
                tab[2, part, :] = (1.0 + o1 + o2) * both
                tab[3, part, :] = (4.0 * a) * (o2 - o1) * both

            return task

        return [rows(n) for n in range(0, modes, 48)]

    def collect(sum_ref, rest_sum_ref, state):
        def task():
            second = dot_nn(sum_ref[...], pick_ref[: share * TILE, :])
            second += dot_nn(rest_sum_ref[...], pick_ref[share * TILE :, :])
            state["second"] = second.T[:share, :]

        return task

    def deliver(x, target, state, first_ref):
        out_ref[x, :share, :] += first_ref[:share, :]
        out_ref[target, :share, :] += state["second"]

    for task in tables(0, tabs[0]):
        task()
    for g in range(2):
        for b in range(block):
            x, step = jnp.int32(g // steps), g % steps
            contract_first(x, step * block + b, b, inners[g])()
    contract_wide(jnp.int32(0), wides[0])()
    prepare_second(jnp.int32(0), 0, wides[0], lefts[0])()
    for b in range(block):
        contract_second(b, lefts[0], inners[0], values[0])()

    def two_pairs(i, carry):
        for e in range(2):
            x = i * 2 + e

            def later(g):
                return jnp.minimum(i * 2 + g // steps, pairs - 1), g % steps

            before = jnp.maximum(x - 1, 0)
            target = partner_ref[before]
            extra = weigh_rest(tabs[e], rest_sums[e], firsts[e])
            extra = extra + tables(jnp.minimum(x + 1, pairs - 1), tabs[1 - e])
            contract_rest(x)()
            done = {}
            for s in range(steps):
                g = e * steps + s
                heavy = []
                if s == 0:
                    contract_wide(jnp.minimum(x + 1, pairs - 1), wides[1 - e])()
                x1, step1 = later(g + 1)
                odd = (g + 1) % 2
                prepare_second(x1, step1, wides[(g + 1) // steps % 2], lefts[odd])()
                for b in range(block):
                    heavy.append(contract_second(b, lefts[odd], inners[odd], values[odd]))
                for b in range(block):
                    x2, step2 = later(g + 2)
                    heavy.append(contract_first(x2, step2 * block + b, b, inners[g % 2]))
                light = weigh(s, values[g % 2], tabs[e], sums[e], firsts[e])
                light = light + extra[s * len(extra) // steps : (s + 1) * len(extra) // steps]
                if s == 0:
                    heavy.insert(1, collect(sums[1 - e], rest_sums[1 - e], done))
                interleave(heavy, light)
            deliver(before, target, done, firsts[1 - e])
        return carry

    lax.fori_loop(0, pairs // 2, two_pairs, 0)
    last = {}
    collect(sums[1], rest_sums[1], last)()
    deliver(pairs - 1, partner_ref[pairs - 1], last, firsts[1])

    totals = jnp.zeros(out_ref.shape[1:], F32)
    for y in range(pairs):
        totals = totals + out_ref[y]
    widths = jnp.sum(totals, axis=1, keepdims=True) * (1.0 / (pairs * modes))
    spread = jnp.where(
        lax.broadcasted_iota(jnp.int32, totals.shape, 0)
        == lax.broadcasted_iota(jnp.int32, totals.shape, 1),
        widths,
        0.0,
    )
    out_ref[:, share, :] = jnp.broadcast_to(
        jnp.sum(spread, axis=0, keepdims=True), (pairs, modes)
    )


def coupling(partner, weights, home, grid, grid_t, freq_rows, freq_cols, moved):
    pairs, modes = grid.shape[0], grid.shape[1]
    share = home.shape[0]
    rest = modes - MAIN
    rest_lanes = ceil_div(share * rest, TILE) * TILE
    row = jnp.repeat(home, rest)
    row = jnp.pad(row, (0, rest_lanes - share * rest), constant_values=1.0)
    s2 = smearing * smearing
    home_row = jnp.stack([row, row * row - s2, (4.0 * s2) * (row * row), 1.0 / row])
    padded = (share // 8 + 1) * 8
    smem = pl.BlockSpec(memory_space=pltpu.SMEM)
    vmem = pl.BlockSpec(memory_space=pltpu.VMEM)
    block = 3 if share % 3 == 0 else 1
    assert pairs % 2 == 0
    scratch = (
        [
            pltpu.VMEM((share * modes, MAIN), BF16),
            pltpu.VMEM((pairs * rest, modes), BF16),
            pltpu.VMEM((pairs, rest_lanes, modes), BF16),
            pltpu.VMEM((share * TILE + rest_lanes, TILE), BF16),
            pltpu.VMEM((modes, rest_lanes), F32),
            pltpu.VMEM((share // block * TILE, modes), BF16),
        ]
        + [pltpu.VMEM((modes, modes), F32)] * 2
        + [pltpu.VMEM((2 * MAIN, block * MAIN), BF16)] * 2
        + [pltpu.VMEM((modes, 2 * MAIN), BF16)] * 2
        + [pltpu.VMEM((modes, share // block * TILE), BF16)] * 2
        + [pltpu.VMEM((modes, block * MAIN), F32)] * 2
        + [pltpu.VMEM((4, modes, MAIN + TILE), F32)] * 2
        + [pltpu.VMEM((modes, share * TILE), BF16)] * 2
        + [pltpu.VMEM((modes, rest_lanes), BF16)] * 2
        + [pltpu.VMEM((padded, modes), F32)] * 2
    )
    return pl.pallas_call(
        functools.partial(coupling_kernel, share, block),
        in_specs=[smem, smem, smem, vmem, vmem, vmem, vmem, vmem, vmem],
        out_specs=vmem,
        out_shape=jax.ShapeDtypeStruct((pairs, padded, modes), F32),
        scratch_shapes=scratch,
        compiler_params=pltpu.CompilerParams(vmem_limit_bytes=VMEM_BYTES),
        cost_estimate=pl.CostEstimate(
            flops=4 * share * pairs * modes**3,
            bytes_accessed=8 * share * modes * modes,
            transcendentals=2 * share * pairs * modes**2,
        ),
        name="coupling",
    )(partner, weights, home, grid, grid_t, freq_rows, freq_cols, home_row, moved)


def local(
    home_vectors, home_freqs, grid_vectors, partner_frequencies, force_table, partner, weights
):
    own_pairs = partner.shape[0]
    modes = home_vectors.shape[0]
    n_mode = lax.axis_size("mode")
    n_fc = lax.axis_size("fc")
    n_qp = lax.axis_size("qp")
    groups = n_mode * n_fc
    group = modes // groups
    pairs = own_pairs * n_qp
    share = ceil_div(group, n_qp)
    here = lax.axis_index("qp")
    if share % 6 == 0 and share > 6:
        chunks = ((0, 6), (6, share - 6))
    else:
        chunks = ((0, share),)

    assert n_fc * TILE == MAIN
    own_part = lax.axis_index("fc").astype(jnp.int32)[None]
    pack = pack_own(own_part, partner, weights, grid_vectors, partner_frequencies)
    pack = lax.all_gather(pack, ("qp", "fc"), axis=0)
    pack = pack.reshape(n_qp, n_fc, own_pairs, pack.shape[2], TILE)

    here_word = here.astype(jnp.int32)[None]
    moved = []
    for first, count in chunks:
        sent = project(here_word, home_vectors, force_table, groups, group, share, first, count)
        moved.append(
            lax.all_to_all(sent, ("mode", "fc"), split_axis=0, concat_axis=0, tiled=True)
        )

    own = lax.axis_index(("mode", "fc"))
    home = home_freqs.astype(F32).reshape(groups, group)
    home = jnp.pad(home, ((0, 0), (0, share * n_qp - group)), constant_values=1.0)
    home = lax.dynamic_slice(home, (own, here * share), (1, share)).reshape(share)

    shared = arrange(pack, modes)
    parts, widths = [], []
    for (first, count), block in zip(chunks, moved):
        found = coupling(
            shared[0], shared[1], home[first : first + count], *shared[2:], block
        )
        back = lax.all_to_all(
            found.reshape(n_qp, own_pairs, found.shape[1], modes),
            "qp",
            split_axis=0,
            concat_axis=0,
            tiled=True,
        )
        widths.append(back[:, 0, count, :count])
        parts.append(back[:, :, :count, :])
    widths = jnp.concatenate(widths, axis=1).reshape(n_qp * share)[:group]
    collision = jnp.transpose(jnp.concatenate(parts, axis=2), (0, 2, 1, 3))
    collision = collision.reshape(n_qp * share, own_pairs, modes)[:group]
    return (widths, collision)


def solution(mesh):
    placed = (
        P("grp", None),
        P("grp"),
        P("qp", None, None),
        P("qp", None),
        P(None, ("mode", "fc")),
        P(("grp", "qp")),
        P(("grp", "qp")),
    )
    return jax.shard_map(
        local,
        mesh=mesh,
        in_specs=placed,
        out_specs=(P(("grp", "mode", "fc")), P(("mode", "fc"), ("grp", "qp"), None)),
        check_vma=False,
    )
```

```python
import functools
import math

import jax
import jax.numpy as jnp
from jax import lax
from jax.experimental import pallas as pl
from jax.experimental.pallas import tpu as pltpu
from jax.sharding import PartitionSpec as P

thermal_reservoir_kelvin = 1.0
smearing = 0.25

MAIN = 256
TILE = 128
F32 = jnp.float32
BF16 = jnp.bfloat16


def ceil_div(a, b):
    return -(-a // b)


VMEM_BYTES = 56 << 20


def occupy(energy):
    return 1.0 / (jnp.exp(energy / thermal_reservoir_kelvin) - 1.0)


def dot_nn(a, b):
    return lax.dot_general(a, b, (((1,), (0,)), ((), ())), preferred_element_type=F32)


def dot_nt(a, b):
    return lax.dot_general(a, b, (((1,), (1,)), ((), ())), preferred_element_type=F32)


def slots_of(count, modes):
    return count + ceil_div(count, MAIN // (modes - MAIN))


STREAMS = 3


def project_kernel(groups, group, share, first, count, here_ref, home_ref, *refs):
    force_refs, (out_ref, rows_ref, main_ref, rest_ref) = refs[:STREAMS], refs[STREAMS:]
    modes = home_ref.shape[0]
    lines = groups * count
    rest = modes - MAIN
    per_slot = MAIN // rest
    depth = out_ref.shape[2]
    step = pl.program_id(0)
    here = force_refs[0].shape[1] // modes
    pitch = lines + 1

    @pl.when(step == 0)
    def _():
        line = lax.broadcasted_iota(jnp.int32, (lines, modes), 0)
        column = lax.broadcasted_iota(jnp.int32, (lines, modes), 1)
        own = here_ref[0] * share + first + line % count
        wanted = (line // count) * group + own
        select = jnp.logical_and(column == wanted, own < group).astype(BF16)
        rows_ref[...] = dot_nt(select, home_ref[...]).astype(BF16)

    force = jnp.concatenate([ref[...] for ref in force_refs], axis=0)
    result = dot_nn(rows_ref[...], force)
    for c in range(here):
        row = (step * here + c) * pitch
        piece = result[:, c * modes : (c + 1) * modes]
        main_ref[0, pl.ds(row, lines), :] = piece[:, :TILE]
        main_ref[1, pl.ds(row, lines), :] = piece[:, TILE:MAIN]
        rest_ref[pl.ds(row, lines), :] = jnp.concatenate(
            [piece[:, MAIN:], jnp.zeros((lines, TILE - rest), F32)], axis=1
        )

    @pl.when(step == pl.num_programs(0) - 1)
    def _():
        lane = lax.broadcasted_iota(jnp.int32, (depth, TILE), 1)
        for t in range(groups):
            base = t * count
            for r in range(count):
                for h in range(2):
                    out_ref[t, r, :, h * TILE : (h + 1) * TILE] = main_ref[
                        h, pl.ds(base + r, depth, stride=pitch), :
                    ].astype(BF16)
            for g in range(ceil_div(count, per_slot)):
                for h in range(2):
                    packed = jnp.zeros((depth, TILE), F32)
                    for b in range(per_slot // 2):
                        r = g * per_slot + h * (per_slot // 2) + b
                        if r < count:
                            piece = rest_ref[pl.ds(base + r, depth, stride=pitch), :]
                            if b > 0:
                                piece = pltpu.roll(piece, b * rest, 1)
                            packed = jnp.where(lane // rest == b, piece, packed)
                    out_ref[t, count + g, :, h * TILE : (h + 1) * TILE] = packed.astype(BF16)


def project(here, home_vectors, force_table, groups, group, share, first, count):
    modes = home_vectors.shape[0]
    lines = groups * count
    depth = force_table.shape[1] // modes
    per_step = 8 if depth % 8 == 0 else 4
    rows = modes // STREAMS
    shape = (groups, slots_of(count, modes), depth, MAIN)

    def stream(k):
        return pl.BlockSpec((rows, per_step * modes), lambda i: (k, i))

    return pl.pallas_call(
        functools.partial(project_kernel, groups, group, share, first, count),
        grid=(depth // per_step,),
        in_specs=[
            pl.BlockSpec(memory_space=pltpu.SMEM),
            pl.BlockSpec((modes, modes), lambda i: (0, 0)),
        ]
        + [stream(k) for k in range(STREAMS)],
        out_specs=pl.BlockSpec(shape, lambda i: (0, 0, 0, 0)),
        out_shape=jax.ShapeDtypeStruct(shape, BF16),
        scratch_shapes=[
            pltpu.VMEM((lines, modes), BF16),
            pltpu.VMEM((2, (depth + 1) * (lines + 1), TILE), F32),
            pltpu.VMEM(((depth + 1) * (lines + 1), TILE), F32),
        ],
        compiler_params=pltpu.CompilerParams(vmem_limit_bytes=VMEM_BYTES),
        cost_estimate=pl.CostEstimate(
            flops=2 * lines * modes * modes * depth,
            bytes_accessed=2 * modes * modes * depth,
            transcendentals=0,
        ),
        name="project",
    )(here, home_vectors, *[force_table] * STREAMS)


def identity(size):
    return (
        lax.broadcasted_iota(jnp.int32, (size, size), 0)
        == lax.broadcasted_iota(jnp.int32, (size, size), 1)
    ).astype(BF16)


def pack_kernel(part_ref, partner_ref, weight_ref, grid_ref, freq_ref, out_ref):
    own_pairs, modes, _ = grid_ref.shape
    rest = modes - MAIN
    lines = rest // 2
    part = part_ref[0]
    line = lax.broadcasted_iota(jnp.int32, (lines, modes), 0)
    column = lax.broadcasted_iota(jnp.int32, (lines, modes), 1)
    select = (column == MAIN + part * lines + line).astype(BF16)
    freqs = freq_ref[...].astype(F32)
    blank = jnp.zeros((own_pairs, TILE - rest), F32)
    freq_tiles = (
        freqs[:, :TILE],
        freqs[:, TILE:MAIN],
        jnp.concatenate([freqs[:, MAIN:], blank], axis=1),
    )
    line16 = lax.broadcasted_iota(jnp.int32, (16, TILE), 0)
    lane16 = lax.broadcasted_iota(jnp.int32, (16, TILE), 1)
    for s in range(own_pairs):
        for p in range(2):

            @pl.when(part == p)
            def _():
                out_ref[s, :modes, :] = grid_ref[s, :, p * TILE : (p + 1) * TILE]

        turned = dot_nt(select, grid_ref[s])
        turned = (
            turned[:, :TILE],
            turned[:, TILE:MAIN],
            jnp.concatenate([turned[:, MAIN:], jnp.zeros((lines, TILE - rest), F32)], axis=1),
        )
        for h in range(3):
            start = modes + h * lines
            out_ref[s, start : start + lines, :] = turned[h].astype(BF16)
        pair = partner_ref[s].astype(F32)
        weight = weight_ref[s].astype(F32)
        side = jnp.where(lane16 == 0, pair, jnp.where(lane16 == 1, weight, 0.0))
        side = jnp.where(line16 == 3, side, 0.0)
        for h in range(3):
            side = jnp.where(line16 == h, freq_tiles[h][s : s + 1], side)
        start = modes + 3 * lines
        out_ref[s, start : start + 16, :] = side.astype(BF16)


def pack_own(part, partner, weights, grid_vectors, partner_frequencies):
    own_pairs, modes, _ = grid_vectors.shape
    smem = pl.BlockSpec(memory_space=pltpu.SMEM)
    vmem = pl.BlockSpec(memory_space=pltpu.VMEM)
    rows = modes + 3 * (modes - MAIN) // 2 + 16
    return pl.pallas_call(
        pack_kernel,
        in_specs=[smem, smem, smem, vmem, vmem],
        out_specs=vmem,
        out_shape=jax.ShapeDtypeStruct((own_pairs, rows, TILE), BF16),
        compiler_params=pltpu.CompilerParams(vmem_limit_bytes=VMEM_BYTES),
        name="pack_own",
    )(part, partner, weights, grid_vectors, partner_frequencies)


def arrange_kernel(
    pack_ref, partner_ref, weight_ref, grid_ref, grid_t_ref, freq_row_ref, freq_col_ref
):
    owners, parts, each, rows, _ = pack_ref.shape
    modes = grid_ref.shape[1]
    rest = modes - MAIN
    lines = rest // parts
    eye = identity(MAIN)
    source = lax.broadcasted_iota(jnp.int32, (TILE, TILE), 0)
    place = lax.broadcasted_iota(jnp.int32, (TILE, TILE), 1)
    spread = (source == place % rest).astype(BF16)
    eye_tile = (source == place).astype(BF16)
    lane = lax.broadcasted_iota(jnp.int32, (TILE, freq_col_ref.shape[1]), 1)
    line16 = lax.broadcasted_iota(jnp.int32, (16, TILE), 0)
    lane16 = lax.broadcasted_iota(jnp.int32, (16, TILE), 1)
    freq_col_ref[...] = jnp.zeros_like(freq_col_ref)

    def one(q, carry):
        for s in range(each):
            x = q * each + s
            for part in range(parts):
                grid_ref[x, :, part * TILE : (part + 1) * TILE] = pack_ref[q, part, s, :modes, :]
                for h in range(3):
                    start, width = modes + h * lines, min(TILE, modes - h * TILE)
                    piece = pack_ref[q, part, s, start : start + lines, :]
                    grid_t_ref[
                        x, MAIN + part * lines : MAIN + (part + 1) * lines, h * TILE : h * TILE + width
                    ] = piece[:, :width]
            grid_t_ref[x, :MAIN, :] = dot_nt(eye, grid_ref[x]).astype(BF16)
            side = pack_ref[q, 0, s, modes + 3 * lines : modes + 3 * lines + 16, :]
            wide = side.astype(F32)
            freq_row_ref[x, :, :TILE] = wide[0:1]
            freq_row_ref[x, :, TILE:MAIN] = wide[1:2]
            freq_row_ref[x, :, MAIN:] = dot_nn(side, spread)[2:3]
            columns = dot_nt(eye_tile, side)
            for h in range(3):
                width = min(TILE, modes - h * TILE)
                here = slice(h * TILE, h * TILE + width)
                freq_col_ref[here, :] = jnp.where(
                    lane[:width] == x, columns[:width, h : h + 1], freq_col_ref[here, :]
                )
            for spot, ref in ((0, partner_ref), (1, weight_ref)):
                found = jnp.sum(
                    jnp.where(jnp.logical_and(line16 == 3, lane16 == spot), wide, 0.0)
                )
                ref[x] = found.astype(ref.dtype)
        return carry

    lax.fori_loop(0, owners, one, 0, unroll=owners <= 4)


def arrange(pack, modes):
    owners, parts, each, _, _ = pack.shape
    pairs = owners * each
    smem = pl.BlockSpec(memory_space=pltpu.SMEM)
    vmem = pl.BlockSpec(memory_space=pltpu.VMEM)
    return pl.pallas_call(
        arrange_kernel,
        in_specs=[vmem],
        out_specs=[smem, smem, vmem, vmem, vmem, vmem],
        out_shape=[
            jax.ShapeDtypeStruct((pairs,), jnp.int32),
            jax.ShapeDtypeStruct((pairs,), F32),
            jax.ShapeDtypeStruct((pairs, modes, MAIN), BF16),
            jax.ShapeDtypeStruct((pairs, modes, modes), BF16),
            jax.ShapeDtypeStruct((pairs, 1, MAIN + TILE), F32),
            jax.ShapeDtypeStruct((modes, TILE), F32),
        ],
        compiler_params=pltpu.CompilerParams(vmem_limit_bytes=VMEM_BYTES),
        name="arrange",
    )(pack)


def interleave(heavy, light):
    done = 0
    for i, task in enumerate(heavy):
        task()
        upto = (i + 1) * len(light) // len(heavy)
        while done < upto:
            light[done]()
            done += 1
    while done < len(light):
        light[done]()
        done += 1


def coupling_kernel(
    share,
    block,
    partner_ref,
    weight_ref,
    home_ref,
    grid_ref,
    grid_t_ref,
    freq_row_ref,
    freq_col_ref,
    moved_ref,
    out_ref,
    turned_ref,
    grid_rest_ref,
    inner_rest_ref,
    pick_ref,
    rest_value_ref,
    home_row_ref,
    *work,
):
    gathers, inners, values, tabs, sums, rest_sums, firsts = (
        work[2 * i : 2 * i + 2] for i in range(7)
    )
    pairs = grid_ref.shape[0]
    modes = grid_ref.shape[1]
    rest = modes - MAIN
    sources, depth = moved_ref.shape[0], moved_ref.shape[2]
    per_slot = MAIN // rest
    rest_lanes = home_row_ref.shape[1]
    s2 = smearing * smearing
    steps = share // block

    for x in range(pairs):
        grid_rest_ref[x * rest : (x + 1) * rest, :] = grid_t_ref[x, MAIN:, :]
    spot = lax.broadcasted_iota(jnp.int32, (1, rest_lanes), 1) // rest
    row = jnp.ones((1, rest_lanes), F32)
    for r in range(share):
        row = jnp.where(spot == r, home_ref[r], row)
    home_row_ref[0:1, :] = row
    home_row_ref[1:2, :] = row * row - s2
    home_row_ref[2:3, :] = (4.0 * s2) * (row * row)
    home_row_ref[3:4, :] = 1.0 / row
    eye = identity(modes)
    if share * rest < rest_lanes:
        inner_rest_ref[...] = jnp.zeros_like(inner_rest_ref)
    for r in range(share):
        slot, spot = share + r // per_slot, r % per_slot
        half, spot = spot // (per_slot // 2), spot % (per_slot // 2)
        gather_ref = gathers[r % 2]
        for s in range(sources):
            gather_ref[s * depth : (s + 1) * depth, :MAIN] = moved_ref[s, r].astype(F32)
            tail = moved_ref[s, slot, :, half * TILE : (half + 1) * TILE].astype(F32)
            if spot > 0:
                tail = pltpu.roll(tail, TILE - spot * rest, 1)
            gather_ref[s * depth : (s + 1) * depth, MAIN:] = tail[:, :rest]
        whole = gather_ref[...].astype(BF16)
        turned_ref[r * modes : (r + 1) * modes, :] = dot_nt(eye, whole).astype(BF16)
        found = dot_nn(grid_rest_ref[...], whole).astype(BF16)
        for x in range(pairs):
            inner_rest_ref[x, r * rest : (r + 1) * rest, :] = found[x * rest : (x + 1) * rest, :]

    row_id = lax.broadcasted_iota(jnp.int32, pick_ref.shape, 0)
    col_id = lax.broadcasted_iota(jnp.int32, pick_ref.shape, 1)
    pick_ref[...] = (row_id // rest == col_id).astype(BF16)
    for ref in (out_ref, *sums, *rest_sums, *firsts):
        ref[...] = jnp.zeros_like(ref)

    def contract_first(x, r, b, into):
        def task():
            found = dot_nn(turned_ref[r * modes : (r + 1) * modes, :], grid_ref[x])
            into[:, b * MAIN : (b + 1) * MAIN] = found.astype(BF16)

        return task

    def contract_second(x, b, source, into):
        lanes = slice(b * MAIN, (b + 1) * MAIN)

        def task():
            into[:, lanes] = dot_nn(grid_t_ref[partner_ref[x]], source[:, lanes])

        return task

    def line_shapes(v, t, w, c1, c2):
        p = v * v
        d = t[0] - w
        e = t[1] - c1
        return (
            (p * t[2]) * pl.reciprocal(d * d + s2, approx=True),
            (p * t[3]) * pl.reciprocal(e * e + c2, approx=True),
        )

    def weigh(step, source, tab, sum_ref, first_ref):
        state = {}

        def begin():
            state["w"] = [home_ref[step * block + b] for b in range(block)]
            state["c1"] = [w * w - s2 for w in state["w"]]
            state["c2"] = [(4.0 * s2) * (w * w) for w in state["w"]]
            state["total"] = [jnp.zeros((8, MAIN), F32) for _ in range(block)]

        def rows(n):
            def task():
                if n == 0:
                    begin()
                t = [tab[k, n : n + 16, :MAIN] for k in range(4)]
                for b in range(block):
                    v = source[n : n + 16, b * MAIN : (b + 1) * MAIN]
                    f, u = line_shapes(v, t, state["w"][b], state["c1"][b], state["c2"][b])
                    state["total"][b] = state["total"][b] + (f[:8] + f[8:])
                    r = step * block + b
                    sum_ref[n : n + 16, r : r + 1] = jnp.sum(
                        u[:, :TILE] + u[:, TILE:], axis=1, keepdims=True
                    )
                if n + 16 == modes:
                    for b in range(block):
                        r = step * block + b
                        line = jnp.sum(state["total"][b], axis=0, keepdims=True)
                        first_ref[r : r + 1, :MAIN] = line * (1.0 / state["w"][b])

            return task

        return [rows(n) for n in range(0, modes, 16)]

    def contract_rest(x):
        def task():
            rest_value_ref[...] = dot_nt(grid_t_ref[partner_ref[x]], inner_rest_ref[x])

        return task

    def weigh_rest(tab, sum_ref, first_ref):
        def tile(start):
            lanes = slice(start, start + TILE)
            state = {}

            def rows(n):
                def task():
                    if n == 0:
                        state["total"] = jnp.zeros((8, TILE), F32)
                        state["w"] = home_row_ref[0:1, lanes]
                        state["c1"] = home_row_ref[1:2, lanes]
                        state["c2"] = home_row_ref[2:3, lanes]
                    for k in range(n, n + 48, 16):
                        t = [tab[i, k : k + 16, MAIN:] for i in range(4)]
                        f, u = line_shapes(
                            rest_value_ref[k : k + 16, lanes], t, state["w"], state["c1"], state["c2"]
                        )
                        state["total"] = state["total"] + (f[:8] + f[8:])
                        sum_ref[k : k + 16, lanes] = u.astype(BF16)
                    if n + 48 == modes:
                        line = jnp.sum(state["total"], axis=0, keepdims=True)
                        line = line * home_row_ref[3:4, lanes]
                        for b in range(TILE // rest):
                            r = start // rest + b
                            if r < share:
                                first_ref[r : r + 1, MAIN:] = line[:, b * rest : (b + 1) * rest]

                return task

            return [rows(n) for n in range(0, modes, 48)]

        return [task for start in range(0, rest_lanes, TILE) for task in tile(start)]

    def tables(x, tab):
        state = {}

        def begin():
            w1 = freq_row_ref[x]
            spots = lax.broadcasted_iota(jnp.int32, freq_col_ref.shape, 1)
            w2 = jnp.sum(
                jnp.where(spots == partner_ref[x], freq_col_ref[...], 0.0), axis=1, keepdims=True
            )
            state["w"] = (w1, w2)
            state["o"] = (occupy(w1), occupy(w2))
            scale = weight_ref[x] * (smearing / math.pi / modes)
            state["i"] = (scale / w1, 1.0 / w2)

        def rows(n):
            def task():
                if n == 0:
                    begin()
                part = slice(n, n + 48)
                (w1, w2), (o1, o2), (i1, i2) = state["w"], state["o"], state["i"]
                w2, o2, i2 = w2[part], o2[part], i2[part]
                a = w1 - w2
                both = i1 * i2
                tab[0, part, :] = w1 + w2
                tab[1, part, :] = a * a
                tab[2, part, :] = (1.0 + o1 + o2) * both
                tab[3, part, :] = (4.0 * a) * (o2 - o1) * both

            return task

        return [rows(n) for n in range(0, modes, 48)]

    def collect(sum_ref, rest_sum_ref, state):
        def task():
            second = sum_ref[...] + dot_nn(rest_sum_ref[...], pick_ref[...])
            state["second"] = second.T[:share, :]

        return task

    def deliver(x, target, state, first_ref):
        out_ref[x, :share, :] += first_ref[:share, :]
        out_ref[target, :share, :] += state["second"]

    for task in tables(0, tabs[0]):
        task()
    for g in range(2):
        for b in range(block):
            x, step = jnp.int32(g // steps), g % steps
            contract_first(x, step * block + b, b, inners[g])()
    for b in range(block):
        contract_second(jnp.int32(0), b, inners[0], values[0])()

    def two_pairs(i, carry):
        for e in range(2):
            x = i * 2 + e

            def later(g):
                return jnp.minimum(i * 2 + g // steps, pairs - 1), g % steps

            before = jnp.maximum(x - 1, 0)
            target = partner_ref[before]
            extra = weigh_rest(tabs[e], rest_sums[e], firsts[e])
            extra = extra + tables(jnp.minimum(x + 1, pairs - 1), tabs[1 - e])
            contract_rest(x)()
            done = {}
            for s in range(steps):
                g = e * steps + s
                heavy = []
                for b in range(block):
                    x1, _ = later(g + 1)
                    heavy.append(contract_second(x1, b, inners[(g + 1) % 2], values[(g + 1) % 2]))
                for b in range(block):
                    x2, step2 = later(g + 2)
                    heavy.append(contract_first(x2, step2 * block + b, b, inners[g % 2]))
                light = weigh(s, values[g % 2], tabs[e], sums[e], firsts[e])
                light = light + extra[s * len(extra) // steps : (s + 1) * len(extra) // steps]
                if s == 0:
                    heavy.insert(1, collect(sums[1 - e], rest_sums[1 - e], done))
                interleave(heavy, light)
            deliver(before, target, done, firsts[1 - e])
        return carry

    lax.fori_loop(0, pairs // 2, two_pairs, 0)
    last = {}
    collect(sums[1], rest_sums[1], last)()
    deliver(pairs - 1, partner_ref[pairs - 1], last, firsts[1])

    totals = jnp.zeros(out_ref.shape[1:], F32)
    for y in range(pairs):
        totals = totals + out_ref[y]
    widths = jnp.sum(totals, axis=1, keepdims=True) * (1.0 / (pairs * modes))
    spread = jnp.where(
        lax.broadcasted_iota(jnp.int32, totals.shape, 0)
        == lax.broadcasted_iota(jnp.int32, totals.shape, 1),
        widths,
        0.0,
    )
    out_ref[:, share, :] = jnp.broadcast_to(
        jnp.sum(spread, axis=0, keepdims=True), (pairs, modes)
    )


def coupling(partner, weights, home, grid, grid_t, freq_rows, freq_cols, moved):
    pairs, modes = grid.shape[0], grid.shape[1]
    share = home.shape[0]
    rest = modes - MAIN
    rest_lanes = ceil_div(share * rest, TILE) * TILE
    padded = (share // 8 + 1) * 8
    smem = pl.BlockSpec(memory_space=pltpu.SMEM)
    vmem = pl.BlockSpec(memory_space=pltpu.VMEM)
    block = 3 if share % 3 == 0 else 1
    assert pairs % 2 == 0
    scratch = (
        [
            pltpu.VMEM((share * modes, modes), BF16),
            pltpu.VMEM((pairs * rest, modes), BF16),
            pltpu.VMEM((pairs, rest_lanes, modes), BF16),
            pltpu.VMEM((rest_lanes, TILE), BF16),
            pltpu.VMEM((modes, rest_lanes), F32),
            pltpu.VMEM((8, rest_lanes), F32),
        ]
        + [pltpu.VMEM((modes, modes), F32)] * 2
        + [pltpu.VMEM((modes, block * MAIN), BF16)] * 2
        + [pltpu.VMEM((modes, block * MAIN), F32)] * 2
        + [pltpu.VMEM((4, modes, MAIN + TILE), F32)] * 2
        + [pltpu.VMEM((modes, TILE), F32)] * 2
        + [pltpu.VMEM((modes, rest_lanes), BF16)] * 2
        + [pltpu.VMEM((padded, modes), F32)] * 2
    )
    return pl.pallas_call(
        functools.partial(coupling_kernel, share, block),
        in_specs=[smem, smem, smem, vmem, vmem, vmem, vmem, vmem],
        out_specs=vmem,
        out_shape=jax.ShapeDtypeStruct((pairs, padded, modes), F32),
        scratch_shapes=scratch,
        compiler_params=pltpu.CompilerParams(vmem_limit_bytes=VMEM_BYTES),
        cost_estimate=pl.CostEstimate(
            flops=4 * share * pairs * modes**3,
            bytes_accessed=8 * share * modes * modes,
            transcendentals=2 * share * pairs * modes**2,
        ),
        name="coupling",
    )(partner, weights, home, grid, grid_t, freq_rows, freq_cols, moved)


def local(
    home_vectors, home_freqs, grid_vectors, partner_frequencies, force_table, partner, weights
):
    own_pairs = partner.shape[0]
    modes = home_vectors.shape[0]
    n_mode = lax.axis_size("mode")
    n_fc = lax.axis_size("fc")
    n_qp = lax.axis_size("qp")
    groups = n_mode * n_fc
    group = modes // groups
    pairs = own_pairs * n_qp
    share = ceil_div(group, n_qp)
    here = lax.axis_index("qp")
    if share % 6 == 0 and share > 6:
        chunks = ((0, 6), (6, share - 6))
    else:
        chunks = ((0, share),)

    assert n_fc * TILE == MAIN
    own_part = lax.axis_index("fc").astype(jnp.int32)[None]
    pack = pack_own(own_part, partner, weights, grid_vectors, partner_frequencies)
    pack = lax.all_gather(pack, ("qp", "fc"), axis=0)
    pack = pack.reshape(n_qp, n_fc, own_pairs, pack.shape[2], TILE)

    here_word = here.astype(jnp.int32)[None]
    moved = []
    for first, count in chunks:
        sent = project(here_word, home_vectors, force_table, groups, group, share, first, count)
        moved.append(
            lax.all_to_all(sent, ("mode", "fc"), split_axis=0, concat_axis=0, tiled=True)
        )

    own = lax.axis_index(("mode", "fc"))
    home = home_freqs.astype(F32).reshape(groups, group)
    home = jnp.pad(home, ((0, 0), (0, share * n_qp - group)), constant_values=1.0)
    home = lax.dynamic_slice(home, (own, here * share), (1, share)).reshape(share)

    shared = arrange(pack, modes)
    parts, widths = [], []
    for (first, count), block in zip(chunks, moved):
        found = coupling(
            shared[0], shared[1], home[first : first + count], *shared[2:], block
        )
        back = lax.all_to_all(
            found.reshape(n_qp, own_pairs, found.shape[1], modes),
            "qp",
            split_axis=0,
            concat_axis=0,
            tiled=True,
        )
        widths.append(back[:, 0, count, :count])
        parts.append(back[:, :, :count, :])
    widths = jnp.concatenate(widths, axis=1).reshape(n_qp * share)[:group]
    collision = jnp.transpose(jnp.concatenate(parts, axis=2), (0, 2, 1, 3))
    collision = collision.reshape(n_qp * share, own_pairs, modes)[:group]
    return (widths, collision)


def solution(mesh):
    placed = (
        P("grp", None),
        P("grp"),
        P("qp", None, None),
        P("qp", None),
        P(None, ("mode", "fc")),
        P(("grp", "qp")),
        P(("grp", "qp")),
    )
    return jax.shard_map(
        local,
        mesh=mesh,
        in_specs=placed,
        out_specs=(P(("grp", "mode", "fc")), P(("mode", "fc"), ("grp", "qp"), None)),
        check_vma=False,
    )
```

```python
import functools
import math

import jax
import jax.numpy as jnp
from jax import lax
from jax.experimental import pallas as pl
from jax.experimental.pallas import tpu as pltpu
from jax.sharding import PartitionSpec as P

thermal_reservoir_kelvin = 1.0
smearing = 0.25

MAIN = 256
TILE = 128
F32 = jnp.float32
BF16 = jnp.bfloat16


def ceil_div(a, b):
    return -(-a // b)


VMEM_BYTES = 56 << 20


def occupy(energy):
    return 1.0 / (jnp.exp(energy / thermal_reservoir_kelvin) - 1.0)


def dot_nn(a, b):
    return lax.dot_general(a, b, (((1,), (0,)), ((), ())), preferred_element_type=F32)


def dot_nt(a, b):
    return lax.dot_general(a, b, (((1,), (1,)), ((), ())), preferred_element_type=F32)


def slots_of(count, modes):
    return count + ceil_div(count, MAIN // (modes - MAIN))


STREAMS = 3


def project_kernel(groups, group, share, first, count, here_ref, home_ref, *refs):
    force_refs, (out_ref, rows_ref, main_ref, rest_ref) = refs[:STREAMS], refs[STREAMS:]
    modes = home_ref.shape[0]
    lines = groups * count
    rest = modes - MAIN
    per_slot = MAIN // rest
    depth = out_ref.shape[2]
    step = pl.program_id(0)
    here = force_refs[0].shape[1] // modes
    pitch = lines + 1

    @pl.when(step == 0)
    def _():
        line = lax.broadcasted_iota(jnp.int32, (lines, modes), 0)
        column = lax.broadcasted_iota(jnp.int32, (lines, modes), 1)
        own = here_ref[0] * share + first + line % count
        wanted = (line // count) * group + own
        select = jnp.logical_and(column == wanted, own < group).astype(BF16)
        rows_ref[...] = dot_nt(select, home_ref[...]).astype(BF16)

    force = jnp.concatenate([ref[...] for ref in force_refs], axis=0)
    result = dot_nn(rows_ref[...], force)
    for c in range(here):
        row = (step * here + c) * pitch
        piece = result[:, c * modes : (c + 1) * modes]
        main_ref[0, pl.ds(row, lines), :] = piece[:, :TILE]
        main_ref[1, pl.ds(row, lines), :] = piece[:, TILE:MAIN]
        rest_ref[pl.ds(row, lines), :] = jnp.concatenate(
            [piece[:, MAIN:], jnp.zeros((lines, TILE - rest), F32)], axis=1
        )

    @pl.when(step == pl.num_programs(0) - 1)
    def _():
        lane = lax.broadcasted_iota(jnp.int32, (depth, TILE), 1)
        for t in range(groups):
            base = t * count
            for r in range(count):
                for h in range(2):
                    out_ref[t, r, :, h * TILE : (h + 1) * TILE] = main_ref[
                        h, pl.ds(base + r, depth, stride=pitch), :
                    ].astype(BF16)
            for g in range(ceil_div(count, per_slot)):
                for h in range(2):
                    packed = jnp.zeros((depth, TILE), F32)
                    for b in range(per_slot // 2):
                        r = g * per_slot + h * (per_slot // 2) + b
                        if r < count:
                            piece = rest_ref[pl.ds(base + r, depth, stride=pitch), :]
                            if b > 0:
                                piece = pltpu.roll(piece, b * rest, 1)
                            packed = jnp.where(lane // rest == b, piece, packed)
                    out_ref[t, count + g, :, h * TILE : (h + 1) * TILE] = packed.astype(BF16)


def project(here, home_vectors, force_table, groups, group, share, first, count):
    modes = home_vectors.shape[0]
    lines = groups * count
    depth = force_table.shape[1] // modes
    per_step = 8 if depth % 8 == 0 else 4
    rows = modes // STREAMS
    shape = (groups, slots_of(count, modes), depth, MAIN)

    def stream(k):
        return pl.BlockSpec((rows, per_step * modes), lambda i: (k, i))

    return pl.pallas_call(
        functools.partial(project_kernel, groups, group, share, first, count),
        grid=(depth // per_step,),
        in_specs=[
            pl.BlockSpec(memory_space=pltpu.SMEM),
            pl.BlockSpec((modes, modes), lambda i: (0, 0)),
        ]
        + [stream(k) for k in range(STREAMS)],
        out_specs=pl.BlockSpec(shape, lambda i: (0, 0, 0, 0)),
        out_shape=jax.ShapeDtypeStruct(shape, BF16),
        scratch_shapes=[
            pltpu.VMEM((lines, modes), BF16),
            pltpu.VMEM((2, (depth + 1) * (lines + 1), TILE), F32),
            pltpu.VMEM(((depth + 1) * (lines + 1), TILE), F32),
        ],
        compiler_params=pltpu.CompilerParams(vmem_limit_bytes=VMEM_BYTES),
        cost_estimate=pl.CostEstimate(
            flops=2 * lines * modes * modes * depth,
            bytes_accessed=2 * modes * modes * depth,
            transcendentals=0,
        ),
        name="project",
    )(here, home_vectors, *[force_table] * STREAMS)


def identity(size):
    return (
        lax.broadcasted_iota(jnp.int32, (size, size), 0)
        == lax.broadcasted_iota(jnp.int32, (size, size), 1)
    ).astype(BF16)


def pack_kernel(part_ref, partner_ref, weight_ref, grid_ref, freq_ref, out_ref):
    own_pairs, modes, _ = grid_ref.shape
    rest = modes - MAIN
    lines = rest // 2
    part = part_ref[0]
    line = lax.broadcasted_iota(jnp.int32, (lines, modes), 0)
    column = lax.broadcasted_iota(jnp.int32, (lines, modes), 1)
    select = (column == MAIN + part * lines + line).astype(BF16)
    freqs = freq_ref[...].astype(F32)
    blank = jnp.zeros((own_pairs, TILE - rest), F32)
    freq_tiles = (
        freqs[:, :TILE],
        freqs[:, TILE:MAIN],
        jnp.concatenate([freqs[:, MAIN:], blank], axis=1),
    )
    line16 = lax.broadcasted_iota(jnp.int32, (16, TILE), 0)
    lane16 = lax.broadcasted_iota(jnp.int32, (16, TILE), 1)
    for s in range(own_pairs):
        for p in range(2):

            @pl.when(part == p)
            def _():
                out_ref[s, :modes, :] = grid_ref[s, :, p * TILE : (p + 1) * TILE]

        turned = dot_nt(select, grid_ref[s])
        turned = (
            turned[:, :TILE],
            turned[:, TILE:MAIN],
            jnp.concatenate([turned[:, MAIN:], jnp.zeros((lines, TILE - rest), F32)], axis=1),
        )
        for h in range(3):
            start = modes + h * lines
            out_ref[s, start : start + lines, :] = turned[h].astype(BF16)
        pair = partner_ref[s].astype(F32)
        weight = weight_ref[s].astype(F32)
        side = jnp.where(lane16 == 0, pair, jnp.where(lane16 == 1, weight, 0.0))
        side = jnp.where(line16 == 3, side, 0.0)
        for h in range(3):
            side = jnp.where(line16 == h, freq_tiles[h][s : s + 1], side)
        start = modes + 3 * lines
        out_ref[s, start : start + 16, :] = side.astype(BF16)


def pack_own(part, partner, weights, grid_vectors, partner_frequencies):
    own_pairs, modes, _ = grid_vectors.shape
    smem = pl.BlockSpec(memory_space=pltpu.SMEM)
    vmem = pl.BlockSpec(memory_space=pltpu.VMEM)
    rows = modes + 3 * (modes - MAIN) // 2 + 16
    return pl.pallas_call(
        pack_kernel,
        in_specs=[smem, smem, smem, vmem, vmem],
        out_specs=vmem,
        out_shape=jax.ShapeDtypeStruct((own_pairs, rows, TILE), BF16),
        compiler_params=pltpu.CompilerParams(vmem_limit_bytes=VMEM_BYTES),
        name="pack_own",
    )(part, partner, weights, grid_vectors, partner_frequencies)


def arrange_kernel(
    pack_ref, partner_ref, weight_ref, grid_ref, grid_t_ref, freq_row_ref, freq_col_ref
):
    owners, parts, each, rows, _ = pack_ref.shape
    modes = grid_ref.shape[1]
    rest = modes - MAIN
    lines = rest // parts
    eye = identity(MAIN)
    source = lax.broadcasted_iota(jnp.int32, (TILE, TILE), 0)
    place = lax.broadcasted_iota(jnp.int32, (TILE, TILE), 1)
    spread = (source == place % rest).astype(BF16)
    eye_tile = (source == place).astype(BF16)
    lane = lax.broadcasted_iota(jnp.int32, (TILE, freq_col_ref.shape[1]), 1)
    line16 = lax.broadcasted_iota(jnp.int32, (16, TILE), 0)
    lane16 = lax.broadcasted_iota(jnp.int32, (16, TILE), 1)
    freq_col_ref[...] = jnp.zeros_like(freq_col_ref)

    def one(q, carry):
        for s in range(each):
            x = q * each + s
            for part in range(parts):
                grid_ref[x, :, part * TILE : (part + 1) * TILE] = pack_ref[q, part, s, :modes, :]
                for h in range(3):
                    start, width = modes + h * lines, min(TILE, modes - h * TILE)
                    piece = pack_ref[q, part, s, start : start + lines, :]
                    grid_t_ref[
                        x, MAIN + part * lines : MAIN + (part + 1) * lines, h * TILE : h * TILE + width
                    ] = piece[:, :width]
            grid_t_ref[x, :MAIN, :] = dot_nt(eye, grid_ref[x]).astype(BF16)
            side = pack_ref[q, 0, s, modes + 3 * lines : modes + 3 * lines + 16, :]
            wide = side.astype(F32)
            freq_row_ref[x, :, :TILE] = wide[0:1]
            freq_row_ref[x, :, TILE:MAIN] = wide[1:2]
            freq_row_ref[x, :, MAIN:] = dot_nn(side, spread)[2:3]
            columns = dot_nt(eye_tile, side)
            for h in range(3):
                width = min(TILE, modes - h * TILE)
                here = slice(h * TILE, h * TILE + width)
                freq_col_ref[here, :] = jnp.where(
                    lane[:width] == x, columns[:width, h : h + 1], freq_col_ref[here, :]
                )
            for spot, ref in ((0, partner_ref), (1, weight_ref)):
                found = jnp.sum(
                    jnp.where(jnp.logical_and(line16 == 3, lane16 == spot), wide, 0.0)
                )
                ref[x] = found.astype(ref.dtype)
        return carry

    lax.fori_loop(0, owners, one, 0, unroll=owners <= 4)


def arrange(pack, modes):
    owners, parts, each, _, _ = pack.shape
    pairs = owners * each
    smem = pl.BlockSpec(memory_space=pltpu.SMEM)
    vmem = pl.BlockSpec(memory_space=pltpu.VMEM)
    return pl.pallas_call(
        arrange_kernel,
        in_specs=[vmem],
        out_specs=[smem, smem, vmem, vmem, vmem, vmem],
        out_shape=[
            jax.ShapeDtypeStruct((pairs,), jnp.int32),
            jax.ShapeDtypeStruct((pairs,), F32),
            jax.ShapeDtypeStruct((pairs, modes, MAIN), BF16),
            jax.ShapeDtypeStruct((pairs, modes, modes), BF16),
            jax.ShapeDtypeStruct((pairs, 1, MAIN + TILE), F32),
            jax.ShapeDtypeStruct((modes, TILE), F32),
        ],
        compiler_params=pltpu.CompilerParams(vmem_limit_bytes=VMEM_BYTES),
        name="arrange",
    )(pack)


def interleave(heavy, light):
    done = 0
    for i, task in enumerate(heavy):
        task()
        upto = (i + 1) * len(light) // len(heavy)
        while done < upto:
            light[done]()
            done += 1
    while done < len(light):
        light[done]()
        done += 1


def coupling_kernel(
    first,
    share,
    block,
    partner_ref,
    weight_ref,
    home_ref,
    grid_source,
    grid_t_source,
    freq_row_ref,
    freq_col_ref,
    moved_ref,
    out_ref,
    turned_ref,
    grid_rest_ref,
    inner_rest_ref,
    pick_ref,
    rest_value_ref,
    home_row_ref,
    grid_ref,
    grid_t_ref,
    copy_sem,
    *work,
):
    gathers, inners, values, tabs, sums, rest_sums, firsts = (
        work[2 * i : 2 * i + 2] for i in range(7)
    )
    pairs = grid_ref.shape[0]
    modes = grid_ref.shape[1]
    rest = modes - MAIN
    sources, depth = moved_ref.shape[0], moved_ref.shape[2]
    per_slot = MAIN // rest
    rest_lanes = home_row_ref.shape[1]
    s2 = smearing * smearing
    steps = share // block

    fetch_turned = pltpu.make_async_copy(grid_t_source, grid_t_ref, copy_sem.at[0])
    fetch_grid = pltpu.make_async_copy(grid_source, grid_ref, copy_sem.at[1])
    fetch_turned.start()
    fetch_grid.start()
    spot = lax.broadcasted_iota(jnp.int32, (1, rest_lanes), 1) // rest
    row = jnp.ones((1, rest_lanes), F32)
    for r in range(share):
        row = jnp.where(spot == r, home_ref[first + r], row)
    home_row_ref[0:1, :] = row
    home_row_ref[1:2, :] = row * row - s2
    home_row_ref[2:3, :] = (4.0 * s2) * (row * row)
    home_row_ref[3:4, :] = 1.0 / row
    eye = identity(modes)
    if share * rest < rest_lanes:
        inner_rest_ref[...] = jnp.zeros_like(inner_rest_ref)
    for r in range(share):
        slot, spot = share + r // per_slot, r % per_slot
        half, spot = spot // (per_slot // 2), spot % (per_slot // 2)
        gather_ref = gathers[r % 2]
        for s in range(sources):
            gather_ref[s * depth : (s + 1) * depth, :MAIN] = moved_ref[s, r].astype(F32)
            tail = moved_ref[s, slot, :, half * TILE : (half + 1) * TILE].astype(F32)
            if spot > 0:
                tail = pltpu.roll(tail, TILE - spot * rest, 1)
            gather_ref[s * depth : (s + 1) * depth, MAIN:] = tail[:, :rest]
        whole = gather_ref[...].astype(BF16)
        turned_ref[r * modes : (r + 1) * modes, :] = dot_nt(eye, whole).astype(BF16)

    fetch_turned.wait()
    for x in range(pairs):
        grid_rest_ref[x * rest : (x + 1) * rest, :] = grid_t_ref[x, MAIN:, :]
    for r in range(share):
        found = dot_nt(grid_rest_ref[...], turned_ref[r * modes : (r + 1) * modes, :]).astype(BF16)
        for x in range(pairs):
            inner_rest_ref[x, r * rest : (r + 1) * rest, :] = found[x * rest : (x + 1) * rest, :]

    fetch_grid.wait()

    row_id = lax.broadcasted_iota(jnp.int32, pick_ref.shape, 0)
    col_id = lax.broadcasted_iota(jnp.int32, pick_ref.shape, 1)
    pick_ref[...] = (row_id // rest == col_id).astype(BF16)
    for ref in (out_ref, *sums, *rest_sums, *firsts):
        ref[...] = jnp.zeros_like(ref)

    def contract_first(x, r, b, into):
        def task():
            found = dot_nn(turned_ref[r * modes : (r + 1) * modes, :], grid_ref[x])
            into[:, b * MAIN : (b + 1) * MAIN] = found.astype(BF16)

        return task

    def contract_second(x, b, source, into):
        lanes = slice(b * MAIN, (b + 1) * MAIN)

        def task():
            into[:, lanes] = dot_nn(grid_t_ref[partner_ref[x]], source[:, lanes])

        return task

    def line_shapes(v, t, w, c1, c2):
        p = v * v
        d = t[0] - w
        e = t[1] - c1
        return (
            (p * t[2]) * pl.reciprocal(d * d + s2, approx=True),
            (p * t[3]) * pl.reciprocal(e * e + c2, approx=True),
        )

    def weigh(step, source, tab, sum_ref, first_ref):
        state = {}

        def begin():
            state["w"] = [home_ref[first + step * block + b] for b in range(block)]
            state["c1"] = [w * w - s2 for w in state["w"]]
            state["c2"] = [(4.0 * s2) * (w * w) for w in state["w"]]
            state["total"] = [jnp.zeros((8, MAIN), F32) for _ in range(block)]

        def rows(n):
            def task():
                if n == 0:
                    begin()
                t = [tab[k, n : n + 16, :MAIN] for k in range(4)]
                for b in range(block):
                    v = source[n : n + 16, b * MAIN : (b + 1) * MAIN]
                    f, u = line_shapes(v, t, state["w"][b], state["c1"][b], state["c2"][b])
                    state["total"][b] = state["total"][b] + (f[:8] + f[8:])
                    r = step * block + b
                    sum_ref[n : n + 16, r : r + 1] = jnp.sum(
                        u[:, :TILE] + u[:, TILE:], axis=1, keepdims=True
                    )
                if n + 16 == modes:
                    for b in range(block):
                        r = step * block + b
                        line = jnp.sum(state["total"][b], axis=0, keepdims=True)
                        first_ref[r : r + 1, :MAIN] = line * (1.0 / state["w"][b])

            return task

        return [rows(n) for n in range(0, modes, 16)]

    def contract_rest(x):
        def task():
            rest_value_ref[...] = dot_nt(grid_t_ref[partner_ref[x]], inner_rest_ref[x])

        return task

    def weigh_rest(tab, sum_ref, first_ref):
        def tile(start):
            lanes = slice(start, start + TILE)
            state = {}

            def rows(n):
                def task():
                    if n == 0:
                        state["total"] = jnp.zeros((8, TILE), F32)
                        state["w"] = home_row_ref[0:1, lanes]
                        state["c1"] = home_row_ref[1:2, lanes]
                        state["c2"] = home_row_ref[2:3, lanes]
                    for k in range(n, n + 48, 16):
                        t = [tab[i, k : k + 16, MAIN:] for i in range(4)]
                        f, u = line_shapes(
                            rest_value_ref[k : k + 16, lanes], t, state["w"], state["c1"], state["c2"]
                        )
                        state["total"] = state["total"] + (f[:8] + f[8:])
                        sum_ref[k : k + 16, lanes] = u.astype(BF16)
                    if n + 48 == modes:
                        line = jnp.sum(state["total"], axis=0, keepdims=True)
                        line = line * home_row_ref[3:4, lanes]
                        for b in range(TILE // rest):
                            r = start // rest + b
                            if r < share:
                                first_ref[r : r + 1, MAIN:] = line[:, b * rest : (b + 1) * rest]

                return task

            return [rows(n) for n in range(0, modes, 48)]

        return [task for start in range(0, rest_lanes, TILE) for task in tile(start)]

    def tables(x, tab):
        state = {}

        def begin():
            w1 = freq_row_ref[x]
            spots = lax.broadcasted_iota(jnp.int32, freq_col_ref.shape, 1)
            w2 = jnp.sum(
                jnp.where(spots == partner_ref[x], freq_col_ref[...], 0.0), axis=1, keepdims=True
            )
            state["w"] = (w1, w2)
            state["o"] = (occupy(w1), occupy(w2))
            scale = weight_ref[x] * (smearing / math.pi / modes)
            state["i"] = (scale / w1, 1.0 / w2)

        def rows(n):
            def task():
                if n == 0:
                    begin()
                part = slice(n, n + 48)
                (w1, w2), (o1, o2), (i1, i2) = state["w"], state["o"], state["i"]
                w2, o2, i2 = w2[part], o2[part], i2[part]
                a = w1 - w2
                both = i1 * i2
                tab[0, part, :] = w1 + w2
                tab[1, part, :] = a * a
                tab[2, part, :] = (1.0 + o1 + o2) * both
                tab[3, part, :] = (4.0 * a) * (o2 - o1) * both

            return task

        return [rows(n) for n in range(0, modes, 48)]

    def collect(sum_ref, rest_sum_ref, state):
        def task():
            second = sum_ref[...] + dot_nn(rest_sum_ref[...], pick_ref[...])
            state["second"] = second.T[:share, :]

        return task

    def deliver(x, target, state, first_ref):
        out_ref[x, :share, :] += first_ref[:share, :]
        out_ref[target, :share, :] += state["second"]

    for task in tables(0, tabs[0]):
        task()
    for g in range(2):
        for b in range(block):
            x, step = jnp.int32(g // steps), g % steps
            contract_first(x, step * block + b, b, inners[g])()
    for b in range(block):
        contract_second(jnp.int32(0), b, inners[0], values[0])()

    def two_pairs(i, carry):
        for e in range(2):
            x = i * 2 + e

            def later(g):
                return jnp.minimum(i * 2 + g // steps, pairs - 1), g % steps

            before = jnp.maximum(x - 1, 0)
            target = partner_ref[before]
            extra = weigh_rest(tabs[e], rest_sums[e], firsts[e])
            extra = extra + tables(jnp.minimum(x + 1, pairs - 1), tabs[1 - e])
            contract_rest(x)()
            done = {}
            for s in range(steps):
                g = e * steps + s
                heavy = []
                for b in range(block):
                    x1, _ = later(g + 1)
                    heavy.append(contract_second(x1, b, inners[(g + 1) % 2], values[(g + 1) % 2]))
                for b in range(block):
                    x2, step2 = later(g + 2)
                    heavy.append(contract_first(x2, step2 * block + b, b, inners[g % 2]))
                light = weigh(s, values[g % 2], tabs[e], sums[e], firsts[e])
                light = light + extra[s * len(extra) // steps : (s + 1) * len(extra) // steps]
                if s == 0:
                    heavy.insert(1, collect(sums[1 - e], rest_sums[1 - e], done))
                interleave(heavy, light)
            deliver(before, target, done, firsts[1 - e])
        return carry

    lax.fori_loop(0, pairs // 2, two_pairs, 0)
    last = {}
    collect(sums[1], rest_sums[1], last)()
    deliver(pairs - 1, partner_ref[pairs - 1], last, firsts[1])

    totals = jnp.zeros(out_ref.shape[1:], F32)
    for y in range(pairs):
        totals = totals + out_ref[y]
    widths = jnp.sum(totals, axis=1, keepdims=True) * (1.0 / (pairs * modes))
    spread = jnp.where(
        lax.broadcasted_iota(jnp.int32, totals.shape, 0)
        == lax.broadcasted_iota(jnp.int32, totals.shape, 1),
        widths,
        0.0,
    )
    out_ref[:, share, :] = jnp.broadcast_to(
        jnp.sum(spread, axis=0, keepdims=True), (pairs, modes)
    )


def coupling(first, share, partner, weights, home, grid, grid_t, freq_rows, freq_cols, moved):
    pairs, modes = grid.shape[0], grid.shape[1]
    rest = modes - MAIN
    rest_lanes = ceil_div(share * rest, TILE) * TILE
    padded = (share // 8 + 1) * 8
    smem = pl.BlockSpec(memory_space=pltpu.SMEM)
    vmem = pl.BlockSpec(memory_space=pltpu.VMEM)
    block = 3 if share % 3 == 0 else 1
    assert pairs % 2 == 0
    scratch = (
        [
            pltpu.VMEM((share * modes, modes), BF16),
            pltpu.VMEM((pairs * rest, modes), BF16),
            pltpu.VMEM((pairs, rest_lanes, modes), BF16),
            pltpu.VMEM((rest_lanes, TILE), BF16),
            pltpu.VMEM((modes, rest_lanes), F32),
            pltpu.VMEM((8, rest_lanes), F32),
            pltpu.VMEM(grid.shape, BF16),
            pltpu.VMEM(grid_t.shape, BF16),
            pltpu.SemaphoreType.DMA((2,)),
        ]
        + [pltpu.VMEM((modes, modes), F32)] * 2
        + [pltpu.VMEM((modes, block * MAIN), BF16)] * 2
        + [pltpu.VMEM((modes, block * MAIN), F32)] * 2
        + [pltpu.VMEM((4, modes, MAIN + TILE), F32)] * 2
        + [pltpu.VMEM((modes, TILE), F32)] * 2
        + [pltpu.VMEM((modes, rest_lanes), BF16)] * 2
        + [pltpu.VMEM((padded, modes), F32)] * 2
    )
    return pl.pallas_call(
        functools.partial(coupling_kernel, first, share, block),
        in_specs=[smem] * 3 + [pl.BlockSpec(memory_space=pl.ANY)] * 2 + [vmem] * 3,
        out_specs=vmem,
        out_shape=jax.ShapeDtypeStruct((pairs, padded, modes), F32),
        scratch_shapes=scratch,
        compiler_params=pltpu.CompilerParams(vmem_limit_bytes=VMEM_BYTES),
        cost_estimate=pl.CostEstimate(
            flops=4 * share * pairs * modes**3,
            bytes_accessed=8 * share * modes * modes,
            transcendentals=2 * share * pairs * modes**2,
        ),
        name="coupling",
    )(partner, weights, home, grid, grid_t, freq_rows, freq_cols, moved)


def local(
    home_vectors, home_freqs, grid_vectors, partner_frequencies, force_table, partner, weights
):
    own_pairs = partner.shape[0]
    modes = home_vectors.shape[0]
    n_mode = lax.axis_size("mode")
    n_fc = lax.axis_size("fc")
    n_qp = lax.axis_size("qp")
    groups = n_mode * n_fc
    group = modes // groups
    pairs = own_pairs * n_qp
    share = ceil_div(group, n_qp)
    here = lax.axis_index("qp")
    if share % 6 == 0 and share > 6:
        chunks = ((0, 6), (6, share - 6))
    else:
        chunks = ((0, share),)

    assert n_fc * TILE == MAIN
    own_part = lax.axis_index("fc").astype(jnp.int32)[None]
    pack = pack_own(own_part, partner, weights, grid_vectors, partner_frequencies)
    pack = lax.all_gather(pack, ("qp", "fc"), axis=0)
    pack = pack.reshape(n_qp, n_fc, own_pairs, pack.shape[2], TILE)

    here_word = here.astype(jnp.int32)[None]
    moved = []
    for first, count in chunks:
        sent = project(here_word, home_vectors, force_table, groups, group, share, first, count)
        moved.append(
            lax.all_to_all(sent, ("mode", "fc"), split_axis=0, concat_axis=0, tiled=True)
        )

    own = lax.axis_index(("mode", "fc"))
    home = home_freqs.astype(F32).reshape(groups, group)
    home = jnp.pad(home, ((0, 0), (0, share * n_qp - group)), constant_values=1.0)
    home = lax.dynamic_slice(home, (own, here * share), (1, share)).reshape(share)

    shared = arrange(pack, modes)
    parts, widths = [], []
    for (first, count), block in zip(chunks, moved):
        found = coupling(
            first, count, shared[0], shared[1], home, *shared[2:], block
        )
        back = lax.all_to_all(
            found.reshape(n_qp, own_pairs, found.shape[1], modes),
            "qp",
            split_axis=0,
            concat_axis=0,
            tiled=True,
        )
        widths.append(back[:, 0, count, :count])
        parts.append(back[:, :, :count, :])
    widths = jnp.concatenate(widths, axis=1).reshape(n_qp * share)[:group]
    collision = jnp.transpose(jnp.concatenate(parts, axis=2), (0, 2, 1, 3))
    collision = collision.reshape(n_qp * share, own_pairs, modes)[:group]
    return (widths, collision)


def solution(mesh):
    placed = (
        P("grp", None),
        P("grp"),
        P("qp", None, None),
        P("qp", None),
        P(None, ("mode", "fc")),
        P(("grp", "qp")),
        P(("grp", "qp")),
    )
    return jax.shard_map(
        local,
        mesh=mesh,
        in_specs=placed,
        out_specs=(P(("grp", "mode", "fc")), P(("mode", "fc"), ("grp", "qp"), None)),
        check_vma=False,
    )
```

```python
import functools
import math

import jax
import jax.numpy as jnp
from jax import lax
from jax.experimental import pallas as pl
from jax.experimental.pallas import tpu as pltpu
from jax.sharding import PartitionSpec as P

thermal_reservoir_kelvin = 1.0
smearing = 0.25

MAIN = 256
TILE = 128
F32 = jnp.float32
BF16 = jnp.bfloat16


def ceil_div(a, b):
    return -(-a // b)


VMEM_BYTES = 56 << 20


def occupy(energy):
    return 1.0 / (jnp.exp(energy / thermal_reservoir_kelvin) - 1.0)


def dot_nn(a, b):
    return lax.dot_general(a, b, (((1,), (0,)), ((), ())), preferred_element_type=F32)


def dot_nt(a, b):
    return lax.dot_general(a, b, (((1,), (1,)), ((), ())), preferred_element_type=F32)


def slots_of(count, modes):
    return count + ceil_div(count, MAIN // (modes - MAIN))


STREAMS = 3


def project_kernel(groups, group, share, first, count, here_ref, home_ref, *refs):
    force_refs, (out_ref, rows_ref, main_ref, rest_ref) = refs[:STREAMS], refs[STREAMS:]
    modes = home_ref.shape[0]
    lines = groups * count
    rest = modes - MAIN
    per_slot = MAIN // rest
    depth = out_ref.shape[2]
    step = pl.program_id(0)
    here = force_refs[0].shape[1] // modes
    pitch = lines + 1

    @pl.when(step == 0)
    def _():
        line = lax.broadcasted_iota(jnp.int32, (lines, modes), 0)
        column = lax.broadcasted_iota(jnp.int32, (lines, modes), 1)
        own = here_ref[0] * share + first + line % count
        wanted = (line // count) * group + own
        select = jnp.logical_and(column == wanted, own < group).astype(BF16)
        rows_ref[...] = dot_nt(select, home_ref[...]).astype(BF16)

    force = jnp.concatenate([ref[...] for ref in force_refs], axis=0)
    result = dot_nn(rows_ref[...], force)
    for c in range(here):
        row = (step * here + c) * pitch
        piece = result[:, c * modes : (c + 1) * modes]
        main_ref[0, pl.ds(row, lines), :] = piece[:, :TILE]
        main_ref[1, pl.ds(row, lines), :] = piece[:, TILE:MAIN]
        rest_ref[pl.ds(row, lines), :] = jnp.concatenate(
            [piece[:, MAIN:], jnp.zeros((lines, TILE - rest), F32)], axis=1
        )

    @pl.when(step == pl.num_programs(0) - 1)
    def _():
        lane = lax.broadcasted_iota(jnp.int32, (depth, TILE), 1)
        for t in range(groups):
            base = t * count
            for r in range(count):
                for h in range(2):
                    out_ref[t, r, :, h * TILE : (h + 1) * TILE] = main_ref[
                        h, pl.ds(base + r, depth, stride=pitch), :
                    ].astype(BF16)
            for g in range(ceil_div(count, per_slot)):
                for h in range(2):
                    packed = jnp.zeros((depth, TILE), F32)
                    for b in range(per_slot // 2):
                        r = g * per_slot + h * (per_slot // 2) + b
                        if r < count:
                            piece = rest_ref[pl.ds(base + r, depth, stride=pitch), :]
                            if b > 0:
                                piece = pltpu.roll(piece, b * rest, 1)
                            packed = jnp.where(lane // rest == b, piece, packed)
                    out_ref[t, count + g, :, h * TILE : (h + 1) * TILE] = packed.astype(BF16)


def project(here, home_vectors, force_table, groups, group, share, first, count):
    modes = home_vectors.shape[0]
    lines = groups * count
    depth = force_table.shape[1] // modes
    per_step = 8 if depth % 8 == 0 else 4
    rows = modes // STREAMS
    shape = (groups, slots_of(count, modes), depth, MAIN)

    def stream(k):
        return pl.BlockSpec((rows, per_step * modes), lambda i: (k, i))

    return pl.pallas_call(
        functools.partial(project_kernel, groups, group, share, first, count),
        grid=(depth // per_step,),
        in_specs=[
            pl.BlockSpec(memory_space=pltpu.SMEM),
            pl.BlockSpec((modes, modes), lambda i: (0, 0)),
        ]
        + [stream(k) for k in range(STREAMS)],
        out_specs=pl.BlockSpec(shape, lambda i: (0, 0, 0, 0)),
        out_shape=jax.ShapeDtypeStruct(shape, BF16),
        scratch_shapes=[
            pltpu.VMEM((lines, modes), BF16),
            pltpu.VMEM((2, (depth + 1) * (lines + 1), TILE), F32),
            pltpu.VMEM(((depth + 1) * (lines + 1), TILE), F32),
        ],
        compiler_params=pltpu.CompilerParams(vmem_limit_bytes=VMEM_BYTES),
        cost_estimate=pl.CostEstimate(
            flops=2 * lines * modes * modes * depth,
            bytes_accessed=2 * modes * modes * depth,
            transcendentals=0,
        ),
        name="project",
    )(here, home_vectors, *[force_table] * STREAMS)


def identity(size):
    return (
        lax.broadcasted_iota(jnp.int32, (size, size), 0)
        == lax.broadcasted_iota(jnp.int32, (size, size), 1)
    ).astype(BF16)


def pack_kernel(part_ref, partner_ref, weight_ref, grid_ref, freq_ref, out_ref):
    own_pairs, modes, _ = grid_ref.shape
    rest = modes - MAIN
    lines = rest // 2
    part = part_ref[0]
    line = lax.broadcasted_iota(jnp.int32, (lines, modes), 0)
    column = lax.broadcasted_iota(jnp.int32, (lines, modes), 1)
    select = (column == MAIN + part * lines + line).astype(BF16)
    freqs = freq_ref[...].astype(F32)
    blank = jnp.zeros((own_pairs, TILE - rest), F32)
    freq_tiles = (
        freqs[:, :TILE],
        freqs[:, TILE:MAIN],
        jnp.concatenate([freqs[:, MAIN:], blank], axis=1),
    )
    line16 = lax.broadcasted_iota(jnp.int32, (16, TILE), 0)
    lane16 = lax.broadcasted_iota(jnp.int32, (16, TILE), 1)
    for s in range(own_pairs):
        for p in range(2):

            @pl.when(part == p)
            def _():
                out_ref[s, :modes, :] = grid_ref[s, :, p * TILE : (p + 1) * TILE]

        turned = dot_nt(select, grid_ref[s])
        turned = (
            turned[:, :TILE],
            turned[:, TILE:MAIN],
            jnp.concatenate([turned[:, MAIN:], jnp.zeros((lines, TILE - rest), F32)], axis=1),
        )
        for h in range(3):
            start = modes + h * lines
            out_ref[s, start : start + lines, :] = turned[h].astype(BF16)
        pair = partner_ref[s].astype(F32)
        weight = weight_ref[s].astype(F32)
        side = jnp.where(lane16 == 0, pair, jnp.where(lane16 == 1, weight, 0.0))
        side = jnp.where(line16 == 3, side, 0.0)
        for h in range(3):
            side = jnp.where(line16 == h, freq_tiles[h][s : s + 1], side)
        start = modes + 3 * lines
        out_ref[s, start : start + 16, :] = side.astype(BF16)


def pack_own(part, partner, weights, grid_vectors, partner_frequencies):
    own_pairs, modes, _ = grid_vectors.shape
    smem = pl.BlockSpec(memory_space=pltpu.SMEM)
    vmem = pl.BlockSpec(memory_space=pltpu.VMEM)
    rows = modes + 3 * (modes - MAIN) // 2 + 16
    return pl.pallas_call(
        pack_kernel,
        in_specs=[smem, smem, smem, vmem, vmem],
        out_specs=vmem,
        out_shape=jax.ShapeDtypeStruct((own_pairs, rows, TILE), BF16),
        compiler_params=pltpu.CompilerParams(vmem_limit_bytes=VMEM_BYTES),
        name="pack_own",
    )(part, partner, weights, grid_vectors, partner_frequencies)


def arrange_kernel(
    pack_ref, partner_ref, weight_ref, grid_ref, grid_t_ref, freq_row_ref, freq_col_ref
):
    owners, parts, each, rows, _ = pack_ref.shape
    modes = grid_ref.shape[1]
    rest = modes - MAIN
    lines = rest // parts
    eye = identity(MAIN)
    source = lax.broadcasted_iota(jnp.int32, (TILE, TILE), 0)
    place = lax.broadcasted_iota(jnp.int32, (TILE, TILE), 1)
    spread = (source == place % rest).astype(BF16)
    eye_tile = (source == place).astype(BF16)
    lane = lax.broadcasted_iota(jnp.int32, (TILE, freq_col_ref.shape[1]), 1)
    line16 = lax.broadcasted_iota(jnp.int32, (16, TILE), 0)
    lane16 = lax.broadcasted_iota(jnp.int32, (16, TILE), 1)
    freq_col_ref[...] = jnp.zeros_like(freq_col_ref)

    def one(q, carry):
        for s in range(each):
            x = q * each + s
            for part in range(parts):
                grid_ref[x, :, part * TILE : (part + 1) * TILE] = pack_ref[q, part, s, :modes, :]
                for h in range(3):
                    start, width = modes + h * lines, min(TILE, modes - h * TILE)
                    piece = pack_ref[q, part, s, start : start + lines, :]
                    grid_t_ref[
                        x, MAIN + part * lines : MAIN + (part + 1) * lines, h * TILE : h * TILE + width
                    ] = piece[:, :width]
            grid_t_ref[x, :MAIN, :] = dot_nt(eye, grid_ref[x]).astype(BF16)
            side = pack_ref[q, 0, s, modes + 3 * lines : modes + 3 * lines + 16, :]
            wide = side.astype(F32)
            freq_row_ref[x, :, :TILE] = wide[0:1]
            freq_row_ref[x, :, TILE:MAIN] = wide[1:2]
            freq_row_ref[x, :, MAIN:] = dot_nn(side, spread)[2:3]
            columns = dot_nt(eye_tile, side)
            for h in range(3):
                width = min(TILE, modes - h * TILE)
                here = slice(h * TILE, h * TILE + width)
                freq_col_ref[here, :] = jnp.where(
                    lane[:width] == x, columns[:width, h : h + 1], freq_col_ref[here, :]
                )
            for spot, ref in ((0, partner_ref), (1, weight_ref)):
                found = jnp.sum(
                    jnp.where(jnp.logical_and(line16 == 3, lane16 == spot), wide, 0.0)
                )
                ref[x] = found.astype(ref.dtype)
        return carry

    lax.fori_loop(0, owners, one, 0, unroll=owners <= 4)


def arrange(pack, modes):
    owners, parts, each, _, _ = pack.shape
    pairs = owners * each
    smem = pl.BlockSpec(memory_space=pltpu.SMEM)
    vmem = pl.BlockSpec(memory_space=pltpu.VMEM)
    return pl.pallas_call(
        arrange_kernel,
        in_specs=[vmem],
        out_specs=[smem, smem, vmem, vmem, vmem, vmem],
        out_shape=[
            jax.ShapeDtypeStruct((pairs,), jnp.int32),
            jax.ShapeDtypeStruct((pairs,), F32),
            jax.ShapeDtypeStruct((pairs, modes, MAIN), BF16),
            jax.ShapeDtypeStruct((pairs, modes, modes), BF16),
            jax.ShapeDtypeStruct((pairs, 1, MAIN + TILE), F32),
            jax.ShapeDtypeStruct((modes, TILE), F32),
        ],
        compiler_params=pltpu.CompilerParams(vmem_limit_bytes=VMEM_BYTES),
        name="arrange",
    )(pack)


def interleave(heavy, light):
    done = 0
    for i, task in enumerate(heavy):
        task()
        upto = (i + 1) * len(light) // len(heavy)
        while done < upto:
            light[done]()
            done += 1
    while done < len(light):
        light[done]()
        done += 1


def coupling_kernel(
    first,
    share,
    block,
    partner_ref,
    weight_ref,
    home_ref,
    grid_source,
    grid_t_source,
    freq_row_ref,
    freq_col_ref,
    moved_ref,
    out_ref,
    turned_ref,
    grid_rest_ref,
    inner_rest_ref,
    pick_ref,
    rest_value_ref,
    home_row_ref,
    grid_ref,
    grid_t_ref,
    copy_sem,
    *work,
):
    gathers, inners, values, tabs, sums, rest_sums, firsts = (
        work[2 * i : 2 * i + 2] for i in range(7)
    )
    pairs = grid_ref.shape[0]
    modes = grid_ref.shape[1]
    rest = modes - MAIN
    sources, depth = moved_ref.shape[0], moved_ref.shape[2]
    per_slot = MAIN // rest
    rest_lanes = home_row_ref.shape[1]
    s2 = smearing * smearing
    steps = share // block

    fetch_turned = pltpu.make_async_copy(grid_t_source, grid_t_ref, copy_sem.at[0])
    fetch_grid = pltpu.make_async_copy(grid_source, grid_ref, copy_sem.at[1])
    fetch_turned.start()
    fetch_grid.start()
    spot = lax.broadcasted_iota(jnp.int32, (1, rest_lanes), 1) // rest
    row = jnp.ones((1, rest_lanes), F32)
    for r in range(share):
        row = jnp.where(spot == r, home_ref[first + r], row)
    home_row_ref[0:1, :] = row
    home_row_ref[1:2, :] = row * row - s2
    home_row_ref[2:3, :] = (4.0 * s2) * (row * row)
    home_row_ref[3:4, :] = 1.0 / row
    eye = identity(modes)
    if share * rest < rest_lanes:
        inner_rest_ref[...] = jnp.zeros_like(inner_rest_ref)
    for r in range(share):
        slot, spot = share + r // per_slot, r % per_slot
        half, spot = spot // (per_slot // 2), spot % (per_slot // 2)
        gather_ref = gathers[r % 2]
        for s in range(sources):
            gather_ref[s * depth : (s + 1) * depth, :MAIN] = moved_ref[s, r].astype(F32)
            tail = moved_ref[s, slot, :, half * TILE : (half + 1) * TILE].astype(F32)
            if spot > 0:
                tail = pltpu.roll(tail, TILE - spot * rest, 1)
            gather_ref[s * depth : (s + 1) * depth, MAIN:] = tail[:, :rest]
        whole = gather_ref[...].astype(BF16)
        turned_ref[r * modes : (r + 1) * modes, :] = dot_nt(eye, whole).astype(BF16)

    fetch_turned.wait()
    for x in range(pairs):
        grid_rest_ref[x * rest : (x + 1) * rest, :] = grid_t_ref[x, MAIN:, :]
    for r in range(share):
        found = dot_nt(grid_rest_ref[...], turned_ref[r * modes : (r + 1) * modes, :]).astype(BF16)
        for x in range(pairs):
            inner_rest_ref[x, r * rest : (r + 1) * rest, :] = found[x * rest : (x + 1) * rest, :]

    fetch_grid.wait()

    row_id = lax.broadcasted_iota(jnp.int32, pick_ref.shape, 0)
    col_id = lax.broadcasted_iota(jnp.int32, pick_ref.shape, 1)
    pick_ref[...] = (row_id // rest == col_id).astype(BF16)
    for ref in (out_ref, *sums, *rest_sums, *firsts):
        ref[...] = jnp.zeros_like(ref)

    def contract_first(x, r, b, into):
        def task():
            found = dot_nn(turned_ref[r * modes : (r + 1) * modes, :], grid_ref[x])
            into[:, b * MAIN : (b + 1) * MAIN] = found.astype(BF16)

        return task

    def contract_second(x, b, source, into):
        lanes = slice(b * MAIN, (b + 1) * MAIN)

        def task():
            into[:, lanes] = dot_nn(grid_t_ref[partner_ref[x]], source[:, lanes])

        return task

    def line_shapes(v, t, w, c1, c2):
        p = v * v
        d = t[0] - w
        e = t[1] - c1
        return (
            (p * t[2]) * pl.reciprocal(d * d + s2, approx=True),
            (p * t[3]) * pl.reciprocal(e * e + c2, approx=True),
        )

    def weigh(step, source, tab, sum_ref, first_ref):
        state = {}

        def begin():
            state["w"] = [home_ref[first + step * block + b] for b in range(block)]
            state["c1"] = [w * w - s2 for w in state["w"]]
            state["c2"] = [(4.0 * s2) * (w * w) for w in state["w"]]
            state["total"] = [jnp.zeros((8, MAIN), F32) for _ in range(block)]

        def rows(n):
            def task():
                if n == 0:
                    begin()
                t = [tab[k, n : n + 8, :MAIN] for k in range(4)]
                for b in range(block):
                    v = source[n : n + 8, b * MAIN : (b + 1) * MAIN]
                    f, u = line_shapes(v, t, state["w"][b], state["c1"][b], state["c2"][b])
                    state["total"][b] = state["total"][b] + f
                    r = step * block + b
                    sum_ref[n : n + 8, r : r + 1] = jnp.sum(
                        u[:, :TILE] + u[:, TILE:], axis=1, keepdims=True
                    )
                if n + 8 == modes:
                    for b in range(block):
                        r = step * block + b
                        line = jnp.sum(state["total"][b], axis=0, keepdims=True)
                        first_ref[r : r + 1, :MAIN] = line * (1.0 / state["w"][b])

            return task

        return [rows(n) for n in range(0, modes, 8)]

    def contract_rest(x):
        def task():
            rest_value_ref[...] = dot_nt(grid_t_ref[partner_ref[x]], inner_rest_ref[x])

        return task

    def weigh_rest(tab, sum_ref, first_ref):
        def tile(start):
            lanes = slice(start, start + TILE)
            state = {}

            def rows(n):
                def task():
                    if n == 0:
                        state["total"] = jnp.zeros((8, TILE), F32)
                        state["w"] = home_row_ref[0:1, lanes]
                        state["c1"] = home_row_ref[1:2, lanes]
                        state["c2"] = home_row_ref[2:3, lanes]
                    for k in range(n, n + 48, 16):
                        t = [tab[i, k : k + 16, MAIN:] for i in range(4)]
                        f, u = line_shapes(
                            rest_value_ref[k : k + 16, lanes], t, state["w"], state["c1"], state["c2"]
                        )
                        state["total"] = state["total"] + (f[:8] + f[8:])
                        sum_ref[k : k + 16, lanes] = u.astype(BF16)
                    if n + 48 == modes:
                        line = jnp.sum(state["total"], axis=0, keepdims=True)
                        line = line * home_row_ref[3:4, lanes]
                        for b in range(TILE // rest):
                            r = start // rest + b
                            if r < share:
                                first_ref[r : r + 1, MAIN:] = line[:, b * rest : (b + 1) * rest]

                return task

            return [rows(n) for n in range(0, modes, 48)]

        return [task for start in range(0, rest_lanes, TILE) for task in tile(start)]

    def tables(x, tab):
        state = {}

        def begin():
            w1 = freq_row_ref[x]
            spots = lax.broadcasted_iota(jnp.int32, freq_col_ref.shape, 1)
            w2 = jnp.sum(
                jnp.where(spots == partner_ref[x], freq_col_ref[...], 0.0), axis=1, keepdims=True
            )
            state["w"] = (w1, w2)
            state["o"] = (occupy(w1), occupy(w2))
            scale = weight_ref[x] * (smearing / math.pi / modes)
            state["i"] = (scale / w1, 1.0 / w2)

        def rows(n):
            def task():
                if n == 0:
                    begin()
                part = slice(n, n + 48)
                (w1, w2), (o1, o2), (i1, i2) = state["w"], state["o"], state["i"]
                w2, o2, i2 = w2[part], o2[part], i2[part]
                a = w1 - w2
                both = i1 * i2
                tab[0, part, :] = w1 + w2
                tab[1, part, :] = a * a
                tab[2, part, :] = (1.0 + o1 + o2) * both
                tab[3, part, :] = (4.0 * a) * (o2 - o1) * both

            return task

        return [rows(n) for n in range(0, modes, 48)]

    def collect(sum_ref, rest_sum_ref, state):
        def task():
            second = sum_ref[...] + dot_nn(rest_sum_ref[...], pick_ref[...])
            state["second"] = second.T[:share, :]

        return task

    def deliver(x, target, state, first_ref):
        out_ref[x, :share, :] += first_ref[:share, :]
        out_ref[target, :share, :] += state["second"]

    for task in tables(0, tabs[0]):
        task()
    for g in range(2):
        for b in range(block):
            x, step = jnp.int32(g // steps), g % steps
            contract_first(x, step * block + b, b, inners[g])()
    for b in range(block):
        contract_second(jnp.int32(0), b, inners[0], values[0])()

    def two_pairs(i, carry):
        for e in range(2):
            x = i * 2 + e

            def later(g):
                return jnp.minimum(i * 2 + g // steps, pairs - 1), g % steps

            before = jnp.maximum(x - 1, 0)
            target = partner_ref[before]
            extra = weigh_rest(tabs[e], rest_sums[e], firsts[e])
            extra = extra + tables(jnp.minimum(x + 1, pairs - 1), tabs[1 - e])
            contract_rest(x)()
            done = {}
            for s in range(steps):
                g = e * steps + s
                heavy = []
                for b in range(block):
                    x1, _ = later(g + 1)
                    heavy.append(contract_second(x1, b, inners[(g + 1) % 2], values[(g + 1) % 2]))
                for b in range(block):
                    x2, step2 = later(g + 2)
                    heavy.append(contract_first(x2, step2 * block + b, b, inners[g % 2]))
                light = weigh(s, values[g % 2], tabs[e], sums[e], firsts[e])
                light = light + extra[s * len(extra) // steps : (s + 1) * len(extra) // steps]
                if s == 0:
                    heavy.insert(1, collect(sums[1 - e], rest_sums[1 - e], done))
                interleave(heavy, light)
            deliver(before, target, done, firsts[1 - e])
        return carry

    lax.fori_loop(0, pairs // 2, two_pairs, 0)
    last = {}
    collect(sums[1], rest_sums[1], last)()
    deliver(pairs - 1, partner_ref[pairs - 1], last, firsts[1])

    totals = jnp.zeros(out_ref.shape[1:], F32)
    for y in range(pairs):
        totals = totals + out_ref[y]
    widths = jnp.sum(totals, axis=1, keepdims=True) * (1.0 / (pairs * modes))
    spread = jnp.where(
        lax.broadcasted_iota(jnp.int32, totals.shape, 0)
        == lax.broadcasted_iota(jnp.int32, totals.shape, 1),
        widths,
        0.0,
    )
    out_ref[:, share, :] = jnp.broadcast_to(
        jnp.sum(spread, axis=0, keepdims=True), (pairs, modes)
    )


def coupling(first, share, partner, weights, home, grid, grid_t, freq_rows, freq_cols, moved):
    pairs, modes = grid.shape[0], grid.shape[1]
    rest = modes - MAIN
    rest_lanes = ceil_div(share * rest, TILE) * TILE
    padded = (share // 8 + 1) * 8
    smem = pl.BlockSpec(memory_space=pltpu.SMEM)
    vmem = pl.BlockSpec(memory_space=pltpu.VMEM)
    block = 3 if share % 3 == 0 else 1
    assert pairs % 2 == 0
    scratch = (
        [
            pltpu.VMEM((share * modes, modes), BF16),
            pltpu.VMEM((pairs * rest, modes), BF16),
            pltpu.VMEM((pairs, rest_lanes, modes), BF16),
            pltpu.VMEM((rest_lanes, TILE), BF16),
            pltpu.VMEM((modes, rest_lanes), F32),
            pltpu.VMEM((8, rest_lanes), F32),
            pltpu.VMEM(grid.shape, BF16),
            pltpu.VMEM(grid_t.shape, BF16),
            pltpu.SemaphoreType.DMA((2,)),
        ]
        + [pltpu.VMEM((modes, modes), F32)] * 2
        + [pltpu.VMEM((modes, block * MAIN), BF16)] * 2
        + [pltpu.VMEM((modes, block * MAIN), F32)] * 2
        + [pltpu.VMEM((4, modes, MAIN + TILE), F32)] * 2
        + [pltpu.VMEM((modes, TILE), F32)] * 2
        + [pltpu.VMEM((modes, rest_lanes), BF16)] * 2
        + [pltpu.VMEM((padded, modes), F32)] * 2
    )
    return pl.pallas_call(
        functools.partial(coupling_kernel, first, share, block),
        in_specs=[smem] * 3 + [pl.BlockSpec(memory_space=pl.ANY)] * 2 + [vmem] * 3,
        out_specs=vmem,
        out_shape=jax.ShapeDtypeStruct((pairs, padded, modes), F32),
        scratch_shapes=scratch,
        compiler_params=pltpu.CompilerParams(vmem_limit_bytes=VMEM_BYTES),
        cost_estimate=pl.CostEstimate(
            flops=4 * share * pairs * modes**3,
            bytes_accessed=8 * share * modes * modes,
            transcendentals=2 * share * pairs * modes**2,
        ),
        name="coupling",
    )(partner, weights, home, grid, grid_t, freq_rows, freq_cols, moved)


def local(
    home_vectors, home_freqs, grid_vectors, partner_frequencies, force_table, partner, weights
):
    own_pairs = partner.shape[0]
    modes = home_vectors.shape[0]
    n_mode = lax.axis_size("mode")
    n_fc = lax.axis_size("fc")
    n_qp = lax.axis_size("qp")
    groups = n_mode * n_fc
    group = modes // groups
    pairs = own_pairs * n_qp
    share = ceil_div(group, n_qp)
    here = lax.axis_index("qp")
    if share % 6 == 0 and share > 6:
        chunks = ((0, 6), (6, share - 6))
    else:
        chunks = ((0, share),)

    assert n_fc * TILE == MAIN
    own_part = lax.axis_index("fc").astype(jnp.int32)[None]
    pack = pack_own(own_part, partner, weights, grid_vectors, partner_frequencies)
    pack = lax.all_gather(pack, ("qp", "fc"), axis=0)
    pack = pack.reshape(n_qp, n_fc, own_pairs, pack.shape[2], TILE)

    here_word = here.astype(jnp.int32)[None]
    moved = []
    for first, count in chunks:
        sent = project(here_word, home_vectors, force_table, groups, group, share, first, count)
        moved.append(
            lax.all_to_all(sent, ("mode", "fc"), split_axis=0, concat_axis=0, tiled=True)
        )

    own = lax.axis_index(("mode", "fc"))
    home = home_freqs.astype(F32).reshape(groups, group)
    home = jnp.pad(home, ((0, 0), (0, share * n_qp - group)), constant_values=1.0)
    home = lax.dynamic_slice(home, (own, here * share), (1, share)).reshape(share)

    shared = arrange(pack, modes)
    parts, widths = [], []
    for (first, count), block in zip(chunks, moved):
        found = coupling(
            first, count, shared[0], shared[1], home, *shared[2:], block
        )
        back = lax.all_to_all(
            found.reshape(n_qp, own_pairs, found.shape[1], modes),
            "qp",
            split_axis=0,
            concat_axis=0,
            tiled=True,
        )
        widths.append(back[:, 0, count, :count])
        parts.append(back[:, :, :count, :])
    widths = jnp.concatenate(widths, axis=1).reshape(n_qp * share)[:group]
    collision = jnp.transpose(jnp.concatenate(parts, axis=2), (0, 2, 1, 3))
    collision = collision.reshape(n_qp * share, own_pairs, modes)[:group]
    return (widths, collision)


def solution(mesh):
    placed = (
        P("grp", None),
        P("grp"),
        P("qp", None, None),
        P("qp", None),
        P(None, ("mode", "fc")),
        P(("grp", "qp")),
        P(("grp", "qp")),
    )
    return jax.shard_map(
        local,
        mesh=mesh,
        in_specs=placed,
        out_specs=(P(("grp", "mode", "fc")), P(("mode", "fc"), ("grp", "qp"), None)),
        check_vma=False,
    )
```
